128 devices in a mesh: px: 8 (over x_hi, y), py: 16 (over z, x_lo, core).
Axes of the slice: x: 4 (x_hi: 2, x_lo: 2; x = x_hi * 2 + x_lo), y: 4, z: 4, core: 2. Of those that a mesh axis runs over, the one named last changes fastest.
Arguments:
- tokens: bfloat16 [128, 128, 6144], P('px', 'py'), may hold values from -6 to 6
- conv_weight: float32 [27, 192], replicated, may hold values from -1.2 to 1.2
- inner_weight: bfloat16 [2, 2, 96, 96], replicated, may hold values from -0.4375 to 0.4375
- outer_weight: bfloat16 [2, 2, 96, 96], replicated, may hold values from -0.625 to 0.625
Outputs:
- mixed: bfloat16 [128, 128, 6144], P('px', 'py')
The draws below stay inside these ranges and needn't reach their ends.
All inputs are finite; a program needn't handle non-finite values.
Results may differ from the reference program's by a relative error of at most 0.0095.
Values may be sent and summed in bfloat16 or wider, within the bound.
No kernel may reach another device: no remote copies, remote signals or barrier semaphores. Data moves between devices by JAX's collectives and lax.ppermute only.
A program may use at most 64 MiB of HBM per device.

```python
import math
import jax
import jax.numpy as jnp
from jax import lax

X = 128
Y = 128
Z = 32
CB = 96
NBLK = 2
KZ = 16
C = 192


def level_of(stream_key, dims, cuts, smallest, top_value):
    gain = 1.0
    for axis_at, parts in cuts:
        steps = jax.random.uniform(jax.random.fold_in(jax.random.fold_in(stream_key, 6), axis_at), (parts,), jnp.float32, smallest / len(cuts), top_value / len(cuts))
        gain = gain * jnp.repeat(jnp.exp(steps), dims[axis_at] // parts).reshape((-1,) + (1,) * (len(dims) - 1 - axis_at))
    return gain


def gaussian(own_key, extent, spread, limit, split=(), kind=jnp.bfloat16):
    entries = spread * jax.random.normal(own_key, extent, jnp.float32)
    if split:
        entries = entries * level_of(own_key, extent, split, -0.22, 0.18)
    return jnp.clip(entries, -limit, limit).astype(kind)


def setup_inputs(seed: int = 0) -> dict:
    arg_keys = jax.random.split(jax.random.key(seed), 5)
    return {
        "tokens": gaussian(arg_keys[0], (X, Y, Z * C), 1.0, 6.0, ((0, 8), (1, 16))),
        "conv_weight": gaussian(arg_keys[1], (27, C), 0.2, 1.2, (), jnp.float32),
        "inner_weight": gaussian(arg_keys[2], (2, NBLK, CB, CB), (2 * CB) ** -0.5, 0.4375),
        "outer_weight": gaussian(arg_keys[3], (2, NBLK, CB, CB), CB ** -0.5, 0.625),
    }


shrink_level = 0.2

def wave_tables(length, modes, weights):
    grid = jnp.arange(length, dtype=jnp.int32)
    product = modes[:, None] * grid[None, :] % length
    angle = product.astype(jnp.float32) * (2.0 * math.pi / length)
    factor = weights[:, None] / math.sqrt(length)
    return ((jnp.cos(angle) * factor).astype(jnp.bfloat16), (jnp.sin(angle) * factor).astype(jnp.bfloat16))

def kept_modes(length):
    quarter = length // 4
    return jnp.concatenate([jnp.arange(quarter, dtype=jnp.int32), jnp.arange(length - quarter, length, dtype=jnp.int32)])

def depth_weights(count):
    return jnp.where(jnp.arange(count, dtype=jnp.int32) == 0, 1.0, 2.0).astype(jnp.float32)

def convolve(padded, weight):
    size_x = padded.shape[0] - 2
    size_y = padded.shape[1] - 2
    depth = padded.shape[2]
    padded = jnp.pad(padded, ((0, 0), (0, 0), (1, 1), (0, 0))).astype(jnp.float32)
    total = jnp.zeros((size_x, size_y, depth, padded.shape[3]), jnp.float32)
    for shift_a in range(3):
        for shift_b in range(3):
            for shift_e in range(3):
                window = padded[shift_a:shift_a + size_x, shift_b:shift_b + size_y, shift_e:shift_e + depth]
                total = total + window * weight[shift_a * 9 + shift_b * 3 + shift_e]
    return total.astype(jnp.bfloat16)

def mult(form, left, right):
    return jnp.einsum(form, left.astype(jnp.float32), right.astype(jnp.float32), precision=lax.Precision.HIGHEST)

def reference(tokens, conv_weight, inner_weight, outer_weight):
    channels = NBLK * CB
    tokens = tokens.reshape(X, Y, Z, channels)
    group = math.gcd(channels, 16)
    count = channels // group
    cos_z, sin_z = wave_tables(Z, jnp.arange(KZ, dtype=jnp.int32), jnp.ones((KZ,), jnp.float32))
    icos_z, isin_z = wave_tables(Z, jnp.arange(KZ, dtype=jnp.int32), depth_weights(KZ))
    cos_y, sin_y = wave_tables(Y, kept_modes(Y), jnp.ones((Y // 2,), jnp.float32))
    cos_x, sin_x = wave_tables(X, kept_modes(X), jnp.ones((X // 2,), jnp.float32))

    def forward(start):
        part = lax.dynamic_slice_in_dim(tokens, start, group, 3)
        weight = lax.dynamic_slice_in_dim(conv_weight, start, group, 1)
        field = convolve(jnp.pad(part, ((1, 1), (1, 1), (0, 0), (0, 0))), weight)
        real_z = mult('xyzc,kz->xykc', field, cos_z).astype(jnp.bfloat16)
        imag_z = (-mult('xyzc,kz->xykc', field, sin_z)).astype(jnp.bfloat16)
        real_y = (mult('xykc,qy->xqkc', real_z, cos_y) + mult('xykc,qy->xqkc', imag_z, sin_y)).astype(jnp.bfloat16)
        imag_y = (mult('xykc,qy->xqkc', imag_z, cos_y) - mult('xykc,qy->xqkc', real_z, sin_y)).astype(jnp.bfloat16)
        spec_r = (mult('xqkc,px->pqkc', real_y, cos_x) + mult('xqkc,px->pqkc', imag_y, sin_x)).astype(jnp.bfloat16)
        spec_i = (mult('xqkc,px->pqkc', imag_y, cos_x) - mult('xqkc,px->pqkc', real_y, sin_x)).astype(jnp.bfloat16)
        return (field, spec_r, spec_i)
    starts = jnp.arange(count, dtype=jnp.int32) * group
    fields, spec_r, spec_i = lax.map(forward, starts)
    spec_r = jnp.moveaxis(spec_r, 0, 3).reshape(X // 2, Y // 2, KZ, channels)
    spec_i = jnp.moveaxis(spec_i, 0, 3).reshape(X // 2, Y // 2, KZ, channels)
    lead = spec_r.shape[:3]
    block_r = spec_r.reshape(lead + (NBLK, CB))
    block_i = spec_i.reshape(lead + (NBLK, CB))
    form = 'pqkbc,bcd->pqkbd'
    hidden_r = jnp.tanh(mult(form, block_r, inner_weight[0]) - mult(form, block_i, inner_weight[1])).astype(jnp.bfloat16)
    hidden_i = jnp.tanh(mult(form, block_r, inner_weight[1]) + mult(form, block_i, inner_weight[0])).astype(jnp.bfloat16)
    out_r = mult(form, hidden_r, outer_weight[0]) - mult(form, hidden_i, outer_weight[1])
    out_i = mult(form, hidden_r, outer_weight[1]) + mult(form, hidden_i, outer_weight[0])
    filt_r = (out_r - jnp.clip(out_r, -shrink_level, shrink_level)).astype(jnp.bfloat16).reshape(lead + (channels,))
    filt_i = (out_i - jnp.clip(out_i, -shrink_level, shrink_level)).astype(jnp.bfloat16).reshape(lead + (channels,))

    def inverse(pair):
        start, field = pair
        part_r = lax.dynamic_slice_in_dim(filt_r, start, group, 3)
        part_i = lax.dynamic_slice_in_dim(filt_i, start, group, 3)
        back_xr = (mult('pqkc,px->xqkc', part_r, cos_x) - mult('pqkc,px->xqkc', part_i, sin_x)).astype(jnp.bfloat16)
        back_xi = (mult('pqkc,px->xqkc', part_i, cos_x) + mult('pqkc,px->xqkc', part_r, sin_x)).astype(jnp.bfloat16)
        back_yr = (mult('xqkc,qy->xykc', back_xr, cos_y) - mult('xqkc,qy->xykc', back_xi, sin_y)).astype(jnp.bfloat16)
        back_yi = (mult('xqkc,qy->xykc', back_xi, cos_y) + mult('xqkc,qy->xykc', back_xr, sin_y)).astype(jnp.bfloat16)
        result = mult('xykc,kz->xyzc', back_yr, icos_z) - mult('xykc,kz->xyzc', back_yi, isin_z)
        return (result + field.astype(jnp.float32)).astype(jnp.bfloat16)
    outputs = lax.map(inverse, (starts, fields))
    return jnp.moveaxis(outputs, 0, 3).reshape(X, Y, Z * channels)
```

```python
import functools
import math

import jax
import jax.numpy as jnp
import ml_dtypes
import numpy as np
from jax import lax
from jax.experimental import pallas as pl
from jax.experimental.pallas import tpu as pltpu
from jax.sharding import PartitionSpec as P

shrink_level = 0.2
F32 = jnp.float32
BF16 = jnp.bfloat16
VMEM = pltpu.VMEM

PX, PY = 8, 16
LX, LY = 16, 8
Z, KZ, C, CB = 32, 16, 192, 96
W = 2 * C
MERGED = Z * C
XP = LX // 2
ZH = Z // 2
Q = 64


def tables(length, modes, weights):
    product = np.asarray(modes)[:, None] * np.arange(length)[None, :] % length
    angle = product.astype(np.float32) * np.float32(2.0 * math.pi / length)
    factor = np.asarray(weights, np.float32)[:, None] / np.float32(math.sqrt(length))
    rounded = [(f(angle) * factor).astype(ml_dtypes.bfloat16) for f in (np.cos, np.sin)]
    return [t.astype(np.float64) for t in rounded]


def kept(length):
    return np.concatenate([np.arange(length // 4), np.arange(length - length // 4, length)])


def forward(cos, sin):
    return np.stack([np.stack([cos, sin], 1), np.stack([-sin, cos], 1)])


def backward(cos, sin):
    cos, sin = cos.T, sin.T
    return np.stack([np.stack([cos, -sin], 1), np.stack([sin, cos], 1)])


def as_bf16(matrix):
    return np.ascontiguousarray(matrix).astype(ml_dtypes.bfloat16)


@functools.cache
def matrices():
    eye = np.eye(LY)
    one = np.ones(KZ)
    cz, sz = tables(Z, np.arange(KZ), one)
    both = np.stack([cz, -sz], 1).reshape(KZ, 2, ZH, 2)
    z_fwd = np.einsum("kpzs,yw->kpyszw", both, eye).reshape(KZ * 2 * LY, 2 * ZH * LY)
    two = np.where(np.arange(KZ) == 0, 1.0, 2.0)
    cz, sz = tables(Z, np.arange(KZ), two)
    both = np.stack([cz, -sz], 1).reshape(KZ, 2, ZH, 2)
    z_inv = np.einsum("kpzs,yw->szykpw", both, eye).reshape(2 * ZH * LY, KZ * 2 * LY)
    n = PY * LY
    cy, sy = tables(n, kept(n), np.ones(Q))
    y_fwd = forward(cy, sy).reshape(2, Q, 2, PY, LY).transpose(0, 1, 3, 2, 4).reshape(2 * Q, 2 * n)
    y_inv = backward(cy, sy).reshape(2, PY, LY, 2, PX, Q // PX)
    y_inv = y_inv.transpose(1, 0, 2, 4, 3, 5).reshape(2 * n, 2 * Q)
    n = PX * LX
    cx, sx = tables(n, kept(n), np.ones(Q))
    x_fwd = forward(cx, sx).reshape(2, Q, 2, PX, XP, 2)
    x_fwd = x_fwd.transpose(5, 0, 1, 3, 2, 4).reshape(4 * Q, 2 * PX * XP)
    x_inv = backward(cx, sx).reshape(2, PX, XP, 2, 2, Q)
    x_inv = x_inv.transpose(3, 0, 1, 2, 4, 5).reshape(4 * PX * XP, 2 * Q)
    return [as_bf16(m) for m in (z_fwd, z_inv, y_fwd, y_inv, x_fwd, x_inv)]


def dot(a, b):
    return jnp.dot(a, b, preferred_element_type=F32)


def low_half(rows):
    return lax.broadcasted_iota(jnp.int32, (rows, W), 1) < C


def swap(value):
    return pltpu.roll(value, C, 1)


def conv_kernel(tok, xlo, xhi, ylo, yhi, weight, z_fwd, field, freq, shifted, ylo_s, yhi_s, edge, conv):
    pad = jnp.zeros((LY, C), F32)
    for i in range(LX + 2):
        row = xlo[0] if i == 0 else xhi[0] if i == LX + 1 else tok[i - 1]
        shifted[i, :, :] = jnp.concatenate([pad, row.astype(F32), pad], axis=1)
    pad = jnp.zeros((LX + 2, C), F32)
    ylo_s[...] = jnp.concatenate([pad, ylo[...].astype(F32), pad], axis=1)
    yhi_s[...] = jnp.concatenate([pad, yhi[...].astype(F32), pad], axis=1)
    row_at = lax.broadcasted_iota(jnp.int32, (LY, 128), 0)

    @pl.loop(0, MERGED // 128)
    def _(j):
        at = pl.multiple_of(j * 128, 128)
        after = pl.multiple_of(j * 128 + W, 128)
        here = pl.ds(at, 128)
        phase = pl.multiple_of(lax.rem(j, 3) * 128, 128)
        taps = [weight[t : t + 1, pl.ds(phase, 128)] for t in range(27)]
        for side, rows, rows_s, b in ((0, ylo, ylo_s, 0), (1, yhi, yhi_s, 2)):
            mid = rows[:, here].astype(F32)
            before = rows_s[:, here]
            behind = rows_s[:, pl.ds(after, 128)]
            total = None
            for a in range(3):
                t = a * 9 + b * 3
                term = before * taps[t] + mid * taps[t + 1] + behind * taps[t + 2]
                term = term[a : a + LX]
                total = term if total is None else total + term
            edge[side] = total
        wide = [jnp.broadcast_to(t, (LY, 128)) for t in taps]
        sums = {}
        for i in range(LX + 2):
            ref = xlo if i == 0 else xhi if i == LX + 1 else tok
            mid = ref[0 if i in (0, LX + 1) else i - 1, :, here].astype(F32)
            before = shifted[i, :, here]
            behind = shifted[i, :, pl.ds(after, 128)]
            for a in range(3):
                x = i - a
                if not 0 <= x < LX:
                    continue
                for b in range(3):
                    t = a * 9 + b * 3
                    term = before * wide[t] + mid * wide[t + 1] + behind * wide[t + 2]
                    sums[x, b] = sums[x, b] + term if (x, b) in sums else term
            x = i - 2
            if x >= 0:
                down = pltpu.roll(sums.pop((x, 0)), 1, 0)
                up = pltpu.roll(sums.pop((x, 2)), LY - 1, 0)
                down = jnp.where(row_at == 0, edge[0, x : x + 1, :], down)
                up = jnp.where(row_at == LY - 1, edge[1, x : x + 1, :], up)
                conv[x, :, here] = sums.pop((x, 1)) + down + up

    low = low_half(ZH * LY)

    @pl.loop(0, XP)
    def _(xp):
        parts = []
        for x in (2 * xp, 2 * xp + 1):
            part = jnp.concatenate([conv[x, :, z * W : (z + 1) * W] for z in range(ZH)], axis=0)
            field[x] = part.astype(BF16)
            parts.append(part)
        first, second = parts
        even = jnp.where(low, first, swap(second)).astype(BF16)
        odd = jnp.where(low, swap(first), second).astype(BF16)
        out = dot(z_fwd[...], jnp.concatenate([even, odd], axis=0))
        freq[:, xp] = out.astype(BF16).reshape(KZ, 2 * LY, W)


def y_forward_kernel(given, y_fwd, out, rows):
    for xp in range(XP):
        data = given[:, xp].reshape(2 * PY * LY, W)
        value = dot(y_fwd[...], data)
        for part in range(2):
            for t in range(W // 128):
                rows[t, pl.ds(part * XP + xp, Q, stride=2 * XP), :] = value[
                    part * Q : (part + 1) * Q, t * 128 : (t + 1) * 128
                ]
    gather(rows, out)


def gather(rows, out):
    count = 2 * XP * Q // PX
    for d in range(PX):
        block = [rows[t, pl.ds(d * count, count), :] for t in range(W // 128)]
        out[d] = jnp.concatenate(block, axis=1).astype(BF16).reshape(out.shape[1:])


def shrink(v):
    return v - jnp.clip(v, -shrink_level, shrink_level)


def spectrum_kernel(given, x_fwd, x_inv, inner, outer, out, rows):
    low = low_half(2 * PX * XP)
    for q in range(Q // PX):
        data = given[:, q].reshape(2 * PX * XP, W)
        both = dot(x_fwd[...], data)
        spec = both[: 2 * Q] + swap(both[2 * Q :])
        spec = spec[:, :256].astype(BF16)
        mixed = dot(spec, inner[...])
        hidden_r = jnp.tanh(mixed[:Q, :256] - mixed[Q:, 256:])
        hidden_i = jnp.tanh(mixed[:Q, 256:] + mixed[Q:, :256])
        hidden = jnp.concatenate([hidden_r, hidden_i], axis=0).astype(BF16)
        mixed = dot(hidden, outer[...])
        filt_r = shrink(mixed[:Q, :W] - mixed[Q:, W:])
        filt_i = shrink(mixed[:Q, W:] + mixed[Q:, :W])
        filt = jnp.concatenate([filt_r, filt_i], axis=0).astype(BF16)
        both = dot(x_inv[...], filt)
        back = jnp.where(low, both[: 2 * PX * XP], both[2 * PX * XP :])
        for part in range(2):
            for t in range(W // 128):
                rows[t, pl.ds(part * (Q // PX) + q, PX * XP, stride=2 * (Q // PX)), :] = back[
                    part * PX * XP : (part + 1) * PX * XP, t * 128 : (t + 1) * 128
                ]
    gather(rows, out)


def y_inverse_kernel(given, y_inv, out):
    for xp in range(XP):
        data = given[:, xp].reshape(2 * Q, W)
        out[:, xp] = dot(y_inv[...], data).astype(BF16).reshape(PY, 2 * LY, W)


def z_inverse_kernel(given, z_inv, field, out):
    low = low_half(ZH * LY)

    @pl.loop(0, XP)
    def _(xp):
        data = given[:, xp].reshape(2 * KZ * LY, W)
        value = dot(z_inv[...], data)
        even, odd = value[: ZH * LY], value[ZH * LY :]
        first = jnp.where(low, even, swap(odd)) + field[2 * xp].astype(F32)
        second = jnp.where(low, swap(even), odd) + field[2 * xp + 1].astype(F32)
        for x, value in ((2 * xp, first), (2 * xp + 1, second)):
            for z in range(ZH):
                out[x, :, z * W : (z + 1) * W] = value[z * LY : (z + 1) * LY].astype(BF16)


def call(kernel, outs, scratch=(), name=None):
    return pl.pallas_call(
        kernel,
        out_shape=outs,
        scratch_shapes=list(scratch),
        compiler_params=pltpu.CompilerParams(vmem_limit_bytes=50 * 2**20),
        name=name,
    )


def shape(*dims):
    return jax.ShapeDtypeStruct(dims, BF16)


def block_diagonal(weight):
    full = jnp.zeros((2, C, C), weight.dtype)
    for b in range(C // CB):
        full = full.at[:, b * CB : (b + 1) * CB, b * CB : (b + 1) * CB].set(weight[:, b])
    return full


def halos(tokens):
    up_x = [(i, i + 1) for i in range(PX - 1)]
    down_x = [(j, i) for i, j in up_x]
    up_y = [(i, i + 1) for i in range(PY - 1)]
    down_y = [(j, i) for i, j in up_y]
    xlo = lax.ppermute(tokens[LX - 1 :], "px", up_x)
    xhi = lax.ppermute(tokens[:1], "px", down_x)
    first, last = (
        jnp.concatenate([xlo[:, y], tokens[:, y], xhi[:, y]], axis=0) for y in (0, LY - 1)
    )
    ylo = lax.ppermute(last, "py", up_y)
    yhi = lax.ppermute(first, "py", down_y)
    return xlo, xhi, ylo, yhi


def body(tokens, conv_weight, inner_weight, outer_weight):
    z_fwd, z_inv, y_fwd, y_inv, x_fwd, x_inv = (jnp.asarray(m) for m in matrices())
    weight = jnp.concatenate([conv_weight, conv_weight], axis=1)
    inner = block_diagonal(inner_weight)
    inner = jnp.pad(inner, ((0, 0), (0, 256 - C), (0, 256 - C)))
    inner = jnp.concatenate([inner[0], inner[1]], axis=1)
    outer = block_diagonal(outer_weight)
    outer = jnp.pad(outer, ((0, 0), (0, 256 - C), (0, 0)))
    outer = jnp.concatenate([outer[0], outer[0], outer[1], outer[1]], axis=1)

    xlo, xhi, ylo, yhi = halos(tokens)
    wide = MERGED + 2 * C
    field, freq = call(
        conv_kernel,
        [shape(LX, ZH * LY, W), shape(KZ, XP, 2 * LY, W)],
        [
            VMEM((LX + 2, LY, wide), F32),
            VMEM((LX + 2, wide), F32),
            VMEM((LX + 2, wide), F32),
            VMEM((2, LX, 128), F32),
            VMEM((LX, LY, MERGED), F32),
        ],
        name="conv_z",
    )(tokens, xlo, xhi, ylo, yhi, weight, z_fwd)
    rows = VMEM((W // 128, 2 * XP * Q, 128), F32)
    freq = lax.all_to_all(freq, "py", 0, 0, tiled=True)
    freq = call(y_forward_kernel, shape(PX, Q // PX, 2 * XP, W), [rows], name="y_fwd")(freq, y_fwd)
    freq = lax.all_to_all(freq, "px", 0, 0, tiled=True)
    freq = call(spectrum_kernel, shape(PX, XP, 2 * Q // PX, W), [rows], name="spec")(
        freq, x_fwd, x_inv, inner, outer
    )
    freq = lax.all_to_all(freq, "px", 0, 0, tiled=True)
    freq = call(y_inverse_kernel, shape(PY, XP, 2 * LY, W), name="y_inv")(freq, y_inv)
    freq = lax.all_to_all(freq, "py", 0, 0, tiled=True)
    return call(z_inverse_kernel, shape(LX, LY, MERGED), name="z_inv")(freq, z_inv, field)


def solution(mesh):
    in_specs = (P("px", "py", None), P(), P(), P())
    out_specs = P("px", "py", None)
    return jax.shard_map(body, mesh=mesh, in_specs=in_specs, out_specs=out_specs, check_vma=False)
```

```python
import functools
import math

import jax
import jax.numpy as jnp
import ml_dtypes
import numpy as np
from jax import lax
from jax.experimental import pallas as pl
from jax.experimental.pallas import tpu as pltpu
from jax.sharding import PartitionSpec as P

shrink_level = 0.2
F32 = jnp.float32
BF16 = jnp.bfloat16
VMEM = pltpu.VMEM

PX, PY = 8, 16
LX, LY = 16, 8
Z, KZ, C, CB = 32, 16, 192, 96
W = 2 * C
MERGED = Z * C
XP = LX // 2
ZH = Z // 2
Q = 64


def tables(length, modes, weights):
    product = np.asarray(modes)[:, None] * np.arange(length)[None, :] % length
    angle = product.astype(np.float32) * np.float32(2.0 * math.pi / length)
    factor = np.asarray(weights, np.float32)[:, None] / np.float32(math.sqrt(length))
    rounded = [(f(angle) * factor).astype(ml_dtypes.bfloat16) for f in (np.cos, np.sin)]
    return [t.astype(np.float64) for t in rounded]


def kept(length):
    return np.concatenate([np.arange(length // 4), np.arange(length - length // 4, length)])


def forward(cos, sin):
    return np.stack([np.stack([cos, sin], 1), np.stack([-sin, cos], 1)])


def backward(cos, sin):
    cos, sin = cos.T, sin.T
    return np.stack([np.stack([cos, -sin], 1), np.stack([sin, cos], 1)])


def as_bf16(matrix):
    return np.ascontiguousarray(matrix).astype(ml_dtypes.bfloat16)


@functools.cache
def matrices():
    eye = np.eye(LY)
    one = np.ones(KZ)
    cz, sz = tables(Z, np.arange(KZ), one)
    both = np.stack([cz, -sz], 1).reshape(KZ, 2, ZH, 2)
    z_fwd = np.einsum("kpzs,yw->kpyszw", both, eye).reshape(KZ * 2 * LY, 2 * ZH * LY)
    two = np.where(np.arange(KZ) == 0, 1.0, 2.0)
    cz, sz = tables(Z, np.arange(KZ), two)
    both = np.stack([cz, -sz], 1).reshape(KZ, 2, ZH, 2)
    z_inv = np.einsum("kpzs,yw->szykpw", both, eye).reshape(2 * ZH * LY, KZ * 2 * LY)
    n = PY * LY
    cy, sy = tables(n, kept(n), np.ones(Q))
    y_fwd = forward(cy, sy).reshape(2, Q, 2, PY, LY).transpose(0, 1, 3, 2, 4).reshape(2 * Q, 2 * n)
    y_inv = backward(cy, sy).reshape(2, PY, LY, 2, PX, Q // PX)
    y_inv = y_inv.transpose(1, 0, 2, 4, 3, 5).reshape(2 * n, 2 * Q)
    n = PX * LX
    cx, sx = tables(n, kept(n), np.ones(Q))
    x_fwd = forward(cx, sx).reshape(2, Q, 2, PX, XP, 2)
    x_fwd = x_fwd.transpose(5, 0, 1, 3, 2, 4).reshape(4 * Q, 2 * PX * XP)
    x_inv = backward(cx, sx).reshape(2, PX, XP, 2, 2, Q)
    x_inv = x_inv.transpose(3, 0, 1, 2, 4, 5).reshape(4 * PX * XP, 2 * Q)
    return [as_bf16(m) for m in (z_fwd, z_inv, y_fwd, y_inv, x_fwd, x_inv)]


def dot(a, b):
    return jnp.dot(a, b, preferred_element_type=F32)


def low_half(rows):
    return lax.broadcasted_iota(jnp.int32, (rows, W), 1) < C


def swap(value):
    return pltpu.roll(value, C, 1)


def conv_rows(rows, weight, out, shifted):
    pad = jnp.zeros((LY, C), F32)
    flat = [row for run in rows for row in run]
    for i, (ref, x) in enumerate(flat):
        shifted[i] = jnp.concatenate([pad, ref[x].astype(F32), pad], axis=1)
    row_at = lax.broadcasted_iota(jnp.int32, (LY, 128), 0)

    @pl.loop(0, MERGED // 128)
    def _(j):
        at = pl.multiple_of(j * 128, 128)
        after = pl.multiple_of(j * 128 + W, 128)
        here = pl.ds(at, 128)
        phase = pl.multiple_of(lax.rem(j, 3) * 128, 128)
        wide = [jnp.broadcast_to(weight[t : t + 1, pl.ds(phase, 128)], (LY, 128)) for t in range(27)]
        done = slot = 0
        for run in rows:
            sums = {}
            for i, (ref, x) in enumerate(run):
                mid = ref[x, :, here].astype(F32)
                before = shifted[slot, :, here]
                behind = shifted[slot, :, pl.ds(after, 128)]
                slot += 1
                for a in range(3):
                    to = i - a
                    if not 0 <= to < len(run) - 2:
                        continue
                    for b in range(3):
                        t = a * 9 + b * 3
                        term = before * wide[t] + mid * wide[t + 1] + behind * wide[t + 2]
                        sums[to, b] = sums[to, b] + term if (to, b) in sums else term
                if i >= 2:
                    to = i - 2
                    down = pltpu.roll(sums.pop((to, 0)), 1, 0)
                    up = pltpu.roll(sums.pop((to, 2)), LY - 1, 0)
                    down = jnp.where(row_at == 0, 0.0, down)
                    up = jnp.where(row_at == LY - 1, 0.0, up)
                    out[done, :, here] = sums.pop((to, 1)) + down + up
                    done += 1


def near_kernel(tok, weight, out, shifted):
    conv_rows([[(tok, x) for x in range(0, LX // 2 + 1)]], weight, out, shifted)


def far_kernel(tok, xlo, xhi, weight, out, shifted):
    start = [(xlo, 0), (tok, 0), (tok, 1)]
    end = [(tok, x) for x in range(LX // 2 - 1, LX)] + [(xhi, 0)]
    conv_rows([start, end], weight, out, shifted)


def edge_kernel(near, far, ylo, yhi, weight, z_fwd, field, freq, ylo_s, yhi_s, edge):
    pad = jnp.zeros((LX + 2, C), F32)
    ylo_s[...] = jnp.concatenate([pad, ylo[...].astype(F32), pad], axis=1)
    yhi_s[...] = jnp.concatenate([pad, yhi[...].astype(F32), pad], axis=1)

    @pl.loop(0, MERGED // 128)
    def _(j):
        at = pl.multiple_of(j * 128, 128)
        after = pl.multiple_of(j * 128 + W, 128)
        here = pl.ds(at, 128)
        phase = pl.multiple_of(lax.rem(j, 3) * 128, 128)
        for side, rows, rows_s, b in ((0, ylo, ylo_s, 0), (1, yhi, yhi_s, 2)):
            mid = rows[:, here].astype(F32)
            before = rows_s[:, here]
            behind = rows_s[:, pl.ds(after, 128)]
            total = None
            for a in range(3):
                t = a * 9 + b * 3
                taps = [weight[t + e : t + e + 1, pl.ds(phase, 128)] for e in range(3)]
                term = before * taps[0] + mid * taps[1] + behind * taps[2]
                term = term[a : a + LX]
                total = term if total is None else total + term
            edge[side, :, here] = total

    low = low_half(ZH * LY)
    row_at = lax.broadcasted_iota(jnp.int32, (LY, W), 0)
    for xp in range(XP):
        parts = []
        for x in (2 * xp, 2 * xp + 1):
            ref, at = (far, x and x - LX // 2 + 1) if x == 0 or x >= LX // 2 else (near, x - 1)
            pieces = []
            for z in range(ZH):
                here = slice(z * W, (z + 1) * W)
                more = jnp.where(row_at == 0, edge[0, x : x + 1, here], 0.0)
                more = jnp.where(row_at == LY - 1, edge[1, x : x + 1, here], more)
                pieces.append(ref[at, :, here] + more)
            part = jnp.concatenate(pieces, axis=0)
            field[x] = part.astype(BF16)
            parts.append(part)
        first, second = parts
        even = jnp.where(low, first, swap(second)).astype(BF16)
        odd = jnp.where(low, swap(first), second).astype(BF16)
        out = dot(z_fwd[...], jnp.concatenate([even, odd], axis=0))
        freq[:, xp] = out.astype(BF16).reshape(KZ, 2 * LY, W)


def y_forward_kernel(given, y_fwd, out, rows):
    for xp in range(XP):
        data = given[:, xp].reshape(2 * PY * LY, W)
        value = dot(y_fwd[...], data)
        for part in range(2):
            for t in range(W // 128):
                rows[t, pl.ds(part * XP + xp, Q, stride=2 * XP), :] = value[
                    part * Q : (part + 1) * Q, t * 128 : (t + 1) * 128
                ]
    gather(rows, out)


def gather(rows, out):
    count = 2 * XP * Q // PX
    for d in range(PX):
        block = [rows[t, pl.ds(d * count, count), :] for t in range(W // 128)]
        out[d] = jnp.concatenate(block, axis=1).astype(BF16).reshape(out.shape[1:])


def shrink(v):
    return v - jnp.clip(v, -shrink_level, shrink_level)


def spectrum_kernel(given, x_fwd, x_inv, inner, outer, out, rows):
    count = Q // PX
    low = low_half(2 * PX * XP)
    data = [given[:, q].reshape(2 * PX * XP, W) for q in range(count)]
    both = dot(x_fwd[...], jnp.concatenate(data, axis=1))
    spec = []
    for q in range(count):
        part = both[:, q * W : (q + 1) * W]
        part = part[: 2 * Q] + swap(part[2 * Q :])
        spec.append(part[:, :256].astype(BF16))
    mixed = dot(jnp.concatenate(spec, axis=0), inner[...]).reshape(count, 2, Q, 512)
    hidden_r = jnp.tanh(mixed[:, 0, :, :256] - mixed[:, 1, :, 256:])
    hidden_i = jnp.tanh(mixed[:, 0, :, 256:] + mixed[:, 1, :, :256])
    hidden = jnp.stack([hidden_r, hidden_i], axis=1).astype(BF16).reshape(count * 2 * Q, 256)
    mixed = dot(hidden, outer[...]).reshape(count, 2, Q, 2 * W)
    filt_r = shrink(mixed[:, 0, :, :W] - mixed[:, 1, :, W:]).astype(BF16)
    filt_i = shrink(mixed[:, 0, :, W:] + mixed[:, 1, :, :W]).astype(BF16)
    filt = [jnp.concatenate([filt_r[q], filt_i[q]], axis=0) for q in range(count)]
    both = dot(x_inv[...], jnp.concatenate(filt, axis=1))
    for q in range(count):
        part = both[:, q * W : (q + 1) * W]
        back = jnp.where(low, part[: 2 * PX * XP], part[2 * PX * XP :])
        for part in range(2):
            for t in range(W // 128):
                rows[t, pl.ds(part * count + q, PX * XP, stride=2 * count), :] = back[
                    part * PX * XP : (part + 1) * PX * XP, t * 128 : (t + 1) * 128
                ]
    gather(rows, out)


def y_inverse_kernel(given, y_inv, out):
    for xp in range(XP):
        data = given[:, xp].reshape(2 * Q, W)
        out[:, xp] = dot(y_inv[...], data).astype(BF16).reshape(PY, 2 * LY, W)


def z_inverse_kernel(given, z_inv, field, out):
    low = low_half(ZH * LY)
    for xp in range(given.shape[1]):
        data = given[:, xp].reshape(2 * KZ * LY, W)
        value = dot(z_inv[...], data)
        even, odd = value[: ZH * LY], value[ZH * LY :]
        first = jnp.where(low, even, swap(odd)) + field[2 * xp].astype(F32)
        second = jnp.where(low, swap(even), odd) + field[2 * xp + 1].astype(F32)
        for x, value in ((2 * xp, first), (2 * xp + 1, second)):
            for z in range(ZH):
                out[x, :, z * W : (z + 1) * W] = value[z * LY : (z + 1) * LY].astype(BF16)


def call(kernel, outs, scratch=(), name=None):
    return pl.pallas_call(
        kernel,
        out_shape=outs,
        scratch_shapes=list(scratch),
        compiler_params=pltpu.CompilerParams(vmem_limit_bytes=50 * 2**20),
        name=name,
    )


def shape(*dims):
    return jax.ShapeDtypeStruct(dims, BF16)


def block_diagonal(weight, width):
    total = 0
    for b in range(C // CB):
        total = total + jnp.pad(weight[b], ((b * CB, 256 - (b + 1) * CB), (b * CB, width - (b + 1) * CB)))
    return total


def pairs(count, step):
    return [(i, i + step) for i in range(count) if 0 <= i + step < count]


def halos_x(tokens):
    return (
        lax.ppermute(tokens[LX - 1 :], "px", pairs(PX, 1)),
        lax.ppermute(tokens[:1], "px", pairs(PX, -1)),
    )


def halos_y(tokens, xlo, xhi):
    first, last = (
        jnp.concatenate([xlo[:, y], tokens[:, y], xhi[:, y]], axis=0) for y in (0, LY - 1)
    )
    return lax.ppermute(last, "py", pairs(PY, 1)), lax.ppermute(first, "py", pairs(PY, -1))


def body(tokens, conv_weight, inner_weight, outer_weight):
    z_fwd, z_inv, y_fwd, y_inv, x_fwd, x_inv = (jnp.asarray(m) for m in matrices())
    weight = jnp.concatenate([conv_weight, conv_weight], axis=1)
    inner = jnp.concatenate([block_diagonal(w, 256) for w in inner_weight], axis=1)
    outer = [block_diagonal(w, C) for w in outer_weight]
    outer = jnp.concatenate([outer[0], outer[0], outer[1], outer[1]], axis=1)

    wide = MERGED + 2 * C
    xlo, xhi = halos_x(tokens)
    near = call(
        near_kernel,
        jax.ShapeDtypeStruct((LX // 2 - 1, LY, MERGED), F32),
        [VMEM((LX // 2 + 1, LY, wide), F32)],
        name="near",
    )(tokens, weight)
    ylo, yhi = halos_y(tokens, xlo, xhi)
    far = call(
        far_kernel,
        jax.ShapeDtypeStruct((LX // 2 + 1, LY, MERGED), F32),
        [VMEM((LX // 2 + 5, LY, wide), F32)],
        name="far",
    )(tokens, xlo, xhi, weight)
    near, inner, outer = lax.optimization_barrier((near, inner, outer))
    field, freq = call(
        edge_kernel,
        [shape(LX, ZH * LY, W), shape(KZ, XP, 2 * LY, W)],
        [VMEM((LX + 2, wide), F32), VMEM((LX + 2, wide), F32), VMEM((2, LX, MERGED), F32)],
        name="edge_z",
    )(near, far, ylo, yhi, weight, z_fwd)
    rows = VMEM((W // 128, 2 * XP * Q, 128), F32)
    freq = lax.all_to_all(freq, "py", 0, 0, tiled=True)
    freq = call(y_forward_kernel, shape(PX, Q // PX, 2 * XP, W), [rows], name="y_fwd")(freq, y_fwd)
    freq = lax.all_to_all(freq, "px", 0, 0, tiled=True)
    freq = call(spectrum_kernel, shape(PX, XP, 2 * Q // PX, W), [rows], name="spec")(
        freq, x_fwd, x_inv, inner, outer
    )
    freq = lax.all_to_all(freq, "px", 0, 0, tiled=True)
    freq = call(y_inverse_kernel, shape(PY, XP, 2 * LY, W), name="y_inv")(freq, y_inv)
    freq = lax.all_to_all(freq, "py", 0, 0, tiled=True)
    steps = 4
    return pl.pallas_call(
        z_inverse_kernel,
        out_shape=shape(LX, LY, MERGED),
        grid=(steps,),
        in_specs=[
            pl.BlockSpec((KZ, XP // steps, 2 * LY, W), lambda i: (0, i, 0, 0)),
            pl.BlockSpec(z_inv.shape, lambda i: (0, 0)),
            pl.BlockSpec((LX // steps, ZH * LY, W), lambda i: (i, 0, 0)),
        ],
        out_specs=pl.BlockSpec((LX // steps, LY, MERGED), lambda i: (i, 0, 0)),
        compiler_params=pltpu.CompilerParams(vmem_limit_bytes=50 * 2**20),
        name="z_inv",
    )(freq, z_inv, field)


def solution(mesh):
    in_specs = (P("px", "py", None), P(), P(), P())
    out_specs = P("px", "py", None)
    return jax.shard_map(body, mesh=mesh, in_specs=in_specs, out_specs=out_specs, check_vma=False)
```

```python
import functools
import math

import jax
import jax.numpy as jnp
import ml_dtypes
import numpy as np
from jax import lax
from jax.experimental import pallas as pl
from jax.experimental.pallas import tpu as pltpu
from jax.sharding import PartitionSpec as P

shrink_level = 0.2
F32 = jnp.float32
BF16 = jnp.bfloat16
VMEM = pltpu.VMEM

PX, PY = 8, 16
LX, LY = 16, 8
Z, KZ, C, CB = 32, 16, 192, 96
W = 2 * C
MERGED = Z * C
XP = LX // 2
ZH = Z // 2
Q = 64


def tables(length, modes, weights):
    product = np.asarray(modes)[:, None] * np.arange(length)[None, :] % length
    angle = product.astype(np.float32) * np.float32(2.0 * math.pi / length)
    factor = np.asarray(weights, np.float32)[:, None] / np.float32(math.sqrt(length))
    rounded = [(f(angle) * factor).astype(ml_dtypes.bfloat16) for f in (np.cos, np.sin)]
    return [t.astype(np.float64) for t in rounded]


def kept(length):
    return np.concatenate([np.arange(length // 4), np.arange(length - length // 4, length)])


def forward(cos, sin):
    return np.stack([np.stack([cos, sin], 1), np.stack([-sin, cos], 1)])


def backward(cos, sin):
    cos, sin = cos.T, sin.T
    return np.stack([np.stack([cos, -sin], 1), np.stack([sin, cos], 1)])


def as_bf16(matrix):
    return np.ascontiguousarray(matrix).astype(ml_dtypes.bfloat16)


@functools.cache
def matrices():
    eye = np.eye(LY)
    one = np.ones(KZ)
    cz, sz = tables(Z, np.arange(KZ), one)
    both = np.stack([cz, -sz], 1).reshape(KZ, 2, ZH, 2)
    z_fwd = np.einsum("kpzs,yw->kpyszw", both, eye).reshape(KZ * 2 * LY, 2 * ZH * LY)
    two = np.where(np.arange(KZ) == 0, 1.0, 2.0)
    cz, sz = tables(Z, np.arange(KZ), two)
    both = np.stack([cz, -sz], 1).reshape(KZ, 2, ZH, 2)
    z_inv = np.einsum("kpzs,yw->szykpw", both, eye).reshape(2 * ZH * LY, KZ * 2 * LY)
    n = PY * LY
    cy, sy = tables(n, kept(n), np.ones(Q))
    y_fwd = forward(cy, sy).reshape(2, Q, 2, PY, LY).transpose(0, 1, 3, 2, 4).reshape(2 * Q, 2 * n)
    y_inv = backward(cy, sy).reshape(2, PY, LY, 2, PX, Q // PX)
    y_inv = y_inv.transpose(1, 0, 2, 4, 3, 5).reshape(2 * n, 2 * Q)
    n = PX * LX
    cx, sx = tables(n, kept(n), np.ones(Q))
    x_fwd = forward(cx, sx).reshape(2, Q, 2, PX, XP, 2)
    x_fwd = x_fwd.transpose(5, 0, 1, 3, 2, 4).reshape(4 * Q, 2 * PX * XP)
    x_inv = backward(cx, sx).reshape(2, PX, XP, 2, 2, Q)
    x_inv = x_inv.transpose(3, 0, 1, 2, 4, 5).reshape(4 * PX * XP, 2 * Q)
    pick = np.zeros((64, LX + 2, LY))
    for i in range(LX + 2):
        pick[i, i, 0] = pick[32 + i, i, LY - 1] = 1
    pick = pick.reshape(64, (LX + 2) * LY)
    return [as_bf16(m) for m in (z_fwd, z_inv, y_fwd, y_inv, x_fwd, x_inv, pick)]


def dot(a, b):
    return jnp.dot(a, b, preferred_element_type=F32)


def low_half(rows):
    return lax.broadcasted_iota(jnp.int32, (rows, W), 1) < C


def swap(value):
    return pltpu.roll(value, C, 1)


def conv_rows(rows, weight, out, shifted):
    pad = jnp.zeros((LY, C), F32)
    flat = [row for run in rows for row in run]
    for i, (ref, x) in enumerate(flat):
        shifted[i] = jnp.concatenate([pad, ref[x].astype(F32), pad], axis=1)
    row_at = lax.broadcasted_iota(jnp.int32, (LY, 128), 0)

    @pl.loop(0, MERGED // 128)
    def _(j):
        at = pl.multiple_of(j * 128, 128)
        after = pl.multiple_of(j * 128 + W, 128)
        here = pl.ds(at, 128)
        phase = pl.multiple_of(lax.rem(j, 3) * 128, 128)
        wide = [jnp.broadcast_to(weight[t : t + 1, pl.ds(phase, 128)], (LY, 128)) for t in range(27)]
        done = slot = 0
        for run in rows:
            sums = {}
            for i, (ref, x) in enumerate(run):
                mid = ref[x, :, here].astype(F32)
                before = shifted[slot, :, here]
                behind = shifted[slot, :, pl.ds(after, 128)]
                slot += 1
                for a in range(3):
                    to = i - a
                    if not 0 <= to < len(run) - 2:
                        continue
                    for b in range(3):
                        t = a * 9 + b * 3
                        term = before * wide[t] + mid * wide[t + 1] + behind * wide[t + 2]
                        sums[to, b] = sums[to, b] + term if (to, b) in sums else term
                if i >= 2:
                    to = i - 2
                    down = pltpu.roll(sums.pop((to, 0)), 1, 0)
                    up = pltpu.roll(sums.pop((to, 2)), LY - 1, 0)
                    down = jnp.where(row_at == 0, 0.0, down)
                    up = jnp.where(row_at == LY - 1, 0.0, up)
                    out[done, :, here] = sums.pop((to, 1)) + down + up
                    done += 1


PIECES = (((1, 5),), ((5, 8),), ((8, 11),), ((0, 1), (11, 16)))


def piece_kernel(runs, *refs):
    if len(refs) == 4:
        tok, weight, out, shifted = refs
    else:
        tok, xlo, xhi, weight, out, shifted = refs
    rows = []
    for first, end in runs:
        run = [(tok, x) for x in range(max(first - 1, 0), min(end + 1, LX))]
        if first == 0:
            run = [(xlo, 0)] + run
        if end == LX:
            run = run + [(xhi, 0)]
        rows.append(run)
    conv_rows(rows, weight, out, shifted)


def piece(at, *operands):
    runs = PIECES[at]
    made = sum(end - first for first, end in runs)
    wide = MERGED + 2 * C
    return call(
        functools.partial(piece_kernel, runs),
        jax.ShapeDtypeStruct((made, LY, MERGED), F32),
        [VMEM((made + 2 * len(runs), LY, wide), F32)],
        name=f"conv{at}",
        cost=pl.CostEstimate(flops=1, bytes_accessed=1, transcendentals=0),
    )(*operands)


def find(x):
    for at, runs in enumerate(PIECES):
        row = 0
        for first, end in runs:
            if first <= x < end:
                return at, row + x - first
            row += end - first


def rows_kernel(tok, xlo, xhi, pick, first, last):
    step = MERGED // 4
    for j in range(4):
        here = slice(j * step, (j + 1) * step)
        parts = [ref[:, :, here].astype(F32) for ref in (xlo, tok, xhi)]
        data = jnp.concatenate(parts, axis=0).reshape((LX + 2) * LY, step).astype(BF16)
        out = dot(pick[...], data).astype(BF16)
        first[:, here] = out[: LX + 2]
        last[:, here] = out[32 : 32 + LX + 2]


def edge_kernel(*refs):
    pieces, refs = refs[: len(PIECES)], refs[len(PIECES) :]
    ylo, yhi, weight, z_fwd, field, freq, ylo_s, yhi_s, edge = refs
    pad = jnp.zeros((LX + 2, C), F32)
    ylo_s[...] = jnp.concatenate([pad, ylo[...].astype(F32), pad], axis=1)
    yhi_s[...] = jnp.concatenate([pad, yhi[...].astype(F32), pad], axis=1)

    @pl.loop(0, MERGED // 128)
    def _(j):
        at = pl.multiple_of(j * 128, 128)
        after = pl.multiple_of(j * 128 + W, 128)
        here = pl.ds(at, 128)
        phase = pl.multiple_of(lax.rem(j, 3) * 128, 128)
        for side, rows, rows_s, b in ((0, ylo, ylo_s, 0), (1, yhi, yhi_s, 2)):
            mid = rows[:, here].astype(F32)
            before = rows_s[:, here]
            behind = rows_s[:, pl.ds(after, 128)]
            total = None
            for a in range(3):
                t = a * 9 + b * 3
                taps = [weight[t + e : t + e + 1, pl.ds(phase, 128)] for e in range(3)]
                term = before * taps[0] + mid * taps[1] + behind * taps[2]
                term = term[a : a + LX]
                total = term if total is None else total + term
            edge[side, :, here] = total

    low = low_half(ZH * LY)
    row_at = lax.broadcasted_iota(jnp.int32, (LY, W), 0)
    for xp in range(XP):
        parts = []
        for x in (2 * xp, 2 * xp + 1):
            ref, at = find(x)
            ref = pieces[ref]
            rows = []
            for z in range(ZH):
                here = slice(z * W, (z + 1) * W)
                more = jnp.where(row_at == 0, edge[0, x : x + 1, here], 0.0)
                more = jnp.where(row_at == LY - 1, edge[1, x : x + 1, here], more)
                rows.append(ref[at, :, here] + more)
            part = jnp.concatenate(rows, axis=0)
            field[x] = part.astype(BF16)
            parts.append(part)
        first, second = parts
        even = jnp.where(low, first, swap(second)).astype(BF16)
        odd = jnp.where(low, swap(first), second).astype(BF16)
        out = dot(z_fwd[...], jnp.concatenate([even, odd], axis=0))
        freq[:, xp] = out.astype(BF16).reshape(KZ, 2 * LY, W)


def y_forward_kernel(given, y_fwd, out, rows):
    for xp in range(XP):
        data = given[:, xp].reshape(2 * PY * LY, W)
        value = dot(y_fwd[...], data)
        for part in range(2):
            for t in range(W // 128):
                rows[t, pl.ds(part * XP + xp, Q, stride=2 * XP), :] = value[
                    part * Q : (part + 1) * Q, t * 128 : (t + 1) * 128
                ]
    gather(rows, out)


def gather(rows, out):
    count = 2 * XP * Q // PX
    for d in range(PX):
        block = [rows[t, pl.ds(d * count, count), :] for t in range(W // 128)]
        out[d] = jnp.concatenate(block, axis=1).astype(BF16).reshape(out.shape[1:])


def shrink(v):
    return v - jnp.clip(v, -shrink_level, shrink_level)


def spectrum_kernel(given, x_fwd, x_inv, inner, outer, out, rows):
    count = Q // PX
    low = low_half(2 * PX * XP)
    data = [given[:, q].reshape(2 * PX * XP, W) for q in range(count)]
    both = dot(x_fwd[...], jnp.concatenate(data, axis=1))
    spec = []
    for q in range(count):
        part = both[:, q * W : (q + 1) * W]
        part = part[: 2 * Q] + swap(part[2 * Q :])
        spec.append(part[:, :256].astype(BF16))
    mixed = dot(jnp.concatenate(spec, axis=0), inner[...]).reshape(count, 2, Q, 512)
    hidden_r = jnp.tanh(mixed[:, 0, :, :256] - mixed[:, 1, :, 256:])
    hidden_i = jnp.tanh(mixed[:, 0, :, 256:] + mixed[:, 1, :, :256])
    hidden = jnp.stack([hidden_r, hidden_i], axis=1).astype(BF16).reshape(count * 2 * Q, 256)
    mixed = dot(hidden, outer[...]).reshape(count, 2, Q, 2 * W)
    filt_r = shrink(mixed[:, 0, :, :W] - mixed[:, 1, :, W:]).astype(BF16)
    filt_i = shrink(mixed[:, 0, :, W:] + mixed[:, 1, :, :W]).astype(BF16)
    filt = [jnp.concatenate([filt_r[q], filt_i[q]], axis=0) for q in range(count)]
    both = dot(x_inv[...], jnp.concatenate(filt, axis=1))
    for q in range(count):
        part = both[:, q * W : (q + 1) * W]
        back = jnp.where(low, part[: 2 * PX * XP], part[2 * PX * XP :])
        for part in range(2):
            for t in range(W // 128):
                rows[t, pl.ds(part * count + q, PX * XP, stride=2 * count), :] = back[
                    part * PX * XP : (part + 1) * PX * XP, t * 128 : (t + 1) * 128
                ]
    gather(rows, out)


def y_inverse_kernel(given, y_inv, out):
    for xp in range(XP):
        data = given[:, xp].reshape(2 * Q, W)
        out[:, xp] = dot(y_inv[...], data).astype(BF16).reshape(PY, 2 * LY, W)


def z_inverse_kernel(given, z_inv, field, out):
    low = low_half(ZH * LY)
    for xp in range(given.shape[1]):
        data = given[:, xp].reshape(2 * KZ * LY, W)
        value = dot(z_inv[...], data)
        even, odd = value[: ZH * LY], value[ZH * LY :]
        first = jnp.where(low, even, swap(odd)) + field[2 * xp].astype(F32)
        second = jnp.where(low, swap(even), odd) + field[2 * xp + 1].astype(F32)
        for x, value in ((2 * xp, first), (2 * xp + 1, second)):
            for z in range(ZH):
                out[x, :, z * W : (z + 1) * W] = value[z * LY : (z + 1) * LY].astype(BF16)


def call(kernel, outs, scratch=(), name=None, cost=None):
    return pl.pallas_call(
        kernel,
        out_shape=outs,
        scratch_shapes=list(scratch),
        compiler_params=pltpu.CompilerParams(vmem_limit_bytes=20 * 2**20),
        cost_estimate=cost,
        name=name,
    )


def shape(*dims):
    return jax.ShapeDtypeStruct(dims, BF16)


def block_diagonal(weight, width):
    total = 0
    for b in range(C // CB):
        total = total + jnp.pad(weight[b], ((b * CB, 256 - (b + 1) * CB), (b * CB, width - (b + 1) * CB)))
    return total


def pairs(count, step):
    return [(i, i + step) for i in range(count) if 0 <= i + step < count]


def body(tokens, conv_weight, inner_weight, outer_weight):
    z_fwd, z_inv, y_fwd, y_inv, x_fwd, x_inv, pick = (jnp.asarray(m) for m in matrices())
    weight = jnp.concatenate([conv_weight, conv_weight], axis=1)
    inner = jnp.concatenate([block_diagonal(w, 256) for w in inner_weight], axis=1)
    outer = [block_diagonal(w, C) for w in outer_weight]
    outer = jnp.concatenate([outer[0], outer[0], outer[1], outer[1]], axis=1)

    wide = MERGED + 2 * C
    xlo = lax.ppermute(tokens[LX - 1 :], "px", pairs(PX, 1))
    piece0 = piece(0, tokens, weight)
    piece0, bottom, xlo = lax.optimization_barrier((piece0, tokens[:1], xlo))
    xhi = lax.ppermute(bottom, "px", pairs(PX, -1))
    tokens, bottom = lax.optimization_barrier((tokens, bottom))
    piece1 = piece(1, tokens, weight)
    piece1, xlo, xhi = lax.optimization_barrier((piece1, xlo, xhi))
    first, last = call(rows_kernel, [shape(LX + 2, MERGED)] * 2, name="y_rows")(tokens, xlo, xhi, pick)
    ylo = lax.ppermute(last, "py", pairs(PY, 1))
    tokens, last = lax.optimization_barrier((tokens, last))
    piece2 = piece(2, tokens, weight)
    piece2, first = lax.optimization_barrier((piece2, first))
    yhi = lax.ppermute(first, "py", pairs(PY, -1))
    piece3 = piece(3, tokens, xlo, xhi, weight)
    piece3, inner, outer = lax.optimization_barrier((piece3, inner, outer))
    field, freq = call(
        edge_kernel,
        [shape(LX, ZH * LY, W), shape(KZ, XP, 2 * LY, W)],
        [VMEM((LX + 2, wide), F32), VMEM((LX + 2, wide), F32), VMEM((2, LX, MERGED), F32)],
        name="edge_z",
    )(piece0, piece1, piece2, piece3, ylo, yhi, weight, z_fwd)
    rows = VMEM((W // 128, 2 * XP * Q, 128), F32)
    freq = lax.all_to_all(freq, "py", 0, 0, tiled=True)
    freq = call(y_forward_kernel, shape(PX, Q // PX, 2 * XP, W), [rows], name="y_fwd")(freq, y_fwd)
    freq = lax.all_to_all(freq, "px", 0, 0, tiled=True)
    freq = call(spectrum_kernel, shape(PX, XP, 2 * Q // PX, W), [rows], name="spec")(
        freq, x_fwd, x_inv, inner, outer
    )
    freq = lax.all_to_all(freq, "px", 0, 0, tiled=True)
    freq = call(y_inverse_kernel, shape(PY, XP, 2 * LY, W), name="y_inv")(freq, y_inv)
    freq = lax.all_to_all(freq, "py", 0, 0, tiled=True)
    steps = 4
    return pl.pallas_call(
        z_inverse_kernel,
        out_shape=shape(LX, LY, MERGED),
        grid=(steps,),
        in_specs=[
            pl.BlockSpec((KZ, XP // steps, 2 * LY, W), lambda i: (0, i, 0, 0)),
            pl.BlockSpec(z_inv.shape, lambda i: (0, 0)),
            pl.BlockSpec((LX // steps, ZH * LY, W), lambda i: (i, 0, 0)),
        ],
        out_specs=pl.BlockSpec((LX // steps, LY, MERGED), lambda i: (i, 0, 0)),
        compiler_params=pltpu.CompilerParams(vmem_limit_bytes=20 * 2**20),
        name="z_inv",
    )(freq, z_inv, field)


def solution(mesh):
    in_specs = (P("px", "py", None), P(), P(), P())
    out_specs = P("px", "py", None)
    return jax.shard_map(body, mesh=mesh, in_specs=in_specs, out_specs=out_specs, check_vma=False)
```

```python
import functools
import math

import jax
import jax.numpy as jnp
import ml_dtypes
import numpy as np
from jax import lax
from jax.experimental import pallas as pl
from jax.experimental.pallas import tpu as pltpu
from jax.sharding import PartitionSpec as P

shrink_level = 0.2
F32 = jnp.float32
BF16 = jnp.bfloat16
VMEM = pltpu.VMEM

PX, PY = 8, 16
LX, LY = 16, 8
Z, KZ, C, CB = 32, 16, 192, 96
W = 2 * C
MERGED = Z * C
XP = LX // 2
ZH = Z // 2
Q = 64


def tables(length, modes, weights):
    product = np.asarray(modes)[:, None] * np.arange(length)[None, :] % length
    angle = product.astype(np.float32) * np.float32(2.0 * math.pi / length)
    factor = np.asarray(weights, np.float32)[:, None] / np.float32(math.sqrt(length))
    rounded = [(f(angle) * factor).astype(ml_dtypes.bfloat16) for f in (np.cos, np.sin)]
    return [t.astype(np.float64) for t in rounded]


def kept(length):
    return np.concatenate([np.arange(length // 4), np.arange(length - length // 4, length)])


def forward(cos, sin):
    return np.stack([np.stack([cos, sin], 1), np.stack([-sin, cos], 1)])


def backward(cos, sin):
    cos, sin = cos.T, sin.T
    return np.stack([np.stack([cos, -sin], 1), np.stack([sin, cos], 1)])


def as_bf16(matrix):
    return np.ascontiguousarray(matrix).astype(ml_dtypes.bfloat16)


@functools.cache
def matrices():
    eye = np.eye(LY)
    one = np.ones(KZ)
    cz, sz = tables(Z, np.arange(KZ), one)
    both = np.stack([cz, -sz], 1).reshape(KZ, 2, ZH, 2)
    z_fwd = np.einsum("kpzs,yw->kpyszw", both, eye).reshape(KZ * 2 * LY, 2 * ZH * LY)
    two = np.where(np.arange(KZ) == 0, 1.0, 2.0)
    cz, sz = tables(Z, np.arange(KZ), two)
    both = np.stack([cz, -sz], 1).reshape(KZ, 2, ZH, 2)
    z_inv = np.einsum("kpzs,yw->szykpw", both, eye).reshape(2 * ZH * LY, KZ * 2 * LY)
    n = PY * LY
    cy, sy = tables(n, kept(n), np.ones(Q))
    y_fwd = forward(cy, sy).reshape(2, Q, 2, PY, LY).transpose(0, 1, 3, 2, 4).reshape(2 * Q, 2 * n)
    y_inv = backward(cy, sy).reshape(2, PY, LY, 2, PX, Q // PX)
    y_inv = y_inv.transpose(1, 0, 2, 4, 3, 5).reshape(2 * n, 2 * Q)
    n = PX * LX
    cx, sx = tables(n, kept(n), np.ones(Q))
    x_fwd = forward(cx, sx).reshape(2, Q, 2, PX, XP, 2)
    x_fwd = x_fwd.transpose(5, 0, 1, 3, 2, 4).reshape(4 * Q, 2 * PX * XP)
    x_inv = backward(cx, sx).reshape(2, PX, XP, 2, 2, Q)
    x_inv = x_inv.transpose(3, 0, 1, 2, 4, 5).reshape(4 * PX * XP, 2 * Q)
    pick = np.zeros((64, LX + 2, LY))
    for i in range(LX + 2):
        pick[i, i, 0] = pick[32 + i, i, LY - 1] = 1
    pick = pick.reshape(64, (LX + 2) * LY)
    return [as_bf16(m) for m in (z_fwd, z_inv, y_fwd, y_inv, x_fwd, x_inv, pick)]


def dot(a, b):
    return jnp.dot(a, b, preferred_element_type=F32)


def low_half(rows):
    return lax.broadcasted_iota(jnp.int32, (rows, W), 1) < C


def swap(value):
    return pltpu.roll(value, C, 1)


def conv_rows(rows, narrow, out, shifted, weight):
    weight[...] = jnp.concatenate([narrow[...], narrow[...]], axis=1)
    pad = jnp.zeros((LY, C), F32)
    flat = [row for run in rows for row in run]
    for i, (ref, x) in enumerate(flat):
        shifted[i] = jnp.concatenate([pad, ref[x].astype(F32), pad], axis=1)
    row_at = lax.broadcasted_iota(jnp.int32, (LY, 128), 0)

    @pl.loop(0, MERGED // 128)
    def _(j):
        at = pl.multiple_of(j * 128, 128)
        after = pl.multiple_of(j * 128 + W, 128)
        here = pl.ds(at, 128)
        phase = pl.multiple_of(lax.rem(j, 3) * 128, 128)
        wide = [jnp.broadcast_to(weight[t : t + 1, pl.ds(phase, 128)], (LY, 128)) for t in range(27)]
        done = slot = 0
        for run in rows:
            sums = {}
            for i, (ref, x) in enumerate(run):
                mid = ref[x, :, here].astype(F32)
                before = shifted[slot, :, here]
                behind = shifted[slot, :, pl.ds(after, 128)]
                slot += 1
                for a in range(3):
                    to = i - a
                    if not 0 <= to < len(run) - 2:
                        continue
                    for b in range(3):
                        t = a * 9 + b * 3
                        term = before * wide[t] + mid * wide[t + 1] + behind * wide[t + 2]
                        sums[to, b] = sums[to, b] + term if (to, b) in sums else term
                if i >= 2:
                    to = i - 2
                    down = pltpu.roll(sums.pop((to, 0)), 1, 0)
                    up = pltpu.roll(sums.pop((to, 2)), LY - 1, 0)
                    down = jnp.where(row_at == 0, 0.0, down)
                    up = jnp.where(row_at == LY - 1, 0.0, up)
                    out[done, :, here] = sums.pop((to, 1)) + down + up
                    done += 1


PIECES = (((1, 8),), ((0, 1), (8, 16)))


def piece_kernel(runs, *refs):
    if len(refs) == 5:
        tok, narrow, out, shifted, weight = refs
    else:
        tok, xlo, xhi, narrow, out, shifted, weight = refs
    rows = []
    for first, end in runs:
        run = [(tok, x) for x in range(max(first - 1, 0), min(end + 1, LX))]
        if first == 0:
            run = [(xlo, 0)] + run
        if end == LX:
            run = run + [(xhi, 0)]
        rows.append(run)
    conv_rows(rows, narrow, out, shifted, weight)


def piece(at, *operands):
    runs = PIECES[at]
    made = sum(end - first for first, end in runs)
    wide = MERGED + 2 * C
    return call(
        functools.partial(piece_kernel, runs),
        jax.ShapeDtypeStruct((made, LY, MERGED), F32),
        [VMEM((made + 2 * len(runs), LY, wide), F32), VMEM((27, W), F32)],
        name=f"conv{at}",
    )(*operands)


def find(x):
    for at, runs in enumerate(PIECES):
        row = 0
        for first, end in runs:
            if first <= x < end:
                return at, row + x - first
            row += end - first


def rows_kernel(tok, xlo, xhi, pick, first, last):
    step = MERGED // 4
    for j in range(4):
        here = slice(j * step, (j + 1) * step)
        parts = [ref[:, :, here].astype(F32) for ref in (xlo, tok, xhi)]
        data = jnp.concatenate(parts, axis=0).reshape((LX + 2) * LY, step).astype(BF16)
        out = dot(pick[...], data).astype(BF16)
        first[:, here] = out[: LX + 2]
        last[:, here] = out[32 : 32 + LX + 2]


def edge_kernel(*refs):
    pieces, refs = refs[: len(PIECES)], refs[len(PIECES) :]
    ylo, yhi, narrow, z_fwd, field, freq, ylo_s, yhi_s, edge, weight = refs
    weight[...] = jnp.concatenate([narrow[...], narrow[...]], axis=1)
    pad = jnp.zeros((LX + 2, C), F32)
    ylo_s[...] = jnp.concatenate([pad, ylo[...].astype(F32), pad], axis=1)
    yhi_s[...] = jnp.concatenate([pad, yhi[...].astype(F32), pad], axis=1)

    @pl.loop(0, MERGED // 128)
    def _(j):
        at = pl.multiple_of(j * 128, 128)
        after = pl.multiple_of(j * 128 + W, 128)
        here = pl.ds(at, 128)
        phase = pl.multiple_of(lax.rem(j, 3) * 128, 128)
        for side, rows, rows_s, b in ((0, ylo, ylo_s, 0), (1, yhi, yhi_s, 2)):
            mid = rows[:, here].astype(F32)
            before = rows_s[:, here]
            behind = rows_s[:, pl.ds(after, 128)]
            total = None
            for a in range(3):
                t = a * 9 + b * 3
                taps = [weight[t + e : t + e + 1, pl.ds(phase, 128)] for e in range(3)]
                term = before * taps[0] + mid * taps[1] + behind * taps[2]
                term = term[a : a + LX]
                total = term if total is None else total + term
            edge[side, :, here] = total

    low = low_half(ZH * LY)
    row_at = lax.broadcasted_iota(jnp.int32, (LY, W), 0)
    for xp in range(XP):
        parts = []
        for x in (2 * xp, 2 * xp + 1):
            ref, at = find(x)
            ref = pieces[ref]
            rows = []
            for z in range(ZH):
                here = slice(z * W, (z + 1) * W)
                more = jnp.where(row_at == 0, edge[0, x : x + 1, here], 0.0)
                more = jnp.where(row_at == LY - 1, edge[1, x : x + 1, here], more)
                rows.append(ref[at, :, here] + more)
            part = jnp.concatenate(rows, axis=0)
            field[x] = part.astype(BF16)
            parts.append(part)
        first, second = parts
        even = jnp.where(low, first, swap(second)).astype(BF16)
        odd = jnp.where(low, swap(first), second).astype(BF16)
        out = dot(z_fwd[...], jnp.concatenate([even, odd], axis=0))
        freq[:, xp] = out.astype(BF16).reshape(KZ, 2 * LY, W)


def y_forward_kernel(given, y_fwd, out, rows):
    for xp in range(XP):
        data = given[:, xp].reshape(2 * PY * LY, W)
        value = dot(y_fwd[...], data)
        for part in range(2):
            for t in range(W // 128):
                rows[t, pl.ds(part * XP + xp, Q, stride=2 * XP), :] = value[
                    part * Q : (part + 1) * Q, t * 128 : (t + 1) * 128
                ]
    gather(rows, out)


def gather(rows, out):
    count = 2 * XP * Q // PX
    for d in range(PX):
        block = [rows[t, pl.ds(d * count, count), :] for t in range(W // 128)]
        out[d] = jnp.concatenate(block, axis=1).astype(BF16).reshape(out.shape[1:])


def shrink(v):
    return v - jnp.clip(v, -shrink_level, shrink_level)


def spectrum_kernel(given, x_fwd, x_inv, inner, outer, out, rows):
    count = Q // PX
    low = low_half(2 * PX * XP)
    data = [given[:, q].reshape(2 * PX * XP, W) for q in range(count)]
    both = dot(x_fwd[...], jnp.concatenate(data, axis=1))
    spec = []
    for q in range(count):
        part = both[:, q * W : (q + 1) * W]
        part = part[: 2 * Q] + swap(part[2 * Q :])
        spec.append(part[:, :256].astype(BF16))
    mixed = dot(jnp.concatenate(spec, axis=0), inner[...]).reshape(count, 2, Q, 512)
    hidden_r = jnp.tanh(mixed[:, 0, :, :256] - mixed[:, 1, :, 256:])
    hidden_i = jnp.tanh(mixed[:, 0, :, 256:] + mixed[:, 1, :, :256])
    hidden = jnp.stack([hidden_r, hidden_i], axis=1).astype(BF16).reshape(count * 2 * Q, 256)
    mixed = dot(hidden, outer[...]).reshape(count, 2, Q, 2 * W)
    filt_r = shrink(mixed[:, 0, :, :W] - mixed[:, 1, :, W:]).astype(BF16)
    filt_i = shrink(mixed[:, 0, :, W:] + mixed[:, 1, :, :W]).astype(BF16)
    filt = [jnp.concatenate([filt_r[q], filt_i[q]], axis=0) for q in range(count)]
    both = dot(x_inv[...], jnp.concatenate(filt, axis=1))
    for q in range(count):
        part = both[:, q * W : (q + 1) * W]
        back = jnp.where(low, part[: 2 * PX * XP], part[2 * PX * XP :])
        for part in range(2):
            for t in range(W // 128):
                rows[t, pl.ds(part * count + q, PX * XP, stride=2 * count), :] = back[
                    part * PX * XP : (part + 1) * PX * XP, t * 128 : (t + 1) * 128
                ]
    gather(rows, out)


def y_inverse_kernel(given, y_inv, out):
    for xp in range(XP):
        data = given[:, xp].reshape(2 * Q, W)
        out[:, xp] = dot(y_inv[...], data).astype(BF16).reshape(PY, 2 * LY, W)


def z_inverse_kernel(given, z_inv, field, out):
    low = low_half(ZH * LY)
    for xp in range(given.shape[1]):
        data = given[:, xp].reshape(2 * KZ * LY, W)
        value = dot(z_inv[...], data)
        even, odd = value[: ZH * LY], value[ZH * LY :]
        first = jnp.where(low, even, swap(odd)) + field[2 * xp].astype(F32)
        second = jnp.where(low, swap(even), odd) + field[2 * xp + 1].astype(F32)
        for x, value in ((2 * xp, first), (2 * xp + 1, second)):
            for z in range(ZH):
                out[x, :, z * W : (z + 1) * W] = value[z * LY : (z + 1) * LY].astype(BF16)


def call(kernel, outs, scratch=(), name=None):
    return pl.pallas_call(
        kernel,
        out_shape=outs,
        scratch_shapes=list(scratch),
        compiler_params=pltpu.CompilerParams(vmem_limit_bytes=20 * 2**20),
        name=name,
    )


def shape(*dims):
    return jax.ShapeDtypeStruct(dims, BF16)


def block_diagonal(weight, width):
    total = 0
    for b in range(C // CB):
        total = total + jnp.pad(weight[b], ((b * CB, 256 - (b + 1) * CB), (b * CB, width - (b + 1) * CB)))
    return total


def pairs(count, step):
    return [(i, i + step) for i in range(count) if 0 <= i + step < count]


def body(tokens, conv_weight, inner_weight, outer_weight):
    z_fwd, z_inv, y_fwd, y_inv, x_fwd, x_inv, pick = (jnp.asarray(m) for m in matrices())
    inner = jnp.concatenate([block_diagonal(w, 256) for w in inner_weight], axis=1)
    outer = [block_diagonal(w, C) for w in outer_weight]
    outer = jnp.concatenate([outer[0], outer[0], outer[1], outer[1]], axis=1)

    wide = MERGED + 2 * C
    xlo = lax.ppermute(tokens[LX - 1 :], "px", pairs(PX, 1))
    xhi = lax.ppermute(tokens[:1], "px", pairs(PX, -1))
    piece0 = piece(0, tokens, conv_weight)
    piece0, xlo, xhi = lax.optimization_barrier((piece0, xlo, xhi))
    first, last = call(rows_kernel, [shape(LX + 2, MERGED)] * 2, name="y_rows")(tokens, xlo, xhi, pick)
    ylo = lax.ppermute(last, "py", pairs(PY, 1))
    yhi = lax.ppermute(first, "py", pairs(PY, -1))
    piece1 = piece(1, tokens, xlo, xhi, conv_weight)
    piece1, inner, outer = lax.optimization_barrier((piece1, inner, outer))
    field, freq = call(
        edge_kernel,
        [shape(LX, ZH * LY, W), shape(KZ, XP, 2 * LY, W)],
        [VMEM((LX + 2, wide), F32), VMEM((LX + 2, wide), F32), VMEM((2, LX, MERGED), F32), VMEM((27, W), F32)],
        name="edge_z",
    )(piece0, piece1, ylo, yhi, conv_weight, z_fwd)
    rows = VMEM((W // 128, 2 * XP * Q, 128), F32)
    freq = lax.all_to_all(freq, "py", 0, 0, tiled=True)
    freq = call(y_forward_kernel, shape(PX, Q // PX, 2 * XP, W), [rows], name="y_fwd")(freq, y_fwd)
    freq = lax.all_to_all(freq, "px", 0, 0, tiled=True)
    freq = call(spectrum_kernel, shape(PX, XP, 2 * Q // PX, W), [rows], name="spec")(
        freq, x_fwd, x_inv, inner, outer
    )
    freq = lax.all_to_all(freq, "px", 0, 0, tiled=True)
    freq = call(y_inverse_kernel, shape(PY, XP, 2 * LY, W), name="y_inv")(freq, y_inv)
    freq = lax.all_to_all(freq, "py", 0, 0, tiled=True)
    steps = 4
    return pl.pallas_call(
        z_inverse_kernel,
        out_shape=shape(LX, LY, MERGED),
        grid=(steps,),
        in_specs=[
            pl.BlockSpec((KZ, XP // steps, 2 * LY, W), lambda i: (0, i, 0, 0)),
            pl.BlockSpec(z_inv.shape, lambda i: (0, 0)),
            pl.BlockSpec((LX // steps, ZH * LY, W), lambda i: (i, 0, 0)),
        ],
        out_specs=pl.BlockSpec((LX // steps, LY, MERGED), lambda i: (i, 0, 0)),
        compiler_params=pltpu.CompilerParams(vmem_limit_bytes=20 * 2**20),
        name="z_inv",
    )(freq, z_inv, field)


def solution(mesh):
    in_specs = (P("px", "py", None), P(), P(), P())
    out_specs = P("px", "py", None)
    return jax.shard_map(body, mesh=mesh, in_specs=in_specs, out_specs=out_specs, check_vma=False)
```

```python
import functools
import math

import jax
import jax.numpy as jnp
import ml_dtypes
import numpy as np
from jax import lax
from jax.experimental import pallas as pl
from jax.experimental.pallas import tpu as pltpu
from jax.sharding import PartitionSpec as P

shrink_level = 0.2
F32 = jnp.float32
BF16 = jnp.bfloat16
VMEM = pltpu.VMEM

PX, PY = 8, 16
LX, LY = 16, 8
Z, KZ, C, CB = 32, 16, 192, 96
W = 2 * C
MERGED = Z * C
XP = LX // 2
ZH = Z // 2
Q = 64


def tables(length, modes, weights):
    product = np.asarray(modes)[:, None] * np.arange(length)[None, :] % length
    angle = product.astype(np.float32) * np.float32(2.0 * math.pi / length)
    factor = np.asarray(weights, np.float32)[:, None] / np.float32(math.sqrt(length))
    rounded = [(f(angle) * factor).astype(ml_dtypes.bfloat16) for f in (np.cos, np.sin)]
    return [t.astype(np.float64) for t in rounded]


def kept(length):
    return np.concatenate([np.arange(length // 4), np.arange(length - length // 4, length)])


def forward(cos, sin):
    return np.stack([np.stack([cos, sin], 1), np.stack([-sin, cos], 1)])


def backward(cos, sin):
    cos, sin = cos.T, sin.T
    return np.stack([np.stack([cos, -sin], 1), np.stack([sin, cos], 1)])


def as_bf16(matrix):
    return np.ascontiguousarray(matrix).astype(ml_dtypes.bfloat16)


@functools.cache
def matrices():
    eye = np.eye(LY)
    one = np.ones(KZ)
    cz, sz = tables(Z, np.arange(KZ), one)
    both = np.stack([cz, -sz], 1).reshape(KZ, 2, ZH, 2)
    z_fwd = np.einsum("kpzs,yw->kpyszw", both, eye).reshape(KZ * 2 * LY, 2 * ZH * LY)
    two = np.where(np.arange(KZ) == 0, 1.0, 2.0)
    cz, sz = tables(Z, np.arange(KZ), two)
    both = np.stack([cz, -sz], 1).reshape(KZ, 2, ZH, 2)
    z_inv = np.einsum("kpzs,yw->szykpw", both, eye).reshape(2 * ZH * LY, KZ * 2 * LY)
    n = PY * LY
    cy, sy = tables(n, kept(n), np.ones(Q))
    y_fwd = forward(cy, sy).reshape(2, Q, 2, PY, LY).transpose(0, 1, 3, 2, 4).reshape(2 * Q, 2 * n)
    y_inv = backward(cy, sy).reshape(2, PY, LY, 2, PX, Q // PX)
    y_inv = y_inv.transpose(1, 0, 2, 4, 3, 5).reshape(2 * n, 2 * Q)
    n = PX * LX
    cx, sx = tables(n, kept(n), np.ones(Q))
    x_fwd = forward(cx, sx).reshape(2, Q, 2, PX, XP, 2)
    x_fwd = x_fwd.transpose(5, 0, 1, 3, 2, 4).reshape(4 * Q, 2 * PX * XP)
    x_inv = backward(cx, sx).reshape(2, PX, XP, 2, 2, Q)
    x_inv = x_inv.transpose(3, 0, 1, 2, 4, 5).reshape(4 * PX * XP, 2 * Q)
    pick = np.zeros((64, LX + 2, LY))
    for i in range(LX + 2):
        pick[i, i, 0] = pick[32 + i, i, LY - 1] = 1
    pick = pick.reshape(64, (LX + 2) * LY)
    return [as_bf16(m) for m in (z_fwd, z_inv, y_fwd, y_inv, x_fwd, x_inv, pick)]


def dot(a, b):
    return jnp.dot(a, b, preferred_element_type=F32)


def low_half(rows):
    return lax.broadcasted_iota(jnp.int32, (rows, W), 1) < C


def swap(value):
    return pltpu.roll(value, C, 1)


def conv_rows(rows, weight, out, shifted):
    pad = jnp.zeros((LY, C), F32)
    flat = [row for run in rows for row in run]
    for i, (ref, x) in enumerate(flat):
        shifted[i] = jnp.concatenate([pad, ref[x].astype(F32), pad], axis=1)
    row_at = lax.broadcasted_iota(jnp.int32, (LY, 128), 0)

    @pl.loop(0, MERGED // 128)
    def _(j):
        at = pl.multiple_of(j * 128, 128)
        after = pl.multiple_of(j * 128 + W, 128)
        here = pl.ds(at, 128)
        phase = pl.multiple_of(lax.rem(j, 3) * 128, 128)
        wide = [jnp.broadcast_to(weight[t : t + 1, pl.ds(phase, 128)], (LY, 128)) for t in range(27)]
        done = slot = 0
        for run in rows:
            sums = {}
            for i, (ref, x) in enumerate(run):
                mid = ref[x, :, here].astype(F32)
                before = shifted[slot, :, here]
                behind = shifted[slot, :, pl.ds(after, 128)]
                slot += 1
                for a in range(3):
                    to = i - a
                    if not 0 <= to < len(run) - 2:
                        continue
                    for b in range(3):
                        t = a * 9 + b * 3
                        term = before * wide[t] + mid * wide[t + 1] + behind * wide[t + 2]
                        sums[to, b] = sums[to, b] + term if (to, b) in sums else term
                if i >= 2:
                    to = i - 2
                    down = pltpu.roll(sums.pop((to, 0)), 1, 0)
                    up = pltpu.roll(sums.pop((to, 2)), LY - 1, 0)
                    down = jnp.where(row_at == 0, 0.0, down)
                    up = jnp.where(row_at == LY - 1, 0.0, up)
                    out[done, :, here] = sums.pop((to, 1)) + down + up
                    done += 1


PIECES = (((1, 8),), ((0, 1), (8, 16)))


def odd(axis):
    return lax.rem(lax.axis_index(axis), 2) == 1


def by_order(axis, first, second):
    second, first = second.astype(F32), first.astype(F32)
    up = odd(axis)
    return jnp.where(up, first, second), jnp.where(up, second, first)


def start_kernel(tok, narrow_hbm, first, second, weight, narrow, sem):
    copy = pltpu.make_async_copy(narrow_hbm, narrow, sem)
    copy.start()
    below, above = tok[0].astype(F32), tok[LX - 1].astype(F32)
    up = odd("px")
    first[0] = jnp.where(up, below, above).astype(BF16)
    second[0] = jnp.where(up, above, below).astype(BF16)
    copy.wait()
    weight[...] = jnp.concatenate([narrow[...], narrow[...]], axis=1)


def inside_kernel(tok, weight, out, shifted):
    conv_rows([[(tok, x) for x in range(first - 1, end + 1)] for first, end in PIECES[0]], weight, out, shifted)


def border_kernel(tok, first, second, weight, out, shifted, sides):
    sides[0], sides[1] = by_order("px", first[0], second[0])
    rows = []
    for start, end in PIECES[1]:
        run = [(tok, x) for x in range(max(start - 1, 0), min(end + 1, LX))]
        if start == 0:
            run = [(sides, 0)] + run
        if end == LX:
            run = run + [(sides, 1)]
        rows.append(run)
    conv_rows(rows, weight, out, shifted)


def piece(at, kernel, extra, *operands):
    runs = PIECES[at]
    made = sum(end - first for first, end in runs)
    return call(
        kernel,
        jax.ShapeDtypeStruct((made, LY, MERGED), F32),
        [VMEM((made + 2 * len(runs), LY, MERGED + 2 * C), F32)] + extra,
        name=f"conv{at}",
    )(*operands)


def find(x):
    for at, runs in enumerate(PIECES):
        row = 0
        for first, end in runs:
            if first <= x < end:
                return at, row + x - first
            row += end - first


def rows_kernel(tok, first, second, pick, send_first, send_second):
    step = MERGED // 4
    up = odd("py")
    for j in range(4):
        here = slice(j * step, (j + 1) * step)
        lo, hi = by_order("px", first[:, :, here], second[:, :, here])
        data = jnp.concatenate([lo, tok[:, :, here].astype(F32), hi], axis=0)
        out = dot(pick[...], data.reshape((LX + 2) * LY, step).astype(BF16))
        below, above = out[: LX + 2], out[32 : 32 + LX + 2]
        send_first[:, here] = jnp.where(up, below, above).astype(BF16)
        send_second[:, here] = jnp.where(up, above, below).astype(BF16)


def edge_kernel(*refs):
    pieces, refs = refs[: len(PIECES)], refs[len(PIECES) :]
    first, second, weight, z_fwd, field, freq, ylo, yhi, ylo_s, yhi_s, edge = refs
    pad = jnp.zeros((LX + 2, C), F32)
    ylo[...], yhi[...] = by_order("py", first[...], second[...])
    ylo_s[...] = jnp.concatenate([pad, ylo[...], pad], axis=1)
    yhi_s[...] = jnp.concatenate([pad, yhi[...], pad], axis=1)

    @pl.loop(0, MERGED // 128)
    def _(j):
        at = pl.multiple_of(j * 128, 128)
        after = pl.multiple_of(j * 128 + W, 128)
        here = pl.ds(at, 128)
        phase = pl.multiple_of(lax.rem(j, 3) * 128, 128)
        for side, rows, rows_s, b in ((0, ylo, ylo_s, 0), (1, yhi, yhi_s, 2)):
            mid = rows[:, here]
            before = rows_s[:, here]
            behind = rows_s[:, pl.ds(after, 128)]
            total = None
            for a in range(3):
                t = a * 9 + b * 3
                taps = [weight[t + e : t + e + 1, pl.ds(phase, 128)] for e in range(3)]
                term = before * taps[0] + mid * taps[1] + behind * taps[2]
                term = term[a : a + LX]
                total = term if total is None else total + term
            edge[side, :, here] = total

    low = low_half(ZH * LY)
    row_at = lax.broadcasted_iota(jnp.int32, (LY, W), 0)
    for xp in range(XP):
        parts = []
        for x in (2 * xp, 2 * xp + 1):
            ref, at = find(x)
            ref = pieces[ref]
            rows = []
            for z in range(ZH):
                here = slice(z * W, (z + 1) * W)
                more = jnp.where(row_at == 0, edge[0, x : x + 1, here], 0.0)
                more = jnp.where(row_at == LY - 1, edge[1, x : x + 1, here], more)
                rows.append(ref[at, :, here] + more)
            part = jnp.concatenate(rows, axis=0)
            field[x] = part.astype(BF16)
            parts.append(part)
        first, second = parts
        even = jnp.where(low, first, swap(second)).astype(BF16)
        odd = jnp.where(low, swap(first), second).astype(BF16)
        out = dot(z_fwd[...], jnp.concatenate([even, odd], axis=0))
        freq[:, xp] = out.astype(BF16).reshape(KZ, 2 * LY, W)


def y_forward_kernel(given, y_fwd, out, rows):
    for xp in range(XP):
        data = given[:, xp].reshape(2 * PY * LY, W)
        value = dot(y_fwd[...], data)
        for part in range(2):
            for t in range(W // 128):
                rows[t, pl.ds(part * XP + xp, Q, stride=2 * XP), :] = value[
                    part * Q : (part + 1) * Q, t * 128 : (t + 1) * 128
                ]
    gather(rows, out)


def gather(rows, out):
    count = 2 * XP * Q // PX
    for d in range(PX):
        block = [rows[t, pl.ds(d * count, count), :] for t in range(W // 128)]
        out[d] = jnp.concatenate(block, axis=1).astype(BF16).reshape(out.shape[1:])


def shrink(v):
    return v - jnp.clip(v, -shrink_level, shrink_level)


def lay_out(weight, width, copies, out):
    for b in range(C // CB):
        columns = []
        for part in range(2):
            block = weight[part, b].astype(F32)
            columns += [jnp.zeros((CB, b * CB), F32)] * (b > 0) + [block]
            columns += [jnp.zeros((CB, width - (b + 1) * CB), F32)] * (width > (b + 1) * CB)
            columns += columns[-2:] * (copies - 1)
        out[b * CB : (b + 1) * CB] = jnp.concatenate(columns, axis=1).astype(BF16)
    out[C:] = jnp.zeros((256 - C, out.shape[1]), BF16)


def spectrum_kernel(given, x_fwd, x_inv, inner_weight, outer_weight, out, rows, inner, outer):
    lay_out(inner_weight, 256, 1, inner)
    lay_out(outer_weight, C, 2, outer)
    count = Q // PX
    low = low_half(2 * PX * XP)
    data = [given[:, q].reshape(2 * PX * XP, W) for q in range(count)]
    both = dot(x_fwd[...], jnp.concatenate(data, axis=1))
    spec = []
    for q in range(count):
        part = both[:, q * W : (q + 1) * W]
        part = part[: 2 * Q] + swap(part[2 * Q :])
        spec.append(part[:, :256].astype(BF16))
    mixed = dot(jnp.concatenate(spec, axis=0), inner[...]).reshape(count, 2, Q, 512)
    hidden_r = jnp.tanh(mixed[:, 0, :, :256] - mixed[:, 1, :, 256:])
    hidden_i = jnp.tanh(mixed[:, 0, :, 256:] + mixed[:, 1, :, :256])
    hidden = jnp.stack([hidden_r, hidden_i], axis=1).astype(BF16).reshape(count * 2 * Q, 256)
    mixed = dot(hidden, outer[...]).reshape(count, 2, Q, 2 * W)
    filt_r = shrink(mixed[:, 0, :, :W] - mixed[:, 1, :, W:]).astype(BF16)
    filt_i = shrink(mixed[:, 0, :, W:] + mixed[:, 1, :, :W]).astype(BF16)
    filt = [jnp.concatenate([filt_r[q], filt_i[q]], axis=0) for q in range(count)]
    both = dot(x_inv[...], jnp.concatenate(filt, axis=1))
    for q in range(count):
        part = both[:, q * W : (q + 1) * W]
        back = jnp.where(low, part[: 2 * PX * XP], part[2 * PX * XP :])
        for part in range(2):
            for t in range(W // 128):
                rows[t, pl.ds(part * count + q, PX * XP, stride=2 * count), :] = back[
                    part * PX * XP : (part + 1) * PX * XP, t * 128 : (t + 1) * 128
                ]
    gather(rows, out)


def y_inverse_kernel(given, y_inv, out):
    for xp in range(XP):
        data = given[:, xp].reshape(2 * Q, W)
        out[:, xp] = dot(y_inv[...], data).astype(BF16).reshape(PY, 2 * LY, W)


def z_inverse_kernel(given, z_inv, field, out):
    low = low_half(ZH * LY)
    for xp in range(given.shape[1]):
        data = given[:, xp].reshape(2 * KZ * LY, W)
        value = dot(z_inv[...], data)
        even, odd = value[: ZH * LY], value[ZH * LY :]
        first = jnp.where(low, even, swap(odd)) + field[2 * xp].astype(F32)
        second = jnp.where(low, swap(even), odd) + field[2 * xp + 1].astype(F32)
        for x, value in ((2 * xp, first), (2 * xp + 1, second)):
            for z in range(ZH):
                out[x, :, z * W : (z + 1) * W] = value[z * LY : (z + 1) * LY].astype(BF16)


def call(kernel, outs, scratch=(), name=None, in_specs=None):
    return pl.pallas_call(
        kernel,
        out_shape=outs,
        scratch_shapes=list(scratch),
        **({} if in_specs is None else {"in_specs": in_specs}),
        compiler_params=pltpu.CompilerParams(vmem_limit_bytes=20 * 2**20),
        name=name,
    )


def shape(*dims):
    return jax.ShapeDtypeStruct(dims, BF16)


def swap_pairs(value, axis, count, start):
    low = range(start, count - 1, 2)
    return lax.ppermute(value, axis, [(i, i + 1) for i in low] + [(i + 1, i) for i in low])


def body(tokens, conv_weight, inner_weight, outer_weight):
    z_fwd, z_inv, y_fwd, y_inv, x_fwd, x_inv, pick = (jnp.asarray(m) for m in matrices())
    wide = MERGED + 2 * C
    first, second, weight = call(
        start_kernel,
        [shape(1, LY, MERGED)] * 2 + [jax.ShapeDtypeStruct((27, W), F32)],
        [VMEM((27, C), F32), pltpu.SemaphoreType.DMA],
        name="x_rows",
        in_specs=[pl.BlockSpec(memory_space=VMEM), pl.BlockSpec(memory_space=pl.ANY)],
    )(tokens, conv_weight)
    first = swap_pairs(first, "px", PX, 0)
    second = swap_pairs(second, "px", PX, 1)
    inside = piece(0, inside_kernel, [], tokens, weight)
    inside, first, second = lax.optimization_barrier((inside, first, second))
    y_first, y_second = call(rows_kernel, [shape(LX + 2, MERGED)] * 2, name="y_rows")(
        tokens, first, second, pick
    )
    y_first = swap_pairs(y_first, "py", PY, 0)
    y_second = swap_pairs(y_second, "py", PY, 1)
    border = piece(1, border_kernel, [VMEM((2, LY, MERGED), F32)], tokens, first, second, weight)
    field, freq = call(
        edge_kernel,
        [shape(LX, ZH * LY, W), shape(KZ, XP, 2 * LY, W)],
        [VMEM((LX + 2, MERGED), F32)] * 2 + [VMEM((LX + 2, wide), F32)] * 2 + [VMEM((2, LX, MERGED), F32)],
        name="edge_z",
    )(inside, border, y_first, y_second, weight, z_fwd)
    rows = VMEM((W // 128, 2 * XP * Q, 128), F32)
    freq = lax.all_to_all(freq, "py", 0, 0, tiled=True)
    freq = call(y_forward_kernel, shape(PX, Q // PX, 2 * XP, W), [rows], name="y_fwd")(freq, y_fwd)
    freq = lax.all_to_all(freq, "px", 0, 0, tiled=True)
    mixing = [VMEM((256, 512), BF16), VMEM((256, 4 * C), BF16)]
    freq = call(spectrum_kernel, shape(PX, XP, 2 * Q // PX, W), [rows] + mixing, name="spec")(
        freq, x_fwd, x_inv, inner_weight, outer_weight
    )
    freq = lax.all_to_all(freq, "px", 0, 0, tiled=True)
    freq = call(y_inverse_kernel, shape(PY, XP, 2 * LY, W), name="y_inv")(freq, y_inv)
    freq = lax.all_to_all(freq, "py", 0, 0, tiled=True)
    steps = 4
    return pl.pallas_call(
        z_inverse_kernel,
        out_shape=shape(LX, LY, MERGED),
        grid=(steps,),
        in_specs=[
            pl.BlockSpec((KZ, XP // steps, 2 * LY, W), lambda i: (0, i, 0, 0)),
            pl.BlockSpec(z_inv.shape, lambda i: (0, 0)),
            pl.BlockSpec((LX // steps, ZH * LY, W), lambda i: (i, 0, 0)),
        ],
        out_specs=pl.BlockSpec((LX // steps, LY, MERGED), lambda i: (i, 0, 0)),
        compiler_params=pltpu.CompilerParams(vmem_limit_bytes=20 * 2**20),
        name="z_inv",
    )(freq, z_inv, field)


def solution(mesh):
    in_specs = (P("px", "py", None), P(), P(), P())
    out_specs = P("px", "py", None)
    return jax.shard_map(body, mesh=mesh, in_specs=in_specs, out_specs=out_specs, check_vma=False)
```

```python
import functools
import math

import jax
import jax.numpy as jnp
import ml_dtypes
import numpy as np
from jax import lax
from jax.experimental import pallas as pl
from jax.experimental.pallas import tpu as pltpu
from jax.sharding import PartitionSpec as P

shrink_level = 0.2
F32 = jnp.float32
BF16 = jnp.bfloat16
VMEM = pltpu.VMEM

PX, PY = 8, 16
LX, LY = 16, 8
Z, KZ, C, CB = 32, 16, 192, 96
W = 2 * C
MERGED = Z * C
XP = LX // 2
XE = XP + 1
ZH = Z // 2
Q = 64


def tables(length, modes, weights):
    product = np.asarray(modes)[:, None] * np.arange(length)[None, :] % length
    angle = product.astype(np.float32) * np.float32(2.0 * math.pi / length)
    factor = np.asarray(weights, np.float32)[:, None] / np.float32(math.sqrt(length))
    rounded = [(f(angle) * factor).astype(ml_dtypes.bfloat16) for f in (np.cos, np.sin)]
    return [t.astype(np.float64) for t in rounded]


def kept(length):
    return np.concatenate([np.arange(length // 4), np.arange(length - length // 4, length)])


def forward(cos, sin):
    return np.stack([np.stack([cos, sin], 1), np.stack([-sin, cos], 1)])


def backward(cos, sin):
    cos, sin = cos.T, sin.T
    return np.stack([np.stack([cos, -sin], 1), np.stack([sin, cos], 1)])


def as_bf16(matrix):
    return np.ascontiguousarray(matrix).astype(ml_dtypes.bfloat16)


@functools.cache
def matrices():
    eye = np.eye(LY)
    one = np.ones(KZ)
    cz, sz = tables(Z, np.arange(KZ), one)
    both = np.stack([cz, -sz], 1).reshape(KZ, 2, ZH, 2)
    z_fwd = np.einsum("kpzs,yw->kpyszw", both, eye).reshape(KZ * 2 * LY, 2 * ZH * LY)
    two = np.where(np.arange(KZ) == 0, 1.0, 2.0)
    cz, sz = tables(Z, np.arange(KZ), two)
    both = np.stack([cz, -sz], 1).reshape(KZ, 2, ZH, 2)
    z_inv = np.einsum("kpzs,yw->szykpw", both, eye).reshape(2 * ZH * LY, KZ * 2 * LY)
    n = PY * LY
    cy, sy = tables(n, kept(n), np.ones(Q))
    y_fwd = forward(cy, sy).reshape(2, PX, Q // PX, 2, PY, LY).transpose(1, 0, 2, 4, 3, 5)
    y_fwd = y_fwd.reshape(2 * Q, 2 * n)
    y_inv = backward(cy, sy).reshape(2, PY, LY, 2, PX, Q // PX)
    y_inv = y_inv.transpose(1, 0, 2, 4, 3, 5).reshape(2 * n, 2 * Q)
    n = PX * LX
    cx, sx = tables(n, kept(n), np.ones(Q))
    x_fwd = forward(cx, sx)
    extra = np.zeros((2, Q, 2, PX, 1, 2))
    extra[..., 1:, 0, 0] = x_fwd[..., LX - 1 : n - LX : LX]
    extra[..., :-1, 0, 1] = x_fwd[..., LX::LX]
    x_fwd = np.concatenate([x_fwd.reshape(2, Q, 2, PX, XP, 2), extra], axis=4)
    x_fwd = x_fwd.transpose(5, 0, 1, 3, 4, 2).reshape(4 * Q, 2 * PX * XE)
    x_inv = backward(cx, sx).reshape(2, PX, XP, 2, 2, Q)
    x_inv = x_inv.transpose(3, 0, 1, 2, 4, 5).reshape(4 * PX * XP, 2 * Q)
    pick = np.zeros((2, LX, LX, LY))
    for x in range(LX):
        pick[0, x, x, 0] = pick[1, x, x, LY - 1] = 1
    pick = pick.reshape(2 * LX, LX * LY)
    return [as_bf16(m) for m in (z_fwd, z_inv, y_fwd, y_inv, x_fwd, x_inv, pick)]


def dot(a, b):
    return jnp.dot(a, b, preferred_element_type=F32)


def low_half(rows):
    return lax.broadcasted_iota(jnp.int32, (rows, W), 1) < C


def swap(value):
    return pltpu.roll(value, C, 1)


def odd(axis):
    return lax.rem(lax.axis_index(axis), 2) == 1


def by_order(axis, first, second):
    second, first = second.astype(F32), first.astype(F32)
    up = odd(axis)
    return jnp.where(up, first, second), jnp.where(up, second, first)


def rows_kernel(tok, pick, send_first, send_second):
    step = MERGED // 4
    up = odd("py")
    for j in range(4):
        here = slice(j * step, (j + 1) * step)
        data = tok[:, :, here].astype(F32).reshape(LX * LY, step).astype(BF16)
        out = dot(pick[...], data)
        send_first[:, here] = jnp.where(up, out[:LX], out[LX:]).astype(BF16)
        send_second[:, here] = jnp.where(up, out[LX:], out[:LX]).astype(BF16)


def conv_kernel(tok, narrow, out, shifted, weight):
    weight[...] = jnp.concatenate([narrow[...], narrow[...]], axis=1)
    pad = jnp.zeros((LY, C), F32)
    for x in range(LX):
        shifted[x] = jnp.concatenate([pad, tok[x].astype(F32), pad], axis=1)
    row_at = lax.broadcasted_iota(jnp.int32, (LY, 128), 0)

    @pl.loop(0, MERGED // 128)
    def _(j):
        at = pl.multiple_of(j * 128, 128)
        after = pl.multiple_of(j * 128 + W, 128)
        here = pl.ds(at, 128)
        phase = pl.multiple_of(lax.rem(j, 3) * 128, 128)
        wide = [jnp.broadcast_to(weight[t : t + 1, pl.ds(phase, 128)], (LY, 128)) for t in range(27)]
        sums = {}
        for x in range(LX + 2):
            if x < LX:
                mid = tok[x, :, here].astype(F32)
                before = shifted[x, :, here]
                behind = shifted[x, :, pl.ds(after, 128)]
                for a in range(3):
                    to = x + 2 - a
                    for b in range(3):
                        t = a * 9 + b * 3
                        term = before * wide[t] + mid * wide[t + 1] + behind * wide[t + 2]
                        sums[to, b] = sums[to, b] + term if (to, b) in sums else term
            down = pltpu.roll(sums.pop((x, 0)), 1, 0)
            up = pltpu.roll(sums.pop((x, 2)), LY - 1, 0)
            down = jnp.where(row_at == 0, 0.0, down)
            up = jnp.where(row_at == LY - 1, 0.0, up)
            out[x, :, here] = sums.pop((x, 1)) + down + up


def edge_kernel(
    conv, first, second, narrow, z_fwd, field, freq, to_below, to_above, ylo, yhi, ylo_s, yhi_s, edge, weight
):
    weight[...] = jnp.concatenate([narrow[...], narrow[...]], axis=1)
    for rows, rows_s, value in zip((ylo, yhi), (ylo_s, yhi_s), by_order("py", first[...], second[...])):
        none = jnp.zeros((2, MERGED), F32)
        value = jnp.concatenate([none, value, none], axis=0)
        rows[...] = value
        pad = jnp.zeros((LX + 4, C), F32)
        rows_s[...] = jnp.concatenate([pad, value, pad], axis=1)

    @pl.loop(0, MERGED // 128)
    def _(j):
        at = pl.multiple_of(j * 128, 128)
        after = pl.multiple_of(j * 128 + W, 128)
        here = pl.ds(at, 128)
        phase = pl.multiple_of(lax.rem(j, 3) * 128, 128)
        for side, rows, rows_s, b in ((0, ylo, ylo_s, 0), (1, yhi, yhi_s, 2)):
            mid = rows[:, here]
            before = rows_s[:, here]
            behind = rows_s[:, pl.ds(after, 128)]
            total = None
            for a in range(3):
                t = a * 9 + b * 3
                taps = [weight[t + e : t + e + 1, pl.ds(phase, 128)] for e in range(3)]
                term = before * taps[0] + mid * taps[1] + behind * taps[2]
                term = term[a : a + LX + 2]
                total = term if total is None else total + term
            edge[side, :, here] = total

    low = low_half(ZH * LY)
    row_at = lax.broadcasted_iota(jnp.int32, (LY, W), 0)
    for xp in range(XE):
        parts = []
        for x in (2 * xp, 2 * xp + 1) if xp < XP else (-1, LX):
            at = x + 1
            rows = []
            for z in range(ZH):
                here = slice(z * W, (z + 1) * W)
                more = jnp.where(row_at == 0, edge[0, at : at + 1, here], 0.0)
                more = jnp.where(row_at == LY - 1, edge[1, at : at + 1, here], more)
                rows.append(conv[at, :, here] + more)
            part = jnp.concatenate(rows, axis=0)
            if xp < XP:
                field[x] = part.astype(BF16)
            parts.append(part)
        first, second = parts
        if xp == XP:
            to_below[...] = first.astype(BF16)
            to_above[...] = second.astype(BF16)
        even = jnp.where(low, first, swap(second)).astype(BF16)
        odd_z = jnp.where(low, swap(first), second).astype(BF16)
        out = dot(z_fwd[...], jnp.concatenate([even, odd_z], axis=0))
        freq[:, xp] = out.astype(BF16).reshape(KZ, 2 * LY, W)


def y_forward_kernel(given, y_fwd, out):
    for xp in range(XE):
        data = given[:, xp].reshape(2 * PY * LY, W)
        out[:, xp] = dot(y_fwd[...], data).astype(BF16).reshape(PX, 2 * Q // PX, W)


def gather(rows, out):
    count = 2 * XP * Q // PX
    for d in range(PX):
        block = [rows[t, pl.ds(d * count, count), :] for t in range(W // 128)]
        out[d] = jnp.concatenate(block, axis=1).astype(BF16).reshape(out.shape[1:])


def shrink(v):
    return v - jnp.clip(v, -shrink_level, shrink_level)


def lay_out(weight, width, copies, out):
    for b in range(C // CB):
        columns = []
        for part in range(2):
            block = weight[part, b].astype(F32)
            columns += [jnp.zeros((CB, b * CB), F32)] * (b > 0) + [block]
            columns += [jnp.zeros((CB, width - (b + 1) * CB), F32)] * (width > (b + 1) * CB)
            columns += columns[-2:] * (copies - 1)
        out[b * CB : (b + 1) * CB] = jnp.concatenate(columns, axis=1).astype(BF16)
    out[C:] = jnp.zeros((256 - C, out.shape[1]), BF16)


def spectrum_kernel(given, x_fwd, x_inv, inner_weight, outer_weight, out, rows, arrived, inner, outer):
    lay_out(inner_weight, 256, 1, inner)
    lay_out(outer_weight, C, 2, outer)
    count = Q // PX
    low = low_half(2 * PX * XP)
    wide = given[...].astype(F32).reshape(2 * count * PX * XE, W)
    for t in range(W // 128):
        arrived[t] = wide[:, t * 128 : (t + 1) * 128]
    data = []
    for q in range(count):
        some = [arrived[t, pl.ds(q, 2 * PX * XE, stride=count), :] for t in range(W // 128)]
        data.append(jnp.concatenate(some, axis=1).astype(BF16))
    both = dot(x_fwd[...], jnp.concatenate(data, axis=1))
    spec = []
    for q in range(count):
        part = both[:, q * W : (q + 1) * W]
        part = part[: 2 * Q] + swap(part[2 * Q :])
        spec.append(part[:, :256].astype(BF16))
    mixed = dot(jnp.concatenate(spec, axis=0), inner[...]).reshape(count, 2, Q, 512)
    hidden_r = jnp.tanh(mixed[:, 0, :, :256] - mixed[:, 1, :, 256:])
    hidden_i = jnp.tanh(mixed[:, 0, :, 256:] + mixed[:, 1, :, :256])
    hidden = jnp.stack([hidden_r, hidden_i], axis=1).astype(BF16).reshape(count * 2 * Q, 256)
    mixed = dot(hidden, outer[...]).reshape(count, 2, Q, 2 * W)
    filt_r = shrink(mixed[:, 0, :, :W] - mixed[:, 1, :, W:]).astype(BF16)
    filt_i = shrink(mixed[:, 0, :, W:] + mixed[:, 1, :, :W]).astype(BF16)
    filt = [jnp.concatenate([filt_r[q], filt_i[q]], axis=0) for q in range(count)]
    both = dot(x_inv[...], jnp.concatenate(filt, axis=1))
    for q in range(count):
        part = both[:, q * W : (q + 1) * W]
        back = jnp.where(low, part[: 2 * PX * XP], part[2 * PX * XP :])
        for part in range(2):
            for t in range(W // 128):
                rows[t, pl.ds(part * count + q, PX * XP, stride=2 * count), :] = back[
                    part * PX * XP : (part + 1) * PX * XP, t * 128 : (t + 1) * 128
                ]
    gather(rows, out)


def y_inverse_kernel(given, y_inv, out):
    for xp in range(XP):
        data = given[:, xp].reshape(2 * Q, W)
        out[:, xp] = dot(y_inv[...], data).astype(BF16).reshape(PY, 2 * LY, W)


def z_inverse_kernel(given, z_inv, field, below, above, out):
    low = low_half(ZH * LY)
    step, pairs = pl.program_id(0), given.shape[1]
    below = jnp.where(step == 0, below[...].astype(F32), 0.0)
    above = jnp.where(step == XP // pairs - 1, above[...].astype(F32), 0.0)
    for xp in range(pairs):
        data = given[:, xp].reshape(2 * KZ * LY, W)
        value = dot(z_inv[...], data)
        even, odd = value[: ZH * LY], value[ZH * LY :]
        first = jnp.where(low, even, swap(odd)) + field[2 * xp].astype(F32)
        second = jnp.where(low, swap(even), odd) + field[2 * xp + 1].astype(F32)
        if xp == 0:
            first = first + below
        if xp == pairs - 1:
            second = second + above
        for x, value in ((2 * xp, first), (2 * xp + 1, second)):
            for z in range(ZH):
                out[x, :, z * W : (z + 1) * W] = value[z * LY : (z + 1) * LY].astype(BF16)


def call(kernel, outs, scratch=(), name=None, in_specs=None):
    return pl.pallas_call(
        kernel,
        out_shape=outs,
        scratch_shapes=list(scratch),
        **({} if in_specs is None else {"in_specs": in_specs}),
        compiler_params=pltpu.CompilerParams(vmem_limit_bytes=20 * 2**20),
        name=name,
    )


def shape(*dims):
    return jax.ShapeDtypeStruct(dims, BF16)


def swap_pairs(value, axis, count, start):
    low = range(start, count - 1, 2)
    return lax.ppermute(value, axis, [(i, i + 1) for i in low] + [(i + 1, i) for i in low])


def body(tokens, conv_weight, inner_weight, outer_weight):
    z_fwd, z_inv, y_fwd, y_inv, x_fwd, x_inv, pick = (jnp.asarray(m) for m in matrices())
    wide = MERGED + 2 * C
    first, second = call(rows_kernel, [shape(LX, MERGED)] * 2, name="y_rows")(tokens, pick)
    second = swap_pairs(second, "py", PY, 1)
    first = swap_pairs(first, "py", PY, 0)
    conv = call(
        conv_kernel,
        jax.ShapeDtypeStruct((LX + 2, LY, MERGED), F32),
        [VMEM((LX, LY, wide), F32), VMEM((27, W), F32)],
        name="conv",
    )(tokens, conv_weight)
    rows = [VMEM((LX + 4, MERGED), F32)] * 2 + [VMEM((LX + 4, wide), F32)] * 2
    field, freq, to_below, to_above = call(
        edge_kernel,
        [shape(LX, ZH * LY, W), shape(KZ, XE, 2 * LY, W)] + [shape(ZH * LY, W)] * 2,
        rows + [VMEM((2, LX + 2, MERGED), F32), VMEM((27, W), F32)],
        name="edge_z",
    )(conv, first, second, conv_weight, z_fwd)
    rows = VMEM((W // 128, 2 * XP * Q, 128), F32)
    up = odd("px")
    first = swap_pairs(jnp.where(up, to_below, to_above), "px", PX, 0)
    second = swap_pairs(jnp.where(up, to_above, to_below), "px", PX, 1)
    below, above = jnp.where(up, first, second), jnp.where(up, second, first)
    freq = lax.all_to_all(freq, "py", 0, 0, tiled=True)
    freq, below, above = lax.optimization_barrier((freq, below, above))
    freq = call(y_forward_kernel, shape(PX, XE, 2 * Q // PX, W), name="y_fwd")(freq, y_fwd)
    freq = lax.all_to_all(freq, "px", 0, 0, tiled=True)
    mixing = [VMEM((256, 512), BF16), VMEM((256, 4 * C), BF16)]
    freq = call(spectrum_kernel, shape(PX, XP, 2 * Q // PX, W), [rows, VMEM((W // 128, 2 * XE * Q, 128), F32)] + mixing, name="spec")(
        freq, x_fwd, x_inv, inner_weight, outer_weight
    )
    freq = lax.all_to_all(freq, "px", 0, 0, tiled=True)
    freq = call(y_inverse_kernel, shape(PY, XP, 2 * LY, W), name="y_inv")(freq, y_inv)
    freq = lax.all_to_all(freq, "py", 0, 0, tiled=True)
    steps = 4
    return pl.pallas_call(
        z_inverse_kernel,
        out_shape=shape(LX, LY, MERGED),
        grid=(steps,),
        in_specs=[
            pl.BlockSpec((KZ, XP // steps, 2 * LY, W), lambda i: (0, i, 0, 0)),
            pl.BlockSpec(z_inv.shape, lambda i: (0, 0)),
            pl.BlockSpec((LX // steps, ZH * LY, W), lambda i: (i, 0, 0)),
            pl.BlockSpec((ZH * LY, W), lambda i: (0, 0)),
            pl.BlockSpec((ZH * LY, W), lambda i: (0, 0)),
        ],
        out_specs=pl.BlockSpec((LX // steps, LY, MERGED), lambda i: (i, 0, 0)),
        compiler_params=pltpu.CompilerParams(vmem_limit_bytes=20 * 2**20),
        name="z_inv",
    )(freq, z_inv, field, below, above)


def solution(mesh):
    in_specs = (P("px", "py", None), P(), P(), P())
    out_specs = P("px", "py", None)
    return jax.shard_map(body, mesh=mesh, in_specs=in_specs, out_specs=out_specs, check_vma=False)
```

```python
import functools
import math

import jax
import jax.numpy as jnp
import ml_dtypes
import numpy as np
from jax import lax
from jax.experimental import pallas as pl
from jax.experimental.pallas import tpu as pltpu
from jax.sharding import PartitionSpec as P

shrink_level = 0.2
F32 = jnp.float32
BF16 = jnp.bfloat16
VMEM = pltpu.VMEM

PX, PY = 8, 16
LX, LY = 16, 8
Z, KZ, C, CB = 32, 16, 192, 96
W = 2 * C
MERGED = Z * C
XP = LX // 2
XE = XP + 1
ZH = Z // 2
Q = 64


def tables(length, modes, weights):
    product = np.asarray(modes)[:, None] * np.arange(length)[None, :] % length
    angle = product.astype(np.float32) * np.float32(2.0 * math.pi / length)
    factor = np.asarray(weights, np.float32)[:, None] / np.float32(math.sqrt(length))
    rounded = [(f(angle) * factor).astype(ml_dtypes.bfloat16) for f in (np.cos, np.sin)]
    return [t.astype(np.float64) for t in rounded]


def kept(length):
    return np.concatenate([np.arange(length // 4), np.arange(length - length // 4, length)])


def forward(cos, sin):
    return np.stack([np.stack([cos, sin], 1), np.stack([-sin, cos], 1)])


def backward(cos, sin):
    cos, sin = cos.T, sin.T
    return np.stack([np.stack([cos, -sin], 1), np.stack([sin, cos], 1)])


def as_bf16(matrix):
    return np.ascontiguousarray(matrix).astype(ml_dtypes.bfloat16)


@functools.cache
def matrices():
    eye = np.eye(LY)
    one = np.ones(KZ)
    cz, sz = tables(Z, np.arange(KZ), one)
    both = np.stack([cz, -sz], 1).reshape(KZ, 2, ZH, 2)
    z_fwd = np.einsum("kpzs,yw->kpyszw", both, eye).reshape(KZ * 2 * LY, 2 * ZH * LY)
    two = np.where(np.arange(KZ) == 0, 1.0, 2.0)
    cz, sz = tables(Z, np.arange(KZ), two)
    both = np.stack([cz, -sz], 1).reshape(KZ, 2, ZH, 2)
    z_inv = np.einsum("kpzs,yw->szykpw", both, eye).reshape(2 * ZH * LY, KZ * 2 * LY)
    n = PY * LY
    cy, sy = tables(n, kept(n), np.ones(Q))
    y_fwd = forward(cy, sy).reshape(2, PX, Q // PX, 2, PY, LY).transpose(1, 0, 2, 4, 3, 5)
    y_fwd = y_fwd.reshape(2 * Q, 2 * n)
    y_inv = backward(cy, sy).reshape(2, PY, LY, 2, PX, Q // PX)
    y_inv = y_inv.transpose(1, 0, 2, 4, 3, 5).reshape(2 * n, 2 * Q)
    n = PX * LX
    cx, sx = tables(n, kept(n), np.ones(Q))
    x_fwd = forward(cx, sx)
    extra = np.zeros((2, Q, 2, PX, 1, 2))
    extra[..., 1:, 0, 0] = x_fwd[..., LX - 1 : n - LX : LX]
    extra[..., :-1, 0, 1] = x_fwd[..., LX::LX]
    x_fwd = np.concatenate([x_fwd.reshape(2, Q, 2, PX, XP, 2), extra], axis=4)
    x_fwd = x_fwd.transpose(5, 0, 1, 3, 4, 2).reshape(4 * Q, 2 * PX * XE)
    x_inv = backward(cx, sx).reshape(2, PX, XP, 2, 2, Q)
    x_inv = x_inv.transpose(3, 0, 1, 2, 4, 5).reshape(4 * PX * XP, 2 * Q)
    return [as_bf16(m) for m in (z_fwd, z_inv, y_fwd, y_inv, x_fwd, x_inv)]


def dot(a, b):
    return jnp.dot(a, b, preferred_element_type=F32)


def low_half(rows):
    return lax.broadcasted_iota(jnp.int32, (rows, W), 1) < C


def swap(value):
    return pltpu.roll(value, C, 1)


def odd(axis):
    return lax.rem(lax.axis_index(axis), 2) == 1


def by_order(axis, first, second):
    second, first = second.astype(F32), first.astype(F32)
    up = odd(axis)
    return jnp.where(up, first, second), jnp.where(up, second, first)


def rows_kernel(tok, send_first, send_second):
    step = MERGED // 4
    row = lax.broadcasted_iota(jnp.int32, (2 * LX, LX * LY), 0)
    cell = lax.broadcasted_iota(jnp.int32, (2 * LX, LX * LY), 1)
    wanted = jnp.where(row < LX, row * LY, (row - LX) * LY + LY - 1)
    pick = jnp.where(cell == wanted, 1.0, 0.0).astype(BF16)
    up = odd("py")
    for j in range(4):
        here = slice(j * step, (j + 1) * step)
        data = tok[:, :, here].astype(F32).reshape(LX * LY, step).astype(BF16)
        out = dot(pick, data)
        send_first[:, here] = jnp.where(up, out[:LX], out[LX:]).astype(BF16)
        send_second[:, here] = jnp.where(up, out[LX:], out[:LX]).astype(BF16)


def conv_kernel(tok, narrow, out, shifted, weight):
    weight[...] = jnp.concatenate([narrow[...], narrow[...]], axis=1)
    pad = jnp.zeros((LY, C), F32)
    for x in range(LX):
        shifted[x] = jnp.concatenate([pad, tok[x].astype(F32), pad], axis=1)
    row_at = lax.broadcasted_iota(jnp.int32, (LY, 128), 0)

    @pl.loop(0, MERGED // 128)
    def _(j):
        at = pl.multiple_of(j * 128, 128)
        after = pl.multiple_of(j * 128 + W, 128)
        here = pl.ds(at, 128)
        phase = pl.multiple_of(lax.rem(j, 3) * 128, 128)
        wide = [jnp.broadcast_to(weight[t : t + 1, pl.ds(phase, 128)], (LY, 128)) for t in range(27)]
        sums = {}
        for x in range(LX + 2):
            if x < LX:
                mid = tok[x, :, here].astype(F32)
                before = shifted[x, :, here]
                behind = shifted[x, :, pl.ds(after, 128)]
                for a in range(3):
                    to = x + 2 - a
                    for b in range(3):
                        t = a * 9 + b * 3
                        term = before * wide[t] + mid * wide[t + 1] + behind * wide[t + 2]
                        sums[to, b] = sums[to, b] + term if (to, b) in sums else term
            down = pltpu.roll(sums.pop((x, 0)), 1, 0)
            up = pltpu.roll(sums.pop((x, 2)), LY - 1, 0)
            down = jnp.where(row_at == 0, 0.0, down)
            up = jnp.where(row_at == LY - 1, 0.0, up)
            out[x, :, here] = sums.pop((x, 1)) + down + up


def edge_kernel(
    conv, first, second, narrow, z_fwd, field, freq, to_below, to_above, ylo, yhi, ylo_s, yhi_s, edge, weight
):
    weight[...] = jnp.concatenate([narrow[...], narrow[...]], axis=1)
    for rows, rows_s, value in zip((ylo, yhi), (ylo_s, yhi_s), by_order("py", first[...], second[...])):
        none = jnp.zeros((2, MERGED), F32)
        value = jnp.concatenate([none, value, none], axis=0)
        rows[...] = value
        pad = jnp.zeros((LX + 4, C), F32)
        rows_s[...] = jnp.concatenate([pad, value, pad], axis=1)

    @pl.loop(0, MERGED // 128)
    def _(j):
        at = pl.multiple_of(j * 128, 128)
        after = pl.multiple_of(j * 128 + W, 128)
        here = pl.ds(at, 128)
        phase = pl.multiple_of(lax.rem(j, 3) * 128, 128)
        for side, rows, rows_s, b in ((0, ylo, ylo_s, 0), (1, yhi, yhi_s, 2)):
            mid = rows[:, here]
            before = rows_s[:, here]
            behind = rows_s[:, pl.ds(after, 128)]
            total = None
            for a in range(3):
                t = a * 9 + b * 3
                taps = [weight[t + e : t + e + 1, pl.ds(phase, 128)] for e in range(3)]
                term = before * taps[0] + mid * taps[1] + behind * taps[2]
                term = term[a : a + LX + 2]
                total = term if total is None else total + term
            edge[side, :, here] = total

    low = low_half(ZH * LY)
    row_at = lax.broadcasted_iota(jnp.int32, (LY, W), 0)
    for xp in range(XE):
        parts = []
        for x in (2 * xp, 2 * xp + 1) if xp < XP else (-1, LX):
            at = x + 1
            rows = []
            for z in range(ZH):
                here = slice(z * W, (z + 1) * W)
                more = jnp.where(row_at == 0, edge[0, at : at + 1, here], 0.0)
                more = jnp.where(row_at == LY - 1, edge[1, at : at + 1, here], more)
                rows.append(conv[at, :, here] + more)
            part = jnp.concatenate(rows, axis=0)
            if xp < XP:
                field[x] = part.astype(BF16)
            parts.append(part)
        first, second = parts
        if xp == XP:
            to_below[...] = first.astype(BF16)
            to_above[...] = second.astype(BF16)
        even = jnp.where(low, first, swap(second)).astype(BF16)
        odd_z = jnp.where(low, swap(first), second).astype(BF16)
        out = dot(z_fwd[...], jnp.concatenate([even, odd_z], axis=0))
        freq[:, xp] = out.astype(BF16).reshape(KZ, 2 * LY, W)


def y_forward_kernel(given, y_fwd, out):
    for xp in range(XE):
        data = given[:, xp].reshape(2 * PY * LY, W)
        out[:, xp] = dot(y_fwd[...], data).astype(BF16).reshape(PX, 2 * Q // PX, W)


def gather(rows, out):
    count = 2 * XP * Q // PX
    for d in range(PX):
        block = [rows[t, pl.ds(d * count, count), :] for t in range(W // 128)]
        out[d] = jnp.concatenate(block, axis=1).astype(BF16).reshape(out.shape[1:])


def shrink(v):
    return v - jnp.clip(v, -shrink_level, shrink_level)


def lay_out(weight, width, copies, out):
    for b in range(C // CB):
        columns = []
        for part in range(2):
            block = weight[part, b].astype(F32)
            columns += [jnp.zeros((CB, b * CB), F32)] * (b > 0) + [block]
            columns += [jnp.zeros((CB, width - (b + 1) * CB), F32)] * (width > (b + 1) * CB)
            columns += columns[-2:] * (copies - 1)
        out[b * CB : (b + 1) * CB] = jnp.concatenate(columns, axis=1).astype(BF16)
    out[C:] = jnp.zeros((256 - C, out.shape[1]), BF16)


def spectrum_kernel(given, x_fwd, x_inv, inner_weight, outer_weight, out, rows, arrived, inner, outer):
    lay_out(inner_weight, 256, 1, inner)
    lay_out(outer_weight, C, 2, outer)
    count = Q // PX
    low = low_half(2 * PX * XP)
    wide = given[...].astype(F32).reshape(2 * count * PX * XE, W)
    for t in range(W // 128):
        arrived[t] = wide[:, t * 128 : (t + 1) * 128]
    data = []
    for q in range(count):
        some = [arrived[t, pl.ds(q, 2 * PX * XE, stride=count), :] for t in range(W // 128)]
        data.append(jnp.concatenate(some, axis=1).astype(BF16))
    both = dot(x_fwd[...], jnp.concatenate(data, axis=1))
    spec = []
    for q in range(count):
        part = both[:, q * W : (q + 1) * W]
        part = part[: 2 * Q] + swap(part[2 * Q :])
        spec.append(part[:, :256].astype(BF16))
    mixed = dot(jnp.concatenate(spec, axis=0), inner[...]).reshape(count, 2, Q, 512)
    hidden_r = jnp.tanh(mixed[:, 0, :, :256] - mixed[:, 1, :, 256:])
    hidden_i = jnp.tanh(mixed[:, 0, :, 256:] + mixed[:, 1, :, :256])
    hidden = jnp.stack([hidden_r, hidden_i], axis=1).astype(BF16).reshape(count * 2 * Q, 256)
    mixed = dot(hidden, outer[...]).reshape(count, 2, Q, 2 * W)
    filt_r = shrink(mixed[:, 0, :, :W] - mixed[:, 1, :, W:]).astype(BF16)
    filt_i = shrink(mixed[:, 0, :, W:] + mixed[:, 1, :, :W]).astype(BF16)
    filt = [jnp.concatenate([filt_r[q], filt_i[q]], axis=0) for q in range(count)]
    both = dot(x_inv[...], jnp.concatenate(filt, axis=1))
    for q in range(count):
        part = both[:, q * W : (q + 1) * W]
        back = jnp.where(low, part[: 2 * PX * XP], part[2 * PX * XP :])
        for part in range(2):
            for t in range(W // 128):
                rows[t, pl.ds(part * count + q, PX * XP, stride=2 * count), :] = back[
                    part * PX * XP : (part + 1) * PX * XP, t * 128 : (t + 1) * 128
                ]
    gather(rows, out)


def y_inverse_kernel(given, y_inv, out):
    for xp in range(XP):
        data = given[:, xp].reshape(2 * Q, W)
        out[:, xp] = dot(y_inv[...], data).astype(BF16).reshape(PY, 2 * LY, W)


def z_inverse_kernel(given, z_inv, field, below, above, out):
    low = low_half(ZH * LY)
    for xp in range(XP):
        data = given[:, xp].reshape(2 * KZ * LY, W)
        value = dot(z_inv[...], data)
        even, odd = value[: ZH * LY], value[ZH * LY :]
        first = jnp.where(low, even, swap(odd)) + field[2 * xp].astype(F32)
        second = jnp.where(low, swap(even), odd) + field[2 * xp + 1].astype(F32)
        if xp == 0:
            first = first + below[...].astype(F32)
        if xp == XP - 1:
            second = second + above[...].astype(F32)
        for x, value in ((2 * xp, first), (2 * xp + 1, second)):
            for z in range(ZH):
                out[x, :, z * W : (z + 1) * W] = value[z * LY : (z + 1) * LY].astype(BF16)


def call(kernel, outs, scratch=(), name=None):
    return pl.pallas_call(
        kernel,
        out_shape=outs,
        scratch_shapes=list(scratch),
        compiler_params=pltpu.CompilerParams(vmem_limit_bytes=20 * 2**20),
        name=name,
    )


def shape(*dims):
    return jax.ShapeDtypeStruct(dims, BF16)


def swap_pairs(value, axis, count, start):
    low = range(start, count - 1, 2)
    return lax.ppermute(value, axis, [(i, i + 1) for i in low] + [(i + 1, i) for i in low])


def body(tokens, conv_weight, inner_weight, outer_weight):
    z_fwd, z_inv, y_fwd, y_inv, x_fwd, x_inv = (jnp.asarray(m) for m in matrices())
    wide = MERGED + 2 * C
    first, second = call(rows_kernel, [shape(LX, MERGED)] * 2, name="y_rows")(tokens)
    second = swap_pairs(second, "py", PY, 1)
    first = swap_pairs(first, "py", PY, 0)
    conv = call(
        conv_kernel,
        jax.ShapeDtypeStruct((LX + 2, LY, MERGED), F32),
        [
            VMEM((LX, LY, wide), F32),
            VMEM((27, W), F32),
        ],
        name="conv",
    )(tokens, conv_weight)
    rows = [VMEM((LX + 4, MERGED), F32)] * 2 + [VMEM((LX + 4, wide), F32)] * 2
    field, freq, to_below, to_above = call(
        edge_kernel,
        [shape(LX, ZH * LY, W), shape(KZ, XE, 2 * LY, W)] + [shape(ZH * LY, W)] * 2,
        rows + [VMEM((2, LX + 2, MERGED), F32), VMEM((27, W), F32)],
        name="edge_z",
    )(conv, first, second, conv_weight, z_fwd)
    rows = VMEM((W // 128, 2 * XP * Q, 128), F32)
    freq = lax.all_to_all(freq, "py", 0, 0, tiled=True)
    freq = call(y_forward_kernel, shape(PX, XE, 2 * Q // PX, W), name="y_fwd")(freq, y_fwd)
    freq = lax.all_to_all(freq, "px", 0, 0, tiled=True)
    mixing = [VMEM((256, 512), BF16), VMEM((256, 4 * C), BF16)]
    freq = call(spectrum_kernel, shape(PX, XP, 2 * Q // PX, W), [rows, VMEM((W // 128, 2 * XE * Q, 128), F32)] + mixing, name="spec")(
        freq, x_fwd, x_inv, inner_weight, outer_weight
    )
    freq, to_below, to_above = lax.optimization_barrier((freq, to_below, to_above))
    up = odd("px")
    first = swap_pairs(jnp.where(up, to_below, to_above), "px", PX, 0)
    second = swap_pairs(jnp.where(up, to_above, to_below), "px", PX, 1)
    below, above = jnp.where(up, first, second), jnp.where(up, second, first)
    freq = lax.all_to_all(freq, "px", 0, 0, tiled=True)
    freq, below, above = lax.optimization_barrier((freq, below, above))
    freq = call(y_inverse_kernel, shape(PY, XP, 2 * LY, W), name="y_inv")(freq, y_inv)
    freq = lax.all_to_all(freq, "py", 0, 0, tiled=True)
    return call(z_inverse_kernel, shape(LX, LY, MERGED), name="z_inv")(freq, z_inv, field, below, above)


def solution(mesh):
    in_specs = (P("px", "py", None), P(), P(), P())
    out_specs = P("px", "py", None)
    return jax.shard_map(body, mesh=mesh, in_specs=in_specs, out_specs=out_specs, check_vma=False)
```

```python
import functools
import math

import jax
import jax.numpy as jnp
import ml_dtypes
import numpy as np
from jax import lax
from jax.experimental import pallas as pl
from jax.experimental.pallas import tpu as pltpu
from jax.sharding import PartitionSpec as P

shrink_level = 0.2
F32 = jnp.float32
BF16 = jnp.bfloat16
VMEM = pltpu.VMEM

PX, PY = 8, 16
LX, LY = 16, 8
Z, KZ, C, CB = 32, 16, 192, 96
W = 2 * C
MERGED = Z * C
XP = LX // 2
XE = XP + 1
ZH = Z // 2
Q = 64


def tables(length, modes, weights):
    product = np.asarray(modes)[:, None] * np.arange(length)[None, :] % length
    angle = product.astype(np.float32) * np.float32(2.0 * math.pi / length)
    factor = np.asarray(weights, np.float32)[:, None] / np.float32(math.sqrt(length))
    rounded = [(f(angle) * factor).astype(ml_dtypes.bfloat16) for f in (np.cos, np.sin)]
    return [t.astype(np.float64) for t in rounded]


def kept(length):
    return np.concatenate([np.arange(length // 4), np.arange(length - length // 4, length)])


def forward(cos, sin):
    return np.stack([np.stack([cos, sin], 1), np.stack([-sin, cos], 1)])


def backward(cos, sin):
    cos, sin = cos.T, sin.T
    return np.stack([np.stack([cos, -sin], 1), np.stack([sin, cos], 1)])


def as_bf16(matrix):
    return np.ascontiguousarray(matrix).astype(ml_dtypes.bfloat16)


@functools.cache
def matrices():
    eye = np.eye(LY)
    one = np.ones(KZ)
    cz, sz = tables(Z, np.arange(KZ), one)
    both = np.stack([cz, -sz], 1).reshape(KZ, 2, ZH, 2)
    z_fwd = np.einsum("kpzs,yw->kpyszw", both, eye).reshape(KZ * 2 * LY, 2 * ZH * LY)
    two = np.where(np.arange(KZ) == 0, 1.0, 2.0)
    cz, sz = tables(Z, np.arange(KZ), two)
    both = np.stack([cz, -sz], 1).reshape(KZ, 2, ZH, 2)
    z_inv = np.einsum("kpzs,yw->szykpw", both, eye).reshape(2 * ZH * LY, KZ * 2 * LY)
    n = PY * LY
    cy, sy = tables(n, kept(n), np.ones(Q))
    y_fwd = forward(cy, sy).reshape(2, PX, Q // PX, 2, PY, LY).transpose(1, 0, 2, 4, 3, 5)
    y_fwd = y_fwd.reshape(2 * Q, 2 * n)
    y_inv = backward(cy, sy).reshape(2, PY, LY, 2, PX, Q // PX)
    y_inv = y_inv.transpose(1, 0, 2, 4, 3, 5).reshape(2 * n, 2 * Q)
    n = PX * LX
    cx, sx = tables(n, kept(n), np.ones(Q))
    x_fwd = forward(cx, sx)
    extra = np.zeros((2, Q, 2, PX, 1, 2))
    extra[..., 1:, 0, 0] = x_fwd[..., LX - 1 : n - LX : LX]
    extra[..., :-1, 0, 1] = x_fwd[..., LX::LX]
    x_fwd = np.concatenate([x_fwd.reshape(2, Q, 2, PX, XP, 2), extra], axis=4)
    x_fwd = x_fwd.transpose(5, 0, 1, 3, 4, 2).reshape(4 * Q, 2 * PX * XE)
    x_inv = backward(cx, sx).reshape(2, PX, XP, 2, 2, Q)
    x_inv = x_inv.transpose(3, 0, 1, 2, 4, 5).reshape(4 * PX * XP, 2 * Q)
    return [as_bf16(m) for m in (z_fwd, z_inv, y_fwd, y_inv, x_fwd, x_inv)]


def dot(a, b):
    return jnp.dot(a, b, preferred_element_type=F32)


def low_half(rows):
    return lax.broadcasted_iota(jnp.int32, (rows, W), 1) < C


def swap(value):
    return pltpu.roll(value, C, 1)


def odd(axis):
    return lax.rem(lax.axis_index(axis), 2) == 1


def by_order(axis, first, second):
    second, first = second.astype(F32), first.astype(F32)
    up, at = odd(axis), lax.axis_index(axis)
    below, above = jnp.where(up, first, second), jnp.where(up, second, first)
    return jnp.where(at == 0, 0.0, below), jnp.where(at == lax.axis_size(axis) - 1, 0.0, above)


def rows_kernel(tok, send_first, send_second):
    step = MERGED // 4
    row = lax.broadcasted_iota(jnp.int32, (2 * LX, LX * LY), 0)
    cell = lax.broadcasted_iota(jnp.int32, (2 * LX, LX * LY), 1)
    wanted = jnp.where(row < LX, row * LY, (row - LX) * LY + LY - 1)
    pick = jnp.where(cell == wanted, 1.0, 0.0).astype(BF16)
    up = odd("py")
    for j in range(4):
        here = slice(j * step, (j + 1) * step)
        data = tok[:, :, here].astype(F32).reshape(LX * LY, step).astype(BF16)
        out = dot(pick, data)
        send_first[:, here] = jnp.where(up, out[:LX], out[LX:]).astype(BF16)
        send_second[:, here] = jnp.where(up, out[LX:], out[:LX]).astype(BF16)


def conv_kernel(tok, narrow, out, shifted, weight):
    weight[...] = jnp.concatenate([narrow[...], narrow[...]], axis=1)
    pad = jnp.zeros((LY, C), F32)
    for x in range(LX):
        shifted[x] = jnp.concatenate([pad, tok[x].astype(F32), pad], axis=1)
    row_at = lax.broadcasted_iota(jnp.int32, (LY, 128), 0)

    @pl.loop(0, MERGED // 128)
    def _(j):
        at = pl.multiple_of(j * 128, 128)
        after = pl.multiple_of(j * 128 + W, 128)
        here = pl.ds(at, 128)
        phase = pl.multiple_of(lax.rem(j, 3) * 128, 128)
        wide = [jnp.broadcast_to(weight[t : t + 1, pl.ds(phase, 128)], (LY, 128)) for t in range(27)]
        sums = {}
        for x in range(LX + 2):
            if x < LX:
                mid = tok[x, :, here].astype(F32)
                before = shifted[x, :, here]
                behind = shifted[x, :, pl.ds(after, 128)]
                for a in range(3):
                    to = x + 2 - a
                    for b in range(3):
                        t = a * 9 + b * 3
                        term = before * wide[t] + mid * wide[t + 1] + behind * wide[t + 2]
                        sums[to, b] = sums[to, b] + term if (to, b) in sums else term
            down = pltpu.roll(sums.pop((x, 0)), 1, 0)
            up = pltpu.roll(sums.pop((x, 2)), LY - 1, 0)
            down = jnp.where(row_at == 0, 0.0, down)
            up = jnp.where(row_at == LY - 1, 0.0, up)
            out[j, x * LY : (x + 1) * LY, :] = sums.pop((x, 1)) + down + up


def edge_kernel(
    conv, first, second, narrow, z_fwd, field, freq, to_below, to_above, ylo, yhi, ylo_s, yhi_s, edge, weight
):
    weight[...] = jnp.concatenate([narrow[...], narrow[...]], axis=1)
    for rows, rows_s, value in zip((ylo, yhi), (ylo_s, yhi_s), by_order("py", first[...], second[...])):
        none = jnp.zeros((2, MERGED), F32)
        value = jnp.concatenate([none, value, none], axis=0)
        rows[...] = value
        pad = jnp.zeros((LX + 4, C), F32)
        rows_s[...] = jnp.concatenate([pad, value, pad], axis=1)

    @pl.loop(0, MERGED // 128)
    def _(j):
        at = pl.multiple_of(j * 128, 128)
        after = pl.multiple_of(j * 128 + W, 128)
        here = pl.ds(at, 128)
        phase = pl.multiple_of(lax.rem(j, 3) * 128, 128)
        edge[j] = jnp.zeros(edge.shape[1:], F32)
        for side, rows, rows_s, b in ((0, ylo, ylo_s, 0), (1, yhi, yhi_s, 2)):
            mid = rows[:, here]
            before = rows_s[:, here]
            behind = rows_s[:, pl.ds(after, 128)]
            total = None
            for a in range(3):
                t = a * 9 + b * 3
                taps = [weight[t + e : t + e + 1, pl.ds(phase, 128)] for e in range(3)]
                term = before * taps[0] + mid * taps[1] + behind * taps[2]
                term = term[a : a + LX + 2]
                total = term if total is None else total + term
            cells = pl.ds(side * (LY - 1), LX + 2, stride=LY)
            edge[j, cells, :] = total

    low = low_half(ZH * LY)
    for xp in range(XE):
        parts = []
        for x in (2 * xp, 2 * xp + 1) if xp < XP else (-1, LX):
            rows = slice((x + 1) * LY, (x + 2) * LY)
            part = (conv[:, rows, :] + edge[:, rows, :]).reshape(ZH, W // 128, LY, 128)
            part = jnp.concatenate([part[:, t].reshape(ZH * LY, 128) for t in range(W // 128)], axis=1)
            part = part.astype(BF16)
            if xp < XP:
                field[x] = part
            parts.append(part)
        first, second = parts
        if xp == XP:
            to_below[...] = first
            to_above[...] = second
        even = jnp.where(low, first, swap(second))
        odd_z = jnp.where(low, swap(first), second)
        out = dot(z_fwd[...], jnp.concatenate([even, odd_z], axis=0))
        freq[:, xp] = out.astype(BF16).reshape(KZ, 2 * LY, W)


def y_forward_kernel(given, y_fwd, out):
    for xp in range(XE):
        data = given[:, xp].reshape(2 * PY * LY, W)
        out[:, xp] = dot(y_fwd[...], data).astype(BF16).reshape(PX, 2 * Q // PX, W)


def gather(rows, out):
    count = 2 * XP * Q // PX
    for d in range(PX):
        block = [rows[t, pl.ds(d * count, count), :] for t in range(W // 128)]
        out[d] = jnp.concatenate(block, axis=1).astype(BF16).reshape(out.shape[1:])


def shrink(v):
    return v - jnp.clip(v, -shrink_level, shrink_level)


def lay_out(weight, width, copies, out):
    for b in range(C // CB):
        columns = []
        for part in range(2):
            block = weight[part, b].astype(F32)
            columns += [jnp.zeros((CB, b * CB), F32)] * (b > 0) + [block]
            columns += [jnp.zeros((CB, width - (b + 1) * CB), F32)] * (width > (b + 1) * CB)
            columns += columns[-2:] * (copies - 1)
        out[b * CB : (b + 1) * CB] = jnp.concatenate(columns, axis=1).astype(BF16)
    out[C:] = jnp.zeros((256 - C, out.shape[1]), BF16)


def spectrum_kernel(given, x_fwd, x_inv, inner_weight, outer_weight, out, rows, arrived, inner, outer):
    lay_out(inner_weight, 256, 1, inner)
    lay_out(outer_weight, C, 2, outer)
    count = Q // PX
    low = low_half(2 * PX * XP)
    wide = given[...].astype(F32).reshape(2 * count * PX * XE, W)
    for t in range(W // 128):
        arrived[t] = wide[:, t * 128 : (t + 1) * 128]
    data = []
    for q in range(count):
        some = [arrived[t, pl.ds(q, 2 * PX * XE, stride=count), :] for t in range(W // 128)]
        data.append(jnp.concatenate(some, axis=1).astype(BF16))
    both = dot(x_fwd[...], jnp.concatenate(data, axis=1))
    spec = []
    for q in range(count):
        part = both[:, q * W : (q + 1) * W]
        part = part[: 2 * Q] + swap(part[2 * Q :])
        spec.append(part[:, :256].astype(BF16))
    mixed = dot(jnp.concatenate(spec, axis=0), inner[...]).reshape(count, 2, Q, 512)
    hidden_r = jnp.tanh(mixed[:, 0, :, :256] - mixed[:, 1, :, 256:])
    hidden_i = jnp.tanh(mixed[:, 0, :, 256:] + mixed[:, 1, :, :256])
    hidden = jnp.stack([hidden_r, hidden_i], axis=1).astype(BF16).reshape(count * 2 * Q, 256)
    mixed = dot(hidden, outer[...]).reshape(count, 2, Q, 2 * W)
    filt_r = shrink(mixed[:, 0, :, :W] - mixed[:, 1, :, W:]).astype(BF16)
    filt_i = shrink(mixed[:, 0, :, W:] + mixed[:, 1, :, :W]).astype(BF16)
    filt = [jnp.concatenate([filt_r[q], filt_i[q]], axis=0) for q in range(count)]
    both = dot(x_inv[...], jnp.concatenate(filt, axis=1))
    for q in range(count):
        part = both[:, q * W : (q + 1) * W]
        back = jnp.where(low, part[: 2 * PX * XP], part[2 * PX * XP :])
        for part in range(2):
            for t in range(W // 128):
                rows[t, pl.ds(part * count + q, PX * XP, stride=2 * count), :] = back[
                    part * PX * XP : (part + 1) * PX * XP, t * 128 : (t + 1) * 128
                ]
    gather(rows, out)


def y_inverse_kernel(given, y_inv, out):
    for xp in range(XP):
        data = given[:, xp].reshape(2 * Q, W)
        out[:, xp] = dot(y_inv[...], data).astype(BF16).reshape(PY, 2 * LY, W)


def z_inverse_kernel(given, z_inv, field, below, above, out_hbm, out, sems):
    low = low_half(ZH * LY)
    copies = []
    for xp in range(XP):
        here = pl.ds(2 * xp, 2)
        data = given[:, xp].reshape(2 * KZ * LY, W)
        value = dot(z_inv[...], data)
        even, odd = value[: ZH * LY], value[ZH * LY :]
        first = jnp.where(low, even, swap(odd)) + field[2 * xp].astype(F32)
        second = jnp.where(low, swap(even), odd) + field[2 * xp + 1].astype(F32)
        if xp == 0:
            first = first + below[...].astype(F32)
        if xp == XP - 1:
            second = second + above[...].astype(F32)
        for x, value in ((2 * xp, first), (2 * xp + 1, second)):
            for z in range(ZH):
                out[x, :, z * W : (z + 1) * W] = value[z * LY : (z + 1) * LY].astype(BF16)
        copies.append(pltpu.make_async_copy(out.at[here], out_hbm.at[here], sems.at[xp]))
        copies[xp].start()
    for copy in copies:
        copy.wait()


def call(kernel, outs, scratch=(), name=None, **specs):
    return pl.pallas_call(
        kernel,
        out_shape=outs,
        scratch_shapes=list(scratch),
        **specs,
        compiler_params=pltpu.CompilerParams(vmem_limit_bytes=20 * 2**20),
        name=name,
    )


def shape(*dims):
    return jax.ShapeDtypeStruct(dims, BF16)


def swap_pairs(value, axis, count, start, ends=False):
    low = range(start, count if ends else count - 1, 2)
    return lax.ppermute(value, axis, [(i, (i + 1) % count) for i in low] + [((i + 1) % count, i) for i in low])


def body(tokens, conv_weight, inner_weight, outer_weight):
    z_fwd, z_inv, y_fwd, y_inv, x_fwd, x_inv = (jnp.asarray(m) for m in matrices())
    wide = MERGED + 2 * C
    first, second = call(rows_kernel, [shape(LX, MERGED)] * 2, name="y_rows")(tokens)
    second = swap_pairs(second, "py", PY, 1, True)
    first = swap_pairs(first, "py", PY, 0)
    filtered = jax.ShapeDtypeStruct((MERGED // 128, (LX + 2) * LY, 128), F32)
    conv = call(
        conv_kernel,
        filtered,
        [
            VMEM((LX, LY, wide), F32),
            VMEM((27, W), F32),
        ],
        name="conv",
    )(tokens, conv_weight)
    rows = [VMEM((LX + 4, MERGED), F32)] * 2 + [VMEM((LX + 4, wide), F32)] * 2
    field, freq, to_below, to_above = call(
        edge_kernel,
        [shape(LX, ZH * LY, W), shape(KZ, XE, 2 * LY, W)] + [shape(ZH * LY, W)] * 2,
        rows + [VMEM(filtered.shape, F32), VMEM((27, W), F32)],
        name="edge_z",
    )(conv, first, second, conv_weight, z_fwd)
    rows = VMEM((W // 128, 2 * XP * Q, 128), F32)
    freq = lax.all_to_all(freq, "py", 0, 0, tiled=True)
    freq = call(y_forward_kernel, shape(PX, XE, 2 * Q // PX, W), name="y_fwd")(freq, y_fwd)
    freq = lax.all_to_all(freq, "px", 0, 0, tiled=True)
    mixing = [VMEM((256, 512), BF16), VMEM((256, 4 * C), BF16)]
    freq = call(spectrum_kernel, shape(PX, XP, 2 * Q // PX, W), [rows, VMEM((W // 128, 2 * XE * Q, 128), F32)] + mixing, name="spec")(
        freq, x_fwd, x_inv, inner_weight, outer_weight
    )
    freq, to_below, to_above = lax.optimization_barrier((freq, to_below, to_above))
    up = odd("px")
    first = swap_pairs(jnp.where(up, to_below, to_above), "px", PX, 0)
    second = swap_pairs(jnp.where(up, to_above, to_below), "px", PX, 1)
    below, above = jnp.where(up, first, second), jnp.where(up, second, first)
    freq = lax.all_to_all(freq, "px", 0, 0, tiled=True)
    freq, below, above = lax.optimization_barrier((freq, below, above))
    freq = call(y_inverse_kernel, shape(PY, XP, 2 * LY, W), name="y_inv")(freq, y_inv)
    freq = lax.all_to_all(freq, "py", 0, 0, tiled=True)
    return call(
        z_inverse_kernel,
        shape(LX, LY, MERGED),
        [VMEM((LX, LY, MERGED), BF16), pltpu.SemaphoreType.DMA((XP,))],
        name="z_inv",
        out_specs=pl.BlockSpec(memory_space=pl.ANY),
    )(freq, z_inv, field, below, above)


def solution(mesh):
    in_specs = (P("px", "py", None), P(), P(), P())
    out_specs = P("px", "py", None)
    return jax.shard_map(body, mesh=mesh, in_specs=in_specs, out_specs=out_specs, check_vma=False)
```

```python
import functools
import math

import jax
import jax.numpy as jnp
import ml_dtypes
import numpy as np
from jax import lax
from jax.experimental import pallas as pl
from jax.experimental.pallas import tpu as pltpu
from jax.sharding import PartitionSpec as P

shrink_level = 0.2
F32 = jnp.float32
BF16 = jnp.bfloat16
VMEM = pltpu.VMEM

PX, PY = 8, 16
LX, LY = 16, 8
Z, KZ, C, CB = 32, 16, 192, 96
W = 2 * C
MERGED = Z * C
XP = LX // 2
XE = XP + 1
ZH = Z // 2
Q = 64


def tables(length, modes, weights):
    product = np.asarray(modes)[:, None] * np.arange(length)[None, :] % length
    angle = product.astype(np.float32) * np.float32(2.0 * math.pi / length)
    factor = np.asarray(weights, np.float32)[:, None] / np.float32(math.sqrt(length))
    rounded = [(f(angle) * factor).astype(ml_dtypes.bfloat16) for f in (np.cos, np.sin)]
    return [t.astype(np.float64) for t in rounded]


def kept(length):
    return np.concatenate([np.arange(length // 4), np.arange(length - length // 4, length)])


def forward(cos, sin):
    return np.stack([np.stack([cos, sin], 1), np.stack([-sin, cos], 1)])


def backward(cos, sin):
    cos, sin = cos.T, sin.T
    return np.stack([np.stack([cos, -sin], 1), np.stack([sin, cos], 1)])


def as_bf16(matrix):
    return np.ascontiguousarray(matrix).astype(ml_dtypes.bfloat16)


@functools.cache
def matrices():
    eye = np.eye(LY)
    one = np.ones(KZ)
    cz, sz = tables(Z, np.arange(KZ), one)
    both = np.stack([cz, -sz], 1).reshape(KZ, 2, ZH, 2)
    z_fwd = np.einsum("kpzs,yw->kpyszw", both, eye).reshape(KZ * 2 * LY, 2 * ZH * LY)
    two = np.where(np.arange(KZ) == 0, 1.0, 2.0)
    cz, sz = tables(Z, np.arange(KZ), two)
    both = np.stack([cz, -sz], 1).reshape(KZ, 2, ZH, 2)
    z_inv = np.einsum("kpzs,yw->szykpw", both, eye).reshape(2 * ZH * LY, KZ * 2 * LY)
    n = PY * LY
    cy, sy = tables(n, kept(n), np.ones(Q))
    y_fwd = forward(cy, sy).reshape(2, PX, Q // PX, 2, PY, LY).transpose(1, 0, 2, 4, 3, 5)
    y_fwd = y_fwd.reshape(2 * Q, 2 * n)
    y_inv = backward(cy, sy).reshape(2, PY, LY, 2, PX, Q // PX)
    y_inv = y_inv.transpose(1, 0, 2, 4, 3, 5).reshape(2 * n, 2 * Q)
    n = PX * LX
    cx, sx = tables(n, kept(n), np.ones(Q))
    x_fwd = forward(cx, sx)
    extra = np.zeros((2, Q, 2, PX, 1, 2))
    extra[..., 1:, 0, 0] = x_fwd[..., LX - 1 : n - LX : LX]
    extra[..., :-1, 0, 1] = x_fwd[..., LX::LX]
    x_fwd = np.concatenate([x_fwd.reshape(2, Q, 2, PX, XP, 2), extra], axis=4)
    x_fwd = x_fwd.transpose(5, 0, 1, 3, 4, 2).reshape(4 * Q, 2 * PX * XE)
    x_inv = backward(cx, sx).reshape(2, PX, XP, 2, 2, Q)
    x_inv = x_inv.transpose(3, 0, 1, 2, 4, 5).reshape(4 * PX * XP, 2 * Q)
    return [as_bf16(m) for m in (z_fwd, z_inv, y_fwd, y_inv, x_fwd, x_inv)]


def dot(a, b):
    return jnp.dot(a, b, preferred_element_type=F32)


def low_half(rows):
    return lax.broadcasted_iota(jnp.int32, (rows, W), 1) < C


def swap(value):
    return pltpu.roll(value, C, 1)


def odd(axis):
    return lax.rem(lax.axis_index(axis), 2) == 1


def by_order(axis, first, second):
    second, first = second.astype(F32), first.astype(F32)
    up, at = odd(axis), lax.axis_index(axis)
    below, above = jnp.where(up, first, second), jnp.where(up, second, first)
    return jnp.where(at == 0, 0.0, below), jnp.where(at == lax.axis_size(axis) - 1, 0.0, above)


def rows_kernel(tok, send_first, send_second):
    step = MERGED // 4
    row = lax.broadcasted_iota(jnp.int32, (2 * LX, LX * LY), 0)
    cell = lax.broadcasted_iota(jnp.int32, (2 * LX, LX * LY), 1)
    wanted = jnp.where(row < LX, row * LY, (row - LX) * LY + LY - 1)
    pick = jnp.where(cell == wanted, 1.0, 0.0).astype(BF16)
    up = odd("py")
    for j in range(4):
        here = slice(j * step, (j + 1) * step)
        data = tok[:, :, here].astype(F32).reshape(LX * LY, step).astype(BF16)
        out = dot(pick, data)
        send_first[:, here] = jnp.where(up, out[:LX], out[LX:]).astype(BF16)
        send_second[:, here] = jnp.where(up, out[LX:], out[:LX]).astype(BF16)


def conv_kernel(tok, narrow, out, shifted, weight):
    weight[...] = jnp.concatenate([narrow[...], narrow[...]], axis=1)
    pad = jnp.zeros((LY, C), F32)
    for x in range(LX):
        shifted[x] = jnp.concatenate([pad, tok[x].astype(F32), pad], axis=1)
    row_at = lax.broadcasted_iota(jnp.int32, (LY, 128), 0)

    @pl.loop(0, MERGED // 128)
    def _(j):
        at = pl.multiple_of(j * 128, 128)
        after = pl.multiple_of(j * 128 + W, 128)
        here = pl.ds(at, 128)
        phase = pl.multiple_of(lax.rem(j, 3) * 128, 128)
        wide = [jnp.broadcast_to(weight[t : t + 1, pl.ds(phase, 128)], (LY, 128)) for t in range(27)]
        sums = {}
        for x in range(LX + 2):
            if x < LX:
                mid = tok[x, :, here].astype(F32)
                before = shifted[x, :, here]
                behind = shifted[x, :, pl.ds(after, 128)]
                for a in range(3):
                    to = x + 2 - a
                    for b in range(3):
                        t = a * 9 + b * 3
                        term = before * wide[t] + mid * wide[t + 1] + behind * wide[t + 2]
                        sums[to, b] = sums[to, b] + term if (to, b) in sums else term
            down = pltpu.roll(sums.pop((x, 0)), 1, 0)
            up = pltpu.roll(sums.pop((x, 2)), LY - 1, 0)
            down = jnp.where(row_at == 0, 0.0, down)
            up = jnp.where(row_at == LY - 1, 0.0, up)
            out[j, x * LY : (x + 1) * LY, :] = sums.pop((x, 1)) + down + up


def edge_kernel(
    conv, first, second, narrow, z_fwd, field, freq, to_below, to_above, ylo, yhi, ylo_s, yhi_s, edge, weight
):
    weight[...] = jnp.concatenate([narrow[...], narrow[...]], axis=1)
    for rows, rows_s, value in zip((ylo, yhi), (ylo_s, yhi_s), by_order("py", first[...], second[...])):
        none = jnp.zeros((2, MERGED), F32)
        value = jnp.concatenate([none, value, none], axis=0)
        rows[...] = value
        pad = jnp.zeros((LX + 4, C), F32)
        rows_s[...] = jnp.concatenate([pad, value, pad], axis=1)

    @pl.loop(0, MERGED // 128)
    def _(j):
        at = pl.multiple_of(j * 128, 128)
        after = pl.multiple_of(j * 128 + W, 128)
        here = pl.ds(at, 128)
        phase = pl.multiple_of(lax.rem(j, 3) * 128, 128)
        edge[j] = jnp.zeros(edge.shape[1:], F32)
        for side, rows, rows_s, b in ((0, ylo, ylo_s, 0), (1, yhi, yhi_s, 2)):
            mid = rows[:, here]
            before = rows_s[:, here]
            behind = rows_s[:, pl.ds(after, 128)]
            total = None
            for a in range(3):
                t = a * 9 + b * 3
                taps = [weight[t + e : t + e + 1, pl.ds(phase, 128)] for e in range(3)]
                term = before * taps[0] + mid * taps[1] + behind * taps[2]
                term = term[a : a + LX + 2]
                total = term if total is None else total + term
            cells = pl.ds(side * (LY - 1), LX + 2, stride=LY)
            edge[j, cells, :] = total

    low = low_half(ZH * LY)
    for xp in range(XE):
        parts = []
        for x in (2 * xp, 2 * xp + 1) if xp < XP else (-1, LX):
            rows = slice((x + 1) * LY, (x + 2) * LY)
            part = (conv[:, rows, :] + edge[:, rows, :]).reshape(ZH, W // 128, LY, 128)
            part = jnp.concatenate([part[:, t].reshape(ZH * LY, 128) for t in range(W // 128)], axis=1)
            part = part.astype(BF16)
            if xp < XP:
                field[x] = part
            parts.append(part)
        first, second = parts
        if xp == XP:
            to_below[...] = first
            to_above[...] = second
        even = jnp.where(low, first, swap(second))
        odd_z = jnp.where(low, swap(first), second)
        out = dot(z_fwd[...], jnp.concatenate([even, odd_z], axis=0))
        freq[:, xp] = out.astype(BF16).reshape(KZ, 2 * LY, W)


def y_forward_kernel(given, y_fwd, out):
    for xp in range(XE):
        data = given[:, xp].reshape(2 * PY * LY, W)
        out[:, xp] = dot(y_fwd[...], data).astype(BF16).reshape(PX, 2 * Q // PX, W)


def gather(rows, out):
    count = 2 * XP * Q // PX
    for d in range(PX):
        block = [rows[t, pl.ds(d * count, count), :] for t in range(W // 128)]
        out[d] = jnp.concatenate(block, axis=1).astype(BF16).reshape(out.shape[1:])


def shrink(v):
    return v - jnp.clip(v, -shrink_level, shrink_level)


def lay_out(weight, width, copies, out):
    for b in range(C // CB):
        columns = []
        for part in range(2):
            block = weight[part, b].astype(F32)
            columns += [jnp.zeros((CB, b * CB), F32)] * (b > 0) + [block]
            columns += [jnp.zeros((CB, width - (b + 1) * CB), F32)] * (width > (b + 1) * CB)
            columns += columns[-2:] * (copies - 1)
        out[b * CB : (b + 1) * CB] = jnp.concatenate(columns, axis=1).astype(BF16)
    out[C:] = jnp.zeros((256 - C, out.shape[1]), BF16)


def spectrum_kernel(given, x_fwd, x_inv, inner_weight, outer_weight, out, rows, arrived, inner, outer):
    lay_out(inner_weight, 256, 1, inner)
    lay_out(outer_weight, C, 2, outer)
    count = Q // PX
    low = low_half(2 * PX * XP)
    wide = given[...].astype(F32).reshape(2 * count * PX * XE, W)
    for t in range(W // 128):
        arrived[t] = wide[:, t * 128 : (t + 1) * 128]
    data = []
    for q in range(count):
        some = [arrived[t, pl.ds(q, 2 * PX * XE, stride=count), :] for t in range(W // 128)]
        data.append(jnp.concatenate(some, axis=1).astype(BF16))
    both = dot(x_fwd[...], jnp.concatenate(data, axis=1))
    spec = []
    for q in range(count):
        part = both[:, q * W : (q + 1) * W]
        part = part[: 2 * Q] + swap(part[2 * Q :])
        spec.append(part[:, :256].astype(BF16))
    mixed = dot(jnp.concatenate(spec, axis=0), inner[...]).reshape(count, 2, Q, 512)
    hidden_r = jnp.tanh(mixed[:, 0, :, :256] - mixed[:, 1, :, 256:])
    hidden_i = jnp.tanh(mixed[:, 0, :, 256:] + mixed[:, 1, :, :256])
    hidden = jnp.stack([hidden_r, hidden_i], axis=1).astype(BF16).reshape(count * 2 * Q, 256)
    mixed = dot(hidden, outer[...]).reshape(count, 2, Q, 2 * W)
    filt_r = shrink(mixed[:, 0, :, :W] - mixed[:, 1, :, W:]).astype(BF16)
    filt_i = shrink(mixed[:, 0, :, W:] + mixed[:, 1, :, :W]).astype(BF16)
    filt = [jnp.concatenate([filt_r[q], filt_i[q]], axis=0) for q in range(count)]
    both = dot(x_inv[...], jnp.concatenate(filt, axis=1))
    for q in range(count):
        part = both[:, q * W : (q + 1) * W]
        back = jnp.where(low, part[: 2 * PX * XP], part[2 * PX * XP :])
        for part in range(2):
            for t in range(W // 128):
                rows[t, pl.ds(part * count + q, PX * XP, stride=2 * count), :] = back[
                    part * PX * XP : (part + 1) * PX * XP, t * 128 : (t + 1) * 128
                ]
    gather(rows, out)


def y_inverse_kernel(given, y_inv, out):
    for xp in range(XP):
        data = given[:, xp].reshape(2 * Q, W)
        out[:, xp] = dot(y_inv[...], data).astype(BF16).reshape(PY, 2 * LY, W)


def z_inverse_kernel(given, z_inv, field, below, above, out_hbm, out, sems):
    low = low_half(ZH * LY)
    below, above = by_order("px", below[...], above[...])
    copies = []
    for xp in range(XP):
        here = pl.ds(2 * xp, 2)
        data = given[:, xp].reshape(2 * KZ * LY, W)
        value = dot(z_inv[...], data)
        even, odd = value[: ZH * LY], value[ZH * LY :]
        first = jnp.where(low, even, swap(odd)) + field[2 * xp].astype(F32)
        second = jnp.where(low, swap(even), odd) + field[2 * xp + 1].astype(F32)
        if xp == 0:
            first = first + below
        if xp == XP - 1:
            second = second + above
        for x, value in ((2 * xp, first), (2 * xp + 1, second)):
            for z in range(ZH):
                out[x, :, z * W : (z + 1) * W] = value[z * LY : (z + 1) * LY].astype(BF16)
        copies.append(pltpu.make_async_copy(out.at[here], out_hbm.at[here], sems.at[xp]))
        copies[xp].start()
    for copy in copies:
        copy.wait()


def call(kernel, outs, scratch=(), name=None, **specs):
    return pl.pallas_call(
        kernel,
        out_shape=outs,
        scratch_shapes=list(scratch),
        **specs,
        compiler_params=pltpu.CompilerParams(vmem_limit_bytes=20 * 2**20),
        name=name,
    )


def shape(*dims):
    return jax.ShapeDtypeStruct(dims, BF16)


def swap_pairs(value, axis, start):
    pairs = []
    for x in range(PX):
        for y in range(PY):
            at, count = (x, PX) if axis == "px" else (y, PY)
            to = at + 1 if (at - start) % 2 == 0 else at - 1
            if 0 <= to < count:
                x_to, y_to = (to, y) if axis == "px" else (x, to)
            else:
                x_to, y_to = (x, y ^ 1) if axis == "px" else (x ^ 1, y)
            pairs.append((x * PY + y, x_to * PY + y_to))
    return lax.ppermute(value, ("px", "py"), pairs)


def body(tokens, conv_weight, inner_weight, outer_weight):
    z_fwd, z_inv, y_fwd, y_inv, x_fwd, x_inv = (jnp.asarray(m) for m in matrices())
    wide = MERGED + 2 * C
    first, second = call(rows_kernel, [shape(LX, MERGED)] * 2, name="y_rows")(tokens)
    second = swap_pairs(second, "py", 1)
    first = swap_pairs(first, "py", 0)
    filtered = jax.ShapeDtypeStruct((MERGED // 128, (LX + 2) * LY, 128), F32)
    conv = call(
        conv_kernel,
        filtered,
        [
            VMEM((LX, LY, wide), F32),
            VMEM((27, W), F32),
        ],
        name="conv",
    )(tokens, conv_weight)
    rows = [VMEM((LX + 4, MERGED), F32)] * 2 + [VMEM((LX + 4, wide), F32)] * 2
    field, freq, to_below, to_above = call(
        edge_kernel,
        [shape(LX, ZH * LY, W), shape(KZ, XE, 2 * LY, W)] + [shape(ZH * LY, W)] * 2,
        rows + [VMEM(filtered.shape, F32), VMEM((27, W), F32)],
        name="edge_z",
    )(conv, first, second, conv_weight, z_fwd)
    rows = VMEM((W // 128, 2 * XP * Q, 128), F32)
    freq = lax.all_to_all(freq, "py", 0, 0, tiled=True)
    freq = call(y_forward_kernel, shape(PX, XE, 2 * Q // PX, W), name="y_fwd")(freq, y_fwd)
    freq = lax.all_to_all(freq, "px", 0, 0, tiled=True)
    mixing = [VMEM((256, 512), BF16), VMEM((256, 4 * C), BF16)]
    freq = call(spectrum_kernel, shape(PX, XP, 2 * Q // PX, W), [rows, VMEM((W // 128, 2 * XE * Q, 128), F32)] + mixing, name="spec")(
        freq, x_fwd, x_inv, inner_weight, outer_weight
    )
    freq, to_below, to_above = lax.optimization_barrier((freq, to_below, to_above))
    up = odd("px")
    first = swap_pairs(jnp.where(up, to_below, to_above), "px", 0)
    second = swap_pairs(jnp.where(up, to_above, to_below), "px", 1)
    freq = lax.all_to_all(freq, "px", 0, 0, tiled=True)
    freq = call(y_inverse_kernel, shape(PY, XP, 2 * LY, W), name="y_inv")(freq, y_inv)
    freq, first, second = lax.optimization_barrier((freq, first, second))
    freq = lax.all_to_all(freq, "py", 0, 0, tiled=True)
    return call(
        z_inverse_kernel,
        shape(LX, LY, MERGED),
        [VMEM((LX, LY, MERGED), BF16), pltpu.SemaphoreType.DMA((XP,))],
        name="z_inv",
        out_specs=pl.BlockSpec(memory_space=pl.ANY),
    )(freq, z_inv, field, first, second)


def solution(mesh):
    in_specs = (P("px", "py", None), P(), P(), P())
    out_specs = P("px", "py", None)
    return jax.shard_map(body, mesh=mesh, in_specs=in_specs, out_specs=out_specs, check_vma=False)
```

```python
import functools
import math

import jax
import jax.numpy as jnp
import ml_dtypes
import numpy as np
from jax import lax
from jax.experimental import pallas as pl
from jax.experimental.pallas import tpu as pltpu
from jax.sharding import PartitionSpec as P

shrink_level = 0.2
F32 = jnp.float32
BF16 = jnp.bfloat16
VMEM = pltpu.VMEM

PX, PY = 8, 16
LX, LY = 16, 8
Z, KZ, C, CB = 32, 16, 192, 96
W = 2 * C
MERGED = Z * C
XP = LX // 2
XE = XP + 1
ZH = Z // 2
Q = 64


def tables(length, modes, weights):
    product = np.asarray(modes)[:, None] * np.arange(length)[None, :] % length
    angle = product.astype(np.float32) * np.float32(2.0 * math.pi / length)
    factor = np.asarray(weights, np.float32)[:, None] / np.float32(math.sqrt(length))
    rounded = [(f(angle) * factor).astype(ml_dtypes.bfloat16) for f in (np.cos, np.sin)]
    return [t.astype(np.float64) for t in rounded]


def kept(length):
    return np.concatenate([np.arange(length // 4), np.arange(length - length // 4, length)])


def forward(cos, sin):
    return np.stack([np.stack([cos, sin], 1), np.stack([-sin, cos], 1)])


def backward(cos, sin):
    cos, sin = cos.T, sin.T
    return np.stack([np.stack([cos, -sin], 1), np.stack([sin, cos], 1)])


def as_bf16(matrix):
    return np.ascontiguousarray(matrix).astype(ml_dtypes.bfloat16)


@functools.cache
def matrices():
    eye = np.eye(LY)
    one = np.ones(KZ)
    cz, sz = tables(Z, np.arange(KZ), one)
    both = np.stack([cz, -sz], 1).reshape(KZ, 2, ZH, 2)
    z_fwd = np.einsum("kpzs,yw->kpyszw", both, eye).reshape(KZ * 2 * LY, 2 * ZH * LY)
    two = np.where(np.arange(KZ) == 0, 1.0, 2.0)
    cz, sz = tables(Z, np.arange(KZ), two)
    both = np.stack([cz, -sz], 1).reshape(KZ, 2, ZH, 2)
    z_inv = np.einsum("kpzs,yw->szykpw", both, eye).reshape(2 * ZH * LY, KZ * 2 * LY)
    n = PY * LY
    cy, sy = tables(n, kept(n), np.ones(Q))
    y_fwd = forward(cy, sy).reshape(2, PX, Q // PX, 2, PY, LY).transpose(1, 0, 2, 4, 3, 5)
    y_fwd = y_fwd.reshape(2 * Q, 2 * n)
    y_inv = backward(cy, sy).reshape(2, PY, LY, 2, PX, Q // PX)
    y_inv = y_inv.transpose(1, 0, 2, 4, 3, 5).reshape(2 * n, 2 * Q)
    n = PX * LX
    cx, sx = tables(n, kept(n), np.ones(Q))
    x_fwd = forward(cx, sx)
    extra = np.zeros((2, Q, 2, PX, 1, 2))
    extra[..., 1:, 0, 0] = x_fwd[..., LX - 1 : n - LX : LX]
    extra[..., :-1, 0, 1] = x_fwd[..., LX::LX]
    x_fwd = np.concatenate([x_fwd.reshape(2, Q, 2, PX, XP, 2), extra], axis=4)
    x_fwd = x_fwd.transpose(5, 0, 1, 3, 4, 2).reshape(4 * Q, 2 * PX * XE)
    x_inv = backward(cx, sx).reshape(2, PX, XP, 2, 2, Q)
    x_inv = x_inv.transpose(3, 0, 1, 2, 4, 5).reshape(4 * PX * XP, 2 * Q)
    return [as_bf16(m) for m in (z_fwd, z_inv, y_fwd, y_inv, x_fwd, x_inv)]


def dot(a, b):
    return jnp.dot(a, b, preferred_element_type=F32)


def low_half(rows):
    return lax.broadcasted_iota(jnp.int32, (rows, W), 1) < C


def swap(value):
    return pltpu.roll(value, C, 1)


def odd(axis):
    return lax.rem(lax.axis_index(axis), 2) == 1


def by_order(axis, first, second):
    second, first = second.astype(F32), first.astype(F32)
    up, at = odd(axis), lax.axis_index(axis)
    below, above = jnp.where(up, first, second), jnp.where(up, second, first)
    return jnp.where(at == 0, 0.0, below), jnp.where(at == lax.axis_size(axis) - 1, 0.0, above)


def rows_kernel(tok, send_first, send_second):
    step = MERGED // 4
    row = lax.broadcasted_iota(jnp.int32, (2 * LX, LX * LY), 0)
    cell = lax.broadcasted_iota(jnp.int32, (2 * LX, LX * LY), 1)
    wanted = jnp.where(row < LX, row * LY, (row - LX) * LY + LY - 1)
    pick = jnp.where(cell == wanted, 1.0, 0.0).astype(BF16)
    up = odd("py")
    for j in range(4):
        here = slice(j * step, (j + 1) * step)
        data = tok[:, :, here].astype(F32).reshape(LX * LY, step).astype(BF16)
        out = dot(pick, data)
        send_first[:, here] = jnp.where(up, out[:LX], out[LX:]).astype(BF16)
        send_second[:, here] = jnp.where(up, out[LX:], out[:LX]).astype(BF16)


def conv_kernel(tok, narrow, out, shifted, weight):
    weight[...] = jnp.concatenate([narrow[...], narrow[...]], axis=1)
    pad = jnp.zeros((LY, C), F32)
    for x in range(LX):
        shifted[x] = jnp.concatenate([pad, tok[x].astype(F32), pad], axis=1)
    row_at = lax.broadcasted_iota(jnp.int32, (LY, 128), 0)

    @pl.loop(0, MERGED // 128)
    def _(j):
        at = pl.multiple_of(j * 128, 128)
        after = pl.multiple_of(j * 128 + W, 128)
        here = pl.ds(at, 128)
        phase = pl.multiple_of(lax.rem(j, 3) * 128, 128)
        wide = [jnp.broadcast_to(weight[t : t + 1, pl.ds(phase, 128)], (LY, 128)) for t in range(27)]
        sums = {}
        for x in range(LX + 2):
            if x < LX:
                mid = tok[x, :, here].astype(F32)
                before = shifted[x, :, here]
                behind = shifted[x, :, pl.ds(after, 128)]
                for a in range(3):
                    to = x + 2 - a
                    for b in range(3):
                        t = a * 9 + b * 3
                        term = before * wide[t] + mid * wide[t + 1] + behind * wide[t + 2]
                        sums[to, b] = sums[to, b] + term if (to, b) in sums else term
            down = pltpu.roll(sums.pop((x, 0)), 1, 0)
            up = pltpu.roll(sums.pop((x, 2)), LY - 1, 0)
            down = jnp.where(row_at == 0, 0.0, down)
            up = jnp.where(row_at == LY - 1, 0.0, up)
            out[j, x * LY : (x + 1) * LY, :] = sums.pop((x, 1)) + down + up


def edge_kernel(
    conv, first, second, narrow, z_fwd, field, freq, to_below, to_above, ylo, yhi, ylo_s, yhi_s, edge, weight
):
    weight[...] = jnp.concatenate([narrow[...], narrow[...]], axis=1)
    for rows, rows_s, value in zip((ylo, yhi), (ylo_s, yhi_s), by_order("py", first[...], second[...])):
        rows[...] = value
        pad = jnp.zeros((LX, C), F32)
        rows_s[...] = jnp.concatenate([pad, value, pad], axis=1)

    @pl.loop(0, MERGED // 128)
    def _(j):
        at = pl.multiple_of(j * 128, 128)
        after = pl.multiple_of(j * 128 + W, 128)
        here = pl.ds(at, 128)
        phase = pl.multiple_of(lax.rem(j, 3) * 128, 128)
        edge[j, : (LX + 2) * LY, :] = jnp.zeros(((LX + 2) * LY, 128), F32)
        for side, rows, rows_s, b in ((0, ylo, ylo_s, 0), (1, yhi, yhi_s, 2)):
            mid = rows[:, here]
            before = rows_s[:, here]
            behind = rows_s[:, pl.ds(after, 128)]
            total = None
            for a in range(3):
                t = a * 9 + b * 3
                taps = [weight[t + e : t + e + 1, pl.ds(phase, 128)] for e in range(3)]
                term = before * taps[0] + mid * taps[1] + behind * taps[2]
                around = [jnp.zeros((n, 128), F32) for n in (2 - a, a) if n]
                term = jnp.concatenate([term] + around if a == 2 else around[:1] + [term] + around[1:], axis=0)
                total = term if total is None else total + term
            cells = pl.ds(side * (LY - 1), LX + 2, stride=LY)
            edge[j, cells, :] = total

    low = low_half(ZH * LY)
    for xp in range(XE):
        parts = []
        for x in (2 * xp, 2 * xp + 1) if xp < XP else (-1, LX):
            rows = slice((x + 1) * LY, (x + 2) * LY)
            part = (conv[:, rows, :] + edge[:, rows, :]).reshape(ZH, W // 128, LY, 128)
            part = jnp.concatenate([part[:, t].reshape(ZH * LY, 128) for t in range(W // 128)], axis=1)
            part = part.astype(BF16)
            if xp < XP:
                field[x] = part
            parts.append(part)
        first, second = parts
        if xp == XP:
            to_below[...] = first
            to_above[...] = second
        even = jnp.where(low, first, swap(second))
        odd_z = jnp.where(low, swap(first), second)
        out = dot(z_fwd[...], jnp.concatenate([even, odd_z], axis=0))
        freq[:, xp] = out.astype(BF16).reshape(KZ, 2 * LY, W)


def y_forward_kernel(given, y_fwd, out):
    for xp in range(XE):
        data = given[:, xp].reshape(2 * PY * LY, W)
        out[:, xp] = dot(y_fwd[...], data).astype(BF16).reshape(PX, 2 * Q // PX, W)


def gather(rows, out):
    count = 2 * XP * Q // PX
    for d in range(PX):
        block = [rows[t, pl.ds(d * count, count), :] for t in range(W // 128)]
        out[d] = jnp.concatenate(block, axis=1).astype(BF16).reshape(out.shape[1:])


def shrink(v):
    return v - jnp.clip(v, -shrink_level, shrink_level)


def lay_out(weight, width, copies, out):
    for b in range(C // CB):
        columns = []
        for part in range(2):
            block = weight[part, b].astype(F32)
            columns += [jnp.zeros((CB, b * CB), F32)] * (b > 0) + [block]
            columns += [jnp.zeros((CB, width - (b + 1) * CB), F32)] * (width > (b + 1) * CB)
            columns += columns[-2:] * (copies - 1)
        out[b * CB : (b + 1) * CB] = jnp.concatenate(columns, axis=1).astype(BF16)
    out[C:] = jnp.zeros((256 - C, out.shape[1]), BF16)


def spectrum_kernel(given, x_fwd, x_inv, inner_weight, outer_weight, out, rows, arrived, inner, outer):
    lay_out(inner_weight, 256, 1, inner)
    lay_out(outer_weight, C, 2, outer)
    count = Q // PX
    low = low_half(2 * PX * XP)
    wide = given[...].astype(F32).reshape(2 * count * PX * XE, W)
    for t in range(W // 128):
        arrived[t] = wide[:, t * 128 : (t + 1) * 128]
    data = []
    for q in range(count):
        some = [arrived[t, pl.ds(q, 2 * PX * XE, stride=count), :] for t in range(W // 128)]
        data.append(jnp.concatenate(some, axis=1).astype(BF16))
    both = dot(x_fwd[...], jnp.concatenate(data, axis=1))
    spec = []
    for q in range(count):
        part = both[:, q * W : (q + 1) * W]
        part = part[: 2 * Q] + swap(part[2 * Q :])
        spec.append(part[:, :256].astype(BF16))
    mixed = dot(jnp.concatenate(spec, axis=0), inner[...]).reshape(count, 2, Q, 512)
    hidden_r = jnp.tanh(mixed[:, 0, :, :256] - mixed[:, 1, :, 256:])
    hidden_i = jnp.tanh(mixed[:, 0, :, 256:] + mixed[:, 1, :, :256])
    hidden = jnp.stack([hidden_r, hidden_i], axis=1).astype(BF16).reshape(count * 2 * Q, 256)
    mixed = dot(hidden, outer[...]).reshape(count, 2, Q, 2 * W)
    filt_r = shrink(mixed[:, 0, :, :W] - mixed[:, 1, :, W:]).astype(BF16)
    filt_i = shrink(mixed[:, 0, :, W:] + mixed[:, 1, :, :W]).astype(BF16)
    filt = [jnp.concatenate([filt_r[q], filt_i[q]], axis=0) for q in range(count)]
    both = dot(x_inv[...], jnp.concatenate(filt, axis=1))
    for q in range(count):
        part = both[:, q * W : (q + 1) * W]
        back = jnp.where(low, part[: 2 * PX * XP], part[2 * PX * XP :])
        for part in range(2):
            for t in range(W // 128):
                rows[t, pl.ds(part * count + q, PX * XP, stride=2 * count), :] = back[
                    part * PX * XP : (part + 1) * PX * XP, t * 128 : (t + 1) * 128
                ]
    gather(rows, out)


def y_inverse_kernel(given, y_inv, out):
    for xp in range(XP):
        data = given[:, xp].reshape(2 * Q, W)
        out[:, xp] = dot(y_inv[...], data).astype(BF16).reshape(PY, 2 * LY, W)


def z_inverse_kernel(given, z_inv, field, below, above, out_hbm, out, sems):
    low = low_half(ZH * LY)
    below, above = by_order("px", below[...], above[...])
    copies = []
    for xp in range(XP):
        here = pl.ds(2 * xp, 2)
        data = given[:, xp].reshape(2 * KZ * LY, W)
        value = dot(z_inv[...], data)
        even, odd = value[: ZH * LY], value[ZH * LY :]
        first = jnp.where(low, even, swap(odd)) + field[2 * xp].astype(F32)
        second = jnp.where(low, swap(even), odd) + field[2 * xp + 1].astype(F32)
        if xp == 0:
            first = first + below
        if xp == XP - 1:
            second = second + above
        for x, value in ((2 * xp, first), (2 * xp + 1, second)):
            for z in range(ZH):
                out[x, :, z * W : (z + 1) * W] = value[z * LY : (z + 1) * LY].astype(BF16)
        copies.append(pltpu.make_async_copy(out.at[here], out_hbm.at[here], sems.at[xp]))
        copies[xp].start()
    for copy in copies:
        copy.wait()


def call(kernel, outs, scratch=(), name=None, **specs):
    return pl.pallas_call(
        kernel,
        out_shape=outs,
        scratch_shapes=list(scratch),
        **specs,
        compiler_params=pltpu.CompilerParams(vmem_limit_bytes=20 * 2**20),
        name=name,
    )


def shape(*dims):
    return jax.ShapeDtypeStruct(dims, BF16)


def swap_pairs(value, axis, start):
    pairs = []
    for x in range(PX):
        for y in range(PY):
            at, count = (x, PX) if axis == "px" else (y, PY)
            to = at + 1 if (at - start) % 2 == 0 else at - 1
            if 0 <= to < count:
                x_to, y_to = (to, y) if axis == "px" else (x, to)
            else:
                x_to, y_to = (x, y ^ 1) if axis == "px" else (x ^ 1, y)
            pairs.append((x * PY + y, x_to * PY + y_to))
    return lax.ppermute(value, ("px", "py"), pairs)


def body(tokens, conv_weight, inner_weight, outer_weight):
    z_fwd, z_inv, y_fwd, y_inv, x_fwd, x_inv = (jnp.asarray(m) for m in matrices())
    wide = MERGED + 2 * C
    first, second = call(rows_kernel, [shape(LX, MERGED)] * 2, name="y_rows")(tokens)
    second = swap_pairs(second, "py", 1)
    first = swap_pairs(first, "py", 0)
    filtered = jax.ShapeDtypeStruct((MERGED // 128, (LX + 2) * LY, 128), F32)
    conv = call(
        conv_kernel,
        filtered,
        [
            VMEM((LX, LY, wide), F32),
            VMEM((27, W), F32),
        ],
        name="conv",
    )(tokens, conv_weight)
    rows = [VMEM((LX, MERGED), F32)] * 2 + [VMEM((LX, wide), F32)] * 2
    field, freq, to_below, to_above = call(
        edge_kernel,
        [shape(LX, ZH * LY, W), shape(KZ, XE, 2 * LY, W)] + [shape(ZH * LY, W)] * 2,
        rows + [VMEM((MERGED // 128, 24 * LY, 128), F32), VMEM((27, W), F32)],
        name="edge_z",
    )(conv, first, second, conv_weight, z_fwd)
    rows = VMEM((W // 128, 2 * XP * Q, 128), F32)
    freq = lax.all_to_all(freq, "py", 0, 0, tiled=True)
    freq = call(y_forward_kernel, shape(PX, XE, 2 * Q // PX, W), name="y_fwd")(freq, y_fwd)
    freq = lax.all_to_all(freq, "px", 0, 0, tiled=True)
    mixing = [VMEM((256, 512), BF16), VMEM((256, 4 * C), BF16)]
    freq = call(spectrum_kernel, shape(PX, XP, 2 * Q // PX, W), [rows, VMEM((W // 128, 2 * XE * Q, 128), F32)] + mixing, name="spec")(
        freq, x_fwd, x_inv, inner_weight, outer_weight
    )
    freq, to_below, to_above = lax.optimization_barrier((freq, to_below, to_above))
    up = odd("px")
    first = swap_pairs(jnp.where(up, to_below, to_above), "px", 0)
    second = swap_pairs(jnp.where(up, to_above, to_below), "px", 1)
    freq = lax.all_to_all(freq, "px", 0, 0, tiled=True)
    freq = call(y_inverse_kernel, shape(PY, XP, 2 * LY, W), name="y_inv")(freq, y_inv)
    freq, first, second = lax.optimization_barrier((freq, first, second))
    freq = lax.all_to_all(freq, "py", 0, 0, tiled=True)
    return call(
        z_inverse_kernel,
        shape(LX, LY, MERGED),
        [VMEM((LX, LY, MERGED), BF16), pltpu.SemaphoreType.DMA((XP,))],
        name="z_inv",
        out_specs=pl.BlockSpec(memory_space=pl.ANY),
    )(freq, z_inv, field, first, second)


def solution(mesh):
    in_specs = (P("px", "py", None), P(), P(), P())
    out_specs = P("px", "py", None)
    return jax.shard_map(body, mesh=mesh, in_specs=in_specs, out_specs=out_specs, check_vma=False)
```

```python
import functools
import math

import jax
import jax.numpy as jnp
import ml_dtypes
import numpy as np
from jax import lax
from jax.experimental import pallas as pl
from jax.experimental.pallas import tpu as pltpu
from jax.sharding import PartitionSpec as P

shrink_level = 0.2
F32 = jnp.float32
BF16 = jnp.bfloat16
VMEM = pltpu.VMEM

PX, PY = 8, 16
LX, LY = 16, 8
Z, KZ, C, CB = 32, 16, 192, 96
W = 2 * C
MERGED = Z * C
XP = LX // 2
XE = XP + 1
ZH = Z // 2
Q = 64


def tables(length, modes, weights):
    product = np.asarray(modes)[:, None] * np.arange(length)[None, :] % length
    angle = product.astype(np.float32) * np.float32(2.0 * math.pi / length)
    factor = np.asarray(weights, np.float32)[:, None] / np.float32(math.sqrt(length))
    rounded = [(f(angle) * factor).astype(ml_dtypes.bfloat16) for f in (np.cos, np.sin)]
    return [t.astype(np.float64) for t in rounded]


def kept(length):
    return np.concatenate([np.arange(length // 4), np.arange(length - length // 4, length)])


def forward(cos, sin):
    return np.stack([np.stack([cos, sin], 1), np.stack([-sin, cos], 1)])


def backward(cos, sin):
    cos, sin = cos.T, sin.T
    return np.stack([np.stack([cos, -sin], 1), np.stack([sin, cos], 1)])


def as_bf16(matrix):
    return np.ascontiguousarray(matrix).astype(ml_dtypes.bfloat16)


@functools.cache
def matrices():
    eye = np.eye(LY)
    one = np.ones(KZ)
    cz, sz = tables(Z, np.arange(KZ), one)
    both = np.stack([cz, -sz], 1).reshape(KZ, 2, ZH, 2)
    z_fwd = np.einsum("kpzs,yw->kpyszw", both, eye).reshape(KZ * 2 * LY, 2 * ZH * LY)
    two = np.where(np.arange(KZ) == 0, 1.0, 2.0)
    cz, sz = tables(Z, np.arange(KZ), two)
    both = np.stack([cz, -sz], 1).reshape(KZ, 2, ZH, 2)
    z_inv = np.einsum("kpzs,yw->szykpw", both, eye).reshape(2 * ZH * LY, KZ * 2 * LY)
    n = PY * LY
    cy, sy = tables(n, kept(n), np.ones(Q))
    y_fwd = forward(cy, sy).reshape(2, PX, Q // PX, 2, PY, LY).transpose(1, 0, 2, 4, 3, 5)
    y_fwd = y_fwd.reshape(2 * Q, 2 * n)
    y_inv = backward(cy, sy).reshape(2, PY, LY, 2, PX, Q // PX)
    y_inv = y_inv.transpose(1, 0, 2, 4, 3, 5).reshape(2 * n, 2 * Q)
    n = PX * LX
    cx, sx = tables(n, kept(n), np.ones(Q))
    x_fwd = forward(cx, sx)
    extra = np.zeros((2, Q, 2, PX, 1, 2))
    extra[..., 1:, 0, 0] = x_fwd[..., LX - 1 : n - LX : LX]
    extra[..., :-1, 0, 1] = x_fwd[..., LX::LX]
    x_fwd = np.concatenate([x_fwd.reshape(2, Q, 2, PX, XP, 2), extra], axis=4)
    x_fwd = x_fwd.transpose(5, 0, 1, 3, 4, 2).reshape(4 * Q, 2 * PX * XE)
    x_inv = backward(cx, sx).reshape(2, PX, XP, 2, 2, Q)
    x_inv = x_inv.transpose(3, 0, 1, 2, 4, 5).reshape(4 * PX * XP, 2 * Q)
    return [as_bf16(m) for m in (z_fwd, z_inv, y_fwd, y_inv, x_fwd, x_inv)]


def dot(a, b):
    return jnp.dot(a, b, preferred_element_type=F32)


def low_half(rows):
    return lax.broadcasted_iota(jnp.int32, (rows, W), 1) < C


def swap(value):
    return pltpu.roll(value, C, 1)


def odd(axis):
    return lax.rem(lax.axis_index(axis), 2) == 1


def by_order(axis, first, second):
    second, first = second.astype(F32), first.astype(F32)
    up, at = odd(axis), lax.axis_index(axis)
    below, above = jnp.where(up, first, second), jnp.where(up, second, first)
    return jnp.where(at == 0, 0.0, below), jnp.where(at == lax.axis_size(axis) - 1, 0.0, above)


def rows_kernel(tok, send_first, send_second):
    step = MERGED // 4
    row = lax.broadcasted_iota(jnp.int32, (2 * LX, LX * LY), 0)
    cell = lax.broadcasted_iota(jnp.int32, (2 * LX, LX * LY), 1)
    wanted = jnp.where(row < LX, row * LY, (row - LX) * LY + LY - 1)
    pick = jnp.where(cell == wanted, 1.0, 0.0).astype(BF16)
    up = odd("py")
    for j in range(4):
        here = slice(j * step, (j + 1) * step)
        data = tok[:, :, here].astype(F32).reshape(LX * LY, step).astype(BF16)
        out = dot(pick, data)
        send_first[:, here] = jnp.where(up, out[:LX], out[LX:]).astype(BF16)
        send_second[:, here] = jnp.where(up, out[LX:], out[:LX]).astype(BF16)


def conv_kernel(tok, narrow, out, shifted, weight):
    weight[...] = jnp.concatenate([narrow[...], narrow[...]], axis=1)
    pad = jnp.zeros((LY, C), F32)
    for x in range(LX):
        shifted[x] = jnp.concatenate([pad, tok[x].astype(F32), pad], axis=1)
    row_at = lax.broadcasted_iota(jnp.int32, (LY, 128), 0)

    @pl.loop(0, MERGED // 128, unroll=6)
    def _(j):
        at = pl.multiple_of(j * 128, 128)
        after = pl.multiple_of(j * 128 + W, 128)
        here = pl.ds(at, 128)
        phase = pl.multiple_of(lax.rem(j, 3) * 128, 128)
        wide = [jnp.broadcast_to(weight[t : t + 1, pl.ds(phase, 128)], (LY, 128)) for t in range(27)]
        sums = {}
        for x in range(LX + 2):
            if x < LX:
                mid = tok[x, :, here].astype(F32)
                before = shifted[x, :, here]
                behind = shifted[x, :, pl.ds(after, 128)]
                for a in range(3):
                    to = x + 2 - a
                    for b in range(3):
                        t = a * 9 + b * 3
                        term = before * wide[t] + mid * wide[t + 1] + behind * wide[t + 2]
                        sums[to, b] = sums[to, b] + term if (to, b) in sums else term
            down = pltpu.roll(sums.pop((x, 0)), 1, 0)
            up = pltpu.roll(sums.pop((x, 2)), LY - 1, 0)
            down = jnp.where(row_at == 0, 0.0, down)
            up = jnp.where(row_at == LY - 1, 0.0, up)
            out[j, x * LY : (x + 1) * LY, :] = sums.pop((x, 1)) + down + up


def edge_kernel(
    conv, first, second, narrow, z_fwd, field, freq, to_below, to_above, ylo, yhi, ylo_s, yhi_s, edge, weight
):
    weight[...] = jnp.concatenate([narrow[...], narrow[...]], axis=1)
    for rows, rows_s, value in zip((ylo, yhi), (ylo_s, yhi_s), by_order("py", first[...], second[...])):
        rows[...] = value
        pad = jnp.zeros((LX, C), F32)
        rows_s[...] = jnp.concatenate([pad, value, pad], axis=1)

    @pl.loop(0, MERGED // 128, unroll=6)
    def _(j):
        at = pl.multiple_of(j * 128, 128)
        after = pl.multiple_of(j * 128 + W, 128)
        here = pl.ds(at, 128)
        phase = pl.multiple_of(lax.rem(j, 3) * 128, 128)
        edge[j, : (LX + 2) * LY, :] = jnp.zeros(((LX + 2) * LY, 128), F32)
        for side, rows, rows_s, b in ((0, ylo, ylo_s, 0), (1, yhi, yhi_s, 2)):
            mid = rows[:, here]
            before = rows_s[:, here]
            behind = rows_s[:, pl.ds(after, 128)]
            total = None
            for a in range(3):
                t = a * 9 + b * 3
                taps = [weight[t + e : t + e + 1, pl.ds(phase, 128)] for e in range(3)]
                term = before * taps[0] + mid * taps[1] + behind * taps[2]
                around = [jnp.zeros((n, 128), F32) for n in (2 - a, a) if n]
                term = jnp.concatenate([term] + around if a == 2 else around[:1] + [term] + around[1:], axis=0)
                total = term if total is None else total + term
            cells = pl.ds(side * (LY - 1), LX + 2, stride=LY)
            edge[j, cells, :] = total

    low = low_half(ZH * LY)
    for xp in range(XE):
        parts = []
        for x in (2 * xp, 2 * xp + 1) if xp < XP else (-1, LX):
            rows = slice((x + 1) * LY, (x + 2) * LY)
            part = (conv[:, rows, :] + edge[:, rows, :]).reshape(ZH, W // 128, LY, 128)
            part = jnp.concatenate([part[:, t].reshape(ZH * LY, 128) for t in range(W // 128)], axis=1)
            part = part.astype(BF16)
            if xp < XP:
                field[x] = part
            parts.append(part)
        first, second = parts
        if xp == XP:
            to_below[...] = first
            to_above[...] = second
        even = jnp.where(low, first, swap(second))
        odd_z = jnp.where(low, swap(first), second)
        out = dot(z_fwd[...], jnp.concatenate([even, odd_z], axis=0))
        freq[:, xp] = out.astype(BF16).reshape(KZ, 2 * LY, W)


def y_forward_kernel(given, y_fwd, out):
    for xp in range(XE):
        data = given[:, xp].reshape(2 * PY * LY, W)
        out[:, xp] = dot(y_fwd[...], data).astype(BF16).reshape(PX, 2 * Q // PX, W)


def gather(rows, out):
    count = 2 * XP * Q // PX
    for d in range(PX):
        block = [rows[t, pl.ds(d * count, count), :] for t in range(W // 128)]
        out[d] = jnp.concatenate(block, axis=1).astype(BF16).reshape(out.shape[1:])


def shrink(v):
    return v - jnp.clip(v, -shrink_level, shrink_level)


def lay_out(weight, width, copies, out):
    for b in range(C // CB):
        columns = []
        for part in range(2):
            block = weight[part, b].astype(F32)
            columns += [jnp.zeros((CB, b * CB), F32)] * (b > 0) + [block]
            columns += [jnp.zeros((CB, width - (b + 1) * CB), F32)] * (width > (b + 1) * CB)
            columns += columns[-2:] * (copies - 1)
        out[b * CB : (b + 1) * CB] = jnp.concatenate(columns, axis=1).astype(BF16)
    out[C:] = jnp.zeros((256 - C, out.shape[1]), BF16)


def spectrum_kernel(given, x_fwd, x_inv, inner_weight, outer_weight, out, rows, arrived, inner, outer):
    lay_out(inner_weight, 256, 1, inner)
    lay_out(outer_weight, C, 2, outer)
    count = Q // PX
    low = low_half(2 * PX * XP)
    wide = given[...].astype(F32).reshape(2 * count * PX * XE, W)
    for t in range(W // 128):
        arrived[t] = wide[:, t * 128 : (t + 1) * 128]
    data = []
    for q in range(count):
        some = [arrived[t, pl.ds(q, 2 * PX * XE, stride=count), :] for t in range(W // 128)]
        data.append(jnp.concatenate(some, axis=1).astype(BF16))
    both = dot(x_fwd[...], jnp.concatenate(data, axis=1))
    spec = []
    for q in range(count):
        part = both[:, q * W : (q + 1) * W]
        part = part[: 2 * Q] + swap(part[2 * Q :])
        spec.append(part[:, :256].astype(BF16))
    mixed = dot(jnp.concatenate(spec, axis=0), inner[...]).reshape(count, 2, Q, 512)
    hidden_r = jnp.tanh(mixed[:, 0, :, :256] - mixed[:, 1, :, 256:])
    hidden_i = jnp.tanh(mixed[:, 0, :, 256:] + mixed[:, 1, :, :256])
    hidden = jnp.stack([hidden_r, hidden_i], axis=1).astype(BF16).reshape(count * 2 * Q, 256)
    mixed = dot(hidden, outer[...]).reshape(count, 2, Q, 2 * W)
    filt_r = shrink(mixed[:, 0, :, :W] - mixed[:, 1, :, W:]).astype(BF16)
    filt_i = shrink(mixed[:, 0, :, W:] + mixed[:, 1, :, :W]).astype(BF16)
    filt = [jnp.concatenate([filt_r[q], filt_i[q]], axis=0) for q in range(count)]
    both = dot(x_inv[...], jnp.concatenate(filt, axis=1))
    for q in range(count):
        part = both[:, q * W : (q + 1) * W]
        back = jnp.where(low, part[: 2 * PX * XP], part[2 * PX * XP :])
        for part in range(2):
            for t in range(W // 128):
                rows[t, pl.ds(part * count + q, PX * XP, stride=2 * count), :] = back[
                    part * PX * XP : (part + 1) * PX * XP, t * 128 : (t + 1) * 128
                ]
    gather(rows, out)


def y_inverse_kernel(given, y_inv, out):
    for xp in range(XP):
        data = given[:, xp].reshape(2 * Q, W)
        out[:, xp] = dot(y_inv[...], data).astype(BF16).reshape(PY, 2 * LY, W)


def z_inverse_kernel(given, z_inv, field, below, above, out_hbm, out, sems):
    low = low_half(ZH * LY)
    below, above = by_order("px", below[...], above[...])
    copies = []
    for xp in range(XP):
        here = pl.ds(2 * xp, 2)
        data = given[:, xp].reshape(2 * KZ * LY, W)
        value = dot(z_inv[...], data)
        even, odd = value[: ZH * LY], value[ZH * LY :]
        first = jnp.where(low, even, swap(odd)) + field[2 * xp].astype(F32)
        second = jnp.where(low, swap(even), odd) + field[2 * xp + 1].astype(F32)
        if xp == 0:
            first = first + below
        if xp == XP - 1:
            second = second + above
        for x, value in ((2 * xp, first), (2 * xp + 1, second)):
            for z in range(ZH):
                out[x, :, z * W : (z + 1) * W] = value[z * LY : (z + 1) * LY].astype(BF16)
        copies.append(pltpu.make_async_copy(out.at[here], out_hbm.at[here], sems.at[xp]))
        copies[xp].start()
    for copy in copies:
        copy.wait()


def call(kernel, outs, scratch=(), name=None, **specs):
    return pl.pallas_call(
        kernel,
        out_shape=outs,
        scratch_shapes=list(scratch),
        **specs,
        compiler_params=pltpu.CompilerParams(vmem_limit_bytes=20 * 2**20),
        name=name,
    )


def shape(*dims):
    return jax.ShapeDtypeStruct(dims, BF16)


def swap_pairs(value, axis, start):
    pairs = []
    for x in range(PX):
        for y in range(PY):
            at, count = (x, PX) if axis == "px" else (y, PY)
            to = at + 1 if (at - start) % 2 == 0 else at - 1
            if 0 <= to < count:
                x_to, y_to = (to, y) if axis == "px" else (x, to)
            else:
                x_to, y_to = (x, y ^ 1) if axis == "px" else (x ^ 1, y)
            pairs.append((x * PY + y, x_to * PY + y_to))
    return lax.ppermute(value, ("px", "py"), pairs)


def body(tokens, conv_weight, inner_weight, outer_weight):
    z_fwd, z_inv, y_fwd, y_inv, x_fwd, x_inv = (jnp.asarray(m) for m in matrices())
    wide = MERGED + 2 * C
    first, second = call(rows_kernel, [shape(LX, MERGED)] * 2, name="y_rows")(tokens)
    second = swap_pairs(second, "py", 1)
    first = swap_pairs(first, "py", 0)
    filtered = jax.ShapeDtypeStruct((MERGED // 128, (LX + 2) * LY, 128), F32)
    conv = call(
        conv_kernel,
        filtered,
        [
            VMEM((LX, LY, wide), F32),
            VMEM((27, W), F32),
        ],
        name="conv",
    )(tokens, conv_weight)
    rows = [VMEM((LX, MERGED), F32)] * 2 + [VMEM((LX, wide), F32)] * 2
    field, freq, to_below, to_above = call(
        edge_kernel,
        [shape(LX, ZH * LY, W), shape(KZ, XE, 2 * LY, W)] + [shape(ZH * LY, W)] * 2,
        rows + [VMEM((MERGED // 128, 24 * LY, 128), F32), VMEM((27, W), F32)],
        name="edge_z",
    )(conv, first, second, conv_weight, z_fwd)
    rows = VMEM((W // 128, 2 * XP * Q, 128), F32)
    freq = lax.all_to_all(freq, "py", 0, 0, tiled=True)
    freq = call(y_forward_kernel, shape(PX, XE, 2 * Q // PX, W), name="y_fwd")(freq, y_fwd)
    freq = lax.all_to_all(freq, "px", 0, 0, tiled=True)
    mixing = [VMEM((256, 512), BF16), VMEM((256, 4 * C), BF16)]
    freq = call(spectrum_kernel, shape(PX, XP, 2 * Q // PX, W), [rows, VMEM((W // 128, 2 * XE * Q, 128), F32)] + mixing, name="spec")(
        freq, x_fwd, x_inv, inner_weight, outer_weight
    )
    freq, to_below, to_above = lax.optimization_barrier((freq, to_below, to_above))
    up = odd("px")
    first = swap_pairs(jnp.where(up, to_below, to_above), "px", 0)
    second = swap_pairs(jnp.where(up, to_above, to_below), "px", 1)
    freq = lax.all_to_all(freq, "px", 0, 0, tiled=True)
    freq = call(y_inverse_kernel, shape(PY, XP, 2 * LY, W), name="y_inv")(freq, y_inv)
    freq, first, second = lax.optimization_barrier((freq, first, second))
    freq = lax.all_to_all(freq, "py", 0, 0, tiled=True)
    return call(
        z_inverse_kernel,
        shape(LX, LY, MERGED),
        [VMEM((LX, LY, MERGED), BF16), pltpu.SemaphoreType.DMA((XP,))],
        name="z_inv",
        out_specs=pl.BlockSpec(memory_space=pl.ANY),
    )(freq, z_inv, field, first, second)


def solution(mesh):
    in_specs = (P("px", "py", None), P(), P(), P())
    out_specs = P("px", "py", None)
    return jax.shard_map(body, mesh=mesh, in_specs=in_specs, out_specs=out_specs, check_vma=False)
```

```python
import functools
import math

import jax
import jax.numpy as jnp
import ml_dtypes
import numpy as np
from jax import lax
from jax.experimental import pallas as pl
from jax.experimental.pallas import tpu as pltpu
from jax.sharding import PartitionSpec as P

shrink_level = 0.2
F32 = jnp.float32
BF16 = jnp.bfloat16
VMEM = pltpu.VMEM

PX, PY = 8, 16
LX, LY = 16, 8
Z, KZ, C, CB = 32, 16, 192, 96
W = 2 * C
MERGED = Z * C
XP = LX // 2
XE = XP + 1
ZH = Z // 2
Q = 64


def tables(length, modes, weights):
    product = np.asarray(modes)[:, None] * np.arange(length)[None, :] % length
    angle = product.astype(np.float32) * np.float32(2.0 * math.pi / length)
    factor = np.asarray(weights, np.float32)[:, None] / np.float32(math.sqrt(length))
    rounded = [(f(angle) * factor).astype(ml_dtypes.bfloat16) for f in (np.cos, np.sin)]
    return [t.astype(np.float64) for t in rounded]


def kept(length):
    return np.concatenate([np.arange(length // 4), np.arange(length - length // 4, length)])


def forward(cos, sin):
    return np.stack([np.stack([cos, sin], 1), np.stack([-sin, cos], 1)])


def backward(cos, sin):
    cos, sin = cos.T, sin.T
    return np.stack([np.stack([cos, -sin], 1), np.stack([sin, cos], 1)])


def as_bf16(matrix):
    return np.ascontiguousarray(matrix).astype(ml_dtypes.bfloat16)


@functools.cache
def matrices():
    eye = np.eye(LY)
    one = np.ones(KZ)
    cz, sz = tables(Z, np.arange(KZ), one)
    both = np.stack([cz, -sz], 1).reshape(KZ, 2, ZH, 2)
    z_fwd = np.einsum("kpzs,yw->kpyszw", both, eye).reshape(KZ * 2 * LY, 2 * ZH * LY)
    two = np.where(np.arange(KZ) == 0, 1.0, 2.0)
    cz, sz = tables(Z, np.arange(KZ), two)
    both = np.stack([cz, -sz], 1).reshape(KZ, 2, ZH, 2)
    z_inv = np.einsum("kpzs,yw->szykpw", both, eye).reshape(2 * ZH * LY, KZ * 2 * LY)
    n = PY * LY
    cy, sy = tables(n, kept(n), np.ones(Q))
    y_fwd = forward(cy, sy).reshape(2, PX, Q // PX, 2, PY, LY).transpose(1, 0, 2, 4, 3, 5)
    y_fwd = y_fwd.reshape(2 * Q, 2 * n)
    y_inv = backward(cy, sy).reshape(2, PY, LY, 2, PX, Q // PX)
    y_inv = y_inv.transpose(1, 0, 2, 4, 3, 5).reshape(2 * n, 2 * Q)
    n = PX * LX
    cx, sx = tables(n, kept(n), np.ones(Q))
    x_fwd = forward(cx, sx)
    extra = np.zeros((2, Q, 2, PX, 1, 2))
    extra[..., 1:, 0, 0] = x_fwd[..., LX - 1 : n - LX : LX]
    extra[..., :-1, 0, 1] = x_fwd[..., LX::LX]
    x_fwd = np.concatenate([x_fwd.reshape(2, Q, 2, PX, XP, 2), extra], axis=4)
    x_fwd = x_fwd.transpose(5, 0, 1, 3, 4, 2).reshape(4 * Q, 2 * PX * XE)
    x_inv = backward(cx, sx).reshape(2, PX, XP, 2, 2, Q)
    x_inv = x_inv.transpose(3, 0, 1, 2, 4, 5).reshape(4 * PX * XP, 2 * Q)
    return [as_bf16(m) for m in (z_fwd, z_inv, y_fwd, y_inv, x_fwd, x_inv)]


def dot(a, b):
    return jnp.dot(a, b, preferred_element_type=F32)


def low_half(rows):
    return lax.broadcasted_iota(jnp.int32, (rows, W), 1) < C


def swap(value):
    return pltpu.roll(value, C, 1)


def odd(axis):
    return lax.rem(lax.axis_index(axis), 2) == 1


def by_order(axis, first, second):
    second, first = second.astype(F32), first.astype(F32)
    up, at = odd(axis), lax.axis_index(axis)
    below, above = jnp.where(up, first, second), jnp.where(up, second, first)
    return jnp.where(at == 0, 0.0, below), jnp.where(at == lax.axis_size(axis) - 1, 0.0, above)


def rows_kernel(tok, send_first, send_second):
    step = MERGED // 4
    row = lax.broadcasted_iota(jnp.int32, (2 * LX, LX * LY), 0)
    cell = lax.broadcasted_iota(jnp.int32, (2 * LX, LX * LY), 1)
    wanted = jnp.where(row < LX, row * LY, (row - LX) * LY + LY - 1)
    pick = jnp.where(cell == wanted, 1.0, 0.0).astype(BF16)
    up = odd("py")
    for j in range(4):
        here = slice(j * step, (j + 1) * step)
        data = tok[:, :, here].astype(F32).reshape(LX * LY, step).astype(BF16)
        out = dot(pick, data)
        send_first[:, here] = jnp.where(up, out[:LX], out[LX:]).astype(BF16)
        send_second[:, here] = jnp.where(up, out[LX:], out[:LX]).astype(BF16)


def conv_kernel(tok, narrow, out, shifted, weight):
    weight[...] = jnp.concatenate([narrow[...], narrow[...]], axis=1)
    pad = jnp.zeros((LY, C), F32)
    for x in range(LX):
        shifted[x] = jnp.concatenate([pad, tok[x].astype(F32), pad], axis=1)
    row_at = lax.broadcasted_iota(jnp.int32, (LY, 128), 0)

    @pl.loop(0, MERGED // 128, unroll=6)
    def _(j):
        at = pl.multiple_of(j * 128, 128)
        after = pl.multiple_of(j * 128 + W, 128)
        here = pl.ds(at, 128)
        phase = pl.multiple_of(lax.rem(j, 3) * 128, 128)
        wide = [jnp.broadcast_to(weight[t : t + 1, pl.ds(phase, 128)], (LY, 128)) for t in range(27)]
        sums = {}
        for x in range(LX + 2):
            if x < LX:
                mid = tok[x, :, here].astype(F32)
                before = shifted[x, :, here]
                behind = shifted[x, :, pl.ds(after, 128)]
                for a in range(3):
                    to = x + 2 - a
                    for b in range(3):
                        t = a * 9 + b * 3
                        term = before * wide[t] + mid * wide[t + 1] + behind * wide[t + 2]
                        sums[to, b] = sums[to, b] + term if (to, b) in sums else term
            down = pltpu.roll(sums.pop((x, 0)), 1, 0)
            up = pltpu.roll(sums.pop((x, 2)), LY - 1, 0)
            down = jnp.where(row_at == 0, 0.0, down)
            up = jnp.where(row_at == LY - 1, 0.0, up)
            out[j, x * LY : (x + 1) * LY, :] = sums.pop((x, 1)) + down + up


def edge_kernel(
    conv, first, second, narrow, z_fwd, field, freq, to_below, to_above, ylo, yhi, ylo_s, yhi_s, edge, weight
):
    weight[...] = jnp.concatenate([narrow[...], narrow[...]], axis=1)
    for rows, rows_s, value in zip((ylo, yhi), (ylo_s, yhi_s), by_order("py", first[...], second[...])):
        rows[...] = value
        pad = jnp.zeros((LX, C), F32)
        rows_s[...] = jnp.concatenate([pad, value, pad], axis=1)

    @pl.loop(0, MERGED // 128, unroll=6)
    def _(j):
        at = pl.multiple_of(j * 128, 128)
        after = pl.multiple_of(j * 128 + W, 128)
        here = pl.ds(at, 128)
        phase = pl.multiple_of(lax.rem(j, 3) * 128, 128)
        edge[j, : (LX + 2) * LY, :] = jnp.zeros(((LX + 2) * LY, 128), F32)
        for side, rows, rows_s, b in ((0, ylo, ylo_s, 0), (1, yhi, yhi_s, 2)):
            mid = rows[:, here]
            before = rows_s[:, here]
            behind = rows_s[:, pl.ds(after, 128)]
            total = None
            for a in range(3):
                t = a * 9 + b * 3
                taps = [weight[t + e : t + e + 1, pl.ds(phase, 128)] for e in range(3)]
                term = before * taps[0] + mid * taps[1] + behind * taps[2]
                around = [jnp.zeros((n, 128), F32) for n in (2 - a, a) if n]
                term = jnp.concatenate([term] + around if a == 2 else around[:1] + [term] + around[1:], axis=0)
                total = term if total is None else total + term
            cells = pl.ds(side * (LY - 1), LX + 2, stride=LY)
            edge[j, cells, :] = total

    low = low_half(ZH * LY)
    for xp in range(XE):
        parts = []
        for x in (2 * xp, 2 * xp + 1) if xp < XP else (-1, LX):
            rows = slice((x + 1) * LY, (x + 2) * LY)
            part = (conv[:, rows, :] + edge[:, rows, :]).reshape(ZH, W // 128, LY, 128)
            part = jnp.concatenate([part[:, t].reshape(ZH * LY, 128) for t in range(W // 128)], axis=1)
            part = part.astype(BF16)
            if xp < XP:
                field[x] = part
            parts.append(part)
        first, second = parts
        if xp == XP:
            to_below[...] = first
            to_above[...] = second
        crossed = swap(jnp.where(low, second, first))
        even = jnp.where(low, first, crossed)
        odd_z = jnp.where(low, crossed, second)
        out = dot(z_fwd[...], jnp.concatenate([even, odd_z], axis=0))
        freq[:, xp] = out.astype(BF16).reshape(KZ, 2 * LY, W)


def y_forward_kernel(given, y_fwd, out):
    for xp in range(XE):
        data = given[:, xp].reshape(2 * PY * LY, W)
        out[:, xp] = dot(y_fwd[...], data).astype(BF16).reshape(PX, 2 * Q // PX, W)


def gather(rows, out):
    count = 2 * XP * Q // PX
    for d in range(PX):
        block = [rows[t, pl.ds(d * count, count), :] for t in range(W // 128)]
        out[d] = jnp.concatenate(block, axis=1).astype(BF16).reshape(out.shape[1:])


def shrink(v):
    return v - jnp.clip(v, -shrink_level, shrink_level)


def lay_out(weight, width, copies, out):
    for b in range(C // CB):
        columns = []
        for part in range(2):
            block = weight[part, b].astype(F32)
            columns += [jnp.zeros((CB, b * CB), F32)] * (b > 0) + [block]
            columns += [jnp.zeros((CB, width - (b + 1) * CB), F32)] * (width > (b + 1) * CB)
            columns += columns[-2:] * (copies - 1)
        out[b * CB : (b + 1) * CB] = jnp.concatenate(columns, axis=1).astype(BF16)
    out[C:] = jnp.zeros((256 - C, out.shape[1]), BF16)


def spectrum_kernel(given, x_fwd, x_inv, inner_weight, outer_weight, out, rows, arrived, inner, outer):
    lay_out(inner_weight, 256, 1, inner)
    lay_out(outer_weight, C, 2, outer)
    count = Q // PX
    low = low_half(2 * PX * XP)
    wide = given[...].astype(F32).reshape(2 * count * PX * XE, W)
    for t in range(W // 128):
        arrived[t] = wide[:, t * 128 : (t + 1) * 128]
    data = []
    for q in range(count):
        some = [arrived[t, pl.ds(q, 2 * PX * XE, stride=count), :] for t in range(W // 128)]
        data.append(jnp.concatenate(some, axis=1).astype(BF16))
    both = dot(x_fwd[...], jnp.concatenate(data, axis=1))
    spec = []
    for q in range(count):
        part = both[:, q * W : (q + 1) * W]
        part = part[: 2 * Q] + swap(part[2 * Q :])
        spec.append(part[:, :256].astype(BF16))
    mixed = dot(jnp.concatenate(spec, axis=0), inner[...]).reshape(count, 2, Q, 512)
    hidden_r = jnp.tanh(mixed[:, 0, :, :256] - mixed[:, 1, :, 256:])
    hidden_i = jnp.tanh(mixed[:, 0, :, 256:] + mixed[:, 1, :, :256])
    hidden = jnp.stack([hidden_r, hidden_i], axis=1).astype(BF16).reshape(count * 2 * Q, 256)
    mixed = dot(hidden, outer[...]).reshape(count, 2, Q, 2 * W)
    filt_r = shrink(mixed[:, 0, :, :W] - mixed[:, 1, :, W:]).astype(BF16)
    filt_i = shrink(mixed[:, 0, :, W:] + mixed[:, 1, :, :W]).astype(BF16)
    filt = [jnp.concatenate([filt_r[q], filt_i[q]], axis=0) for q in range(count)]
    both = dot(x_inv[...], jnp.concatenate(filt, axis=1))
    for q in range(count):
        part = both[:, q * W : (q + 1) * W]
        back = jnp.where(low, part[: 2 * PX * XP], part[2 * PX * XP :])
        for part in range(2):
            for t in range(W // 128):
                rows[t, pl.ds(part * count + q, PX * XP, stride=2 * count), :] = back[
                    part * PX * XP : (part + 1) * PX * XP, t * 128 : (t + 1) * 128
                ]
    gather(rows, out)


def y_inverse_kernel(given, y_inv, out):
    for xp in range(XP):
        data = given[:, xp].reshape(2 * Q, W)
        out[:, xp] = dot(y_inv[...], data).astype(BF16).reshape(PY, 2 * LY, W)


def z_inverse_kernel(given, z_inv, field, below, above, out_hbm, out, sems):
    low = low_half(ZH * LY)
    below, above = by_order("px", below[...], above[...])
    copies = []
    for xp in range(XP):
        here = pl.ds(2 * xp, 2)
        data = given[:, xp].reshape(2 * KZ * LY, W)
        value = dot(z_inv[...], data)
        even, odd = value[: ZH * LY], value[ZH * LY :]
        crossed = swap(jnp.where(low, odd, even))
        first = jnp.where(low, even, crossed) + field[2 * xp].astype(F32)
        second = jnp.where(low, crossed, odd) + field[2 * xp + 1].astype(F32)
        if xp == 0:
            first = first + below
        if xp == XP - 1:
            second = second + above
        for x, value in ((2 * xp, first), (2 * xp + 1, second)):
            for z in range(ZH):
                out[x, :, z * W : (z + 1) * W] = value[z * LY : (z + 1) * LY].astype(BF16)
        copies.append(pltpu.make_async_copy(out.at[here], out_hbm.at[here], sems.at[xp]))
        copies[xp].start()
    for copy in copies:
        copy.wait()


def call(kernel, outs, scratch=(), name=None, **specs):
    return pl.pallas_call(
        kernel,
        out_shape=outs,
        scratch_shapes=list(scratch),
        **specs,
        compiler_params=pltpu.CompilerParams(vmem_limit_bytes=20 * 2**20),
        name=name,
    )


def shape(*dims):
    return jax.ShapeDtypeStruct(dims, BF16)


def swap_pairs(value, axis, start):
    pairs = []
    for x in range(PX):
        for y in range(PY):
            at, count = (x, PX) if axis == "px" else (y, PY)
            to = at + 1 if (at - start) % 2 == 0 else at - 1
            if 0 <= to < count:
                x_to, y_to = (to, y) if axis == "px" else (x, to)
            else:
                x_to, y_to = (x, y ^ 1) if axis == "px" else (x ^ 1, y)
            pairs.append((x * PY + y, x_to * PY + y_to))
    return lax.ppermute(value, ("px", "py"), pairs)


def body(tokens, conv_weight, inner_weight, outer_weight):
    z_fwd, z_inv, y_fwd, y_inv, x_fwd, x_inv = (jnp.asarray(m) for m in matrices())
    wide = MERGED + 2 * C
    first, second = call(rows_kernel, [shape(LX, MERGED)] * 2, name="y_rows")(tokens)
    second = swap_pairs(second, "py", 1)
    first = swap_pairs(first, "py", 0)
    filtered = jax.ShapeDtypeStruct((MERGED // 128, (LX + 2) * LY, 128), F32)
    conv = call(
        conv_kernel,
        filtered,
        [
            VMEM((LX, LY, wide), F32),
            VMEM((27, W), F32),
        ],
        name="conv",
    )(tokens, conv_weight)
    rows = [VMEM((LX, MERGED), F32)] * 2 + [VMEM((LX, wide), F32)] * 2
    field, freq, to_below, to_above = call(
        edge_kernel,
        [shape(LX, ZH * LY, W), shape(KZ, XE, 2 * LY, W)] + [shape(ZH * LY, W)] * 2,
        rows + [VMEM((MERGED // 128, 24 * LY, 128), F32), VMEM((27, W), F32)],
        name="edge_z",
    )(conv, first, second, conv_weight, z_fwd)
    rows = VMEM((W // 128, 2 * XP * Q, 128), F32)
    freq = lax.all_to_all(freq, "py", 0, 0, tiled=True)
    freq = call(y_forward_kernel, shape(PX, XE, 2 * Q // PX, W), name="y_fwd")(freq, y_fwd)
    freq = lax.all_to_all(freq, "px", 0, 0, tiled=True)
    mixing = [VMEM((256, 512), BF16), VMEM((256, 4 * C), BF16)]
    freq = call(spectrum_kernel, shape(PX, XP, 2 * Q // PX, W), [rows, VMEM((W // 128, 2 * XE * Q, 128), F32)] + mixing, name="spec")(
        freq, x_fwd, x_inv, inner_weight, outer_weight
    )
    freq, to_below, to_above = lax.optimization_barrier((freq, to_below, to_above))
    up = odd("px")
    first = swap_pairs(jnp.where(up, to_below, to_above), "px", 0)
    second = swap_pairs(jnp.where(up, to_above, to_below), "px", 1)
    freq = lax.all_to_all(freq, "px", 0, 0, tiled=True)
    freq = call(y_inverse_kernel, shape(PY, XP, 2 * LY, W), name="y_inv")(freq, y_inv)
    freq, first, second = lax.optimization_barrier((freq, first, second))
    freq = lax.all_to_all(freq, "py", 0, 0, tiled=True)
    return call(
        z_inverse_kernel,
        shape(LX, LY, MERGED),
        [VMEM((LX, LY, MERGED), BF16), pltpu.SemaphoreType.DMA((XP,))],
        name="z_inv",
        out_specs=pl.BlockSpec(memory_space=pl.ANY),
    )(freq, z_inv, field, first, second)


def solution(mesh):
    in_specs = (P("px", "py", None), P(), P(), P())
    out_specs = P("px", "py", None)
    return jax.shard_map(body, mesh=mesh, in_specs=in_specs, out_specs=out_specs, check_vma=False)
```

```python
import functools
import math

import jax
import jax.numpy as jnp
import ml_dtypes
import numpy as np
from jax import lax
from jax.experimental import pallas as pl
from jax.experimental.pallas import tpu as pltpu
from jax.sharding import PartitionSpec as P

shrink_level = 0.2
F32 = jnp.float32
BF16 = jnp.bfloat16
VMEM = pltpu.VMEM

PX, PY = 8, 16
LX, LY = 16, 8
Z, KZ, C, CB = 32, 16, 192, 96
W = 2 * C
MERGED = Z * C
XP = LX // 2
XE = XP + 1
ZH = Z // 2
Q = 64


def tables(length, modes, weights):
    product = np.asarray(modes)[:, None] * np.arange(length)[None, :] % length
    angle = product.astype(np.float32) * np.float32(2.0 * math.pi / length)
    factor = np.asarray(weights, np.float32)[:, None] / np.float32(math.sqrt(length))
    rounded = [(f(angle) * factor).astype(ml_dtypes.bfloat16) for f in (np.cos, np.sin)]
    return [t.astype(np.float64) for t in rounded]


def kept(length):
    return np.concatenate([np.arange(length // 4), np.arange(length - length // 4, length)])


def forward(cos, sin):
    return np.stack([np.stack([cos, sin], 1), np.stack([-sin, cos], 1)])


def backward(cos, sin):
    cos, sin = cos.T, sin.T
    return np.stack([np.stack([cos, -sin], 1), np.stack([sin, cos], 1)])


def as_bf16(matrix):
    return np.ascontiguousarray(matrix).astype(ml_dtypes.bfloat16)


@functools.cache
def matrices():
    eye = np.eye(LY)
    one = np.ones(KZ)
    cz, sz = tables(Z, np.arange(KZ), one)
    both = np.stack([cz, -sz], 1).reshape(KZ, 2, ZH, 2)
    z_fwd = np.einsum("kpzs,yw->kpyszw", both, eye).reshape(KZ * 2 * LY, 2 * ZH * LY)
    two = np.where(np.arange(KZ) == 0, 1.0, 2.0)
    cz, sz = tables(Z, np.arange(KZ), two)
    both = np.stack([cz, -sz], 1).reshape(KZ, 2, ZH, 2)
    z_inv = np.einsum("kpzs,yw->szykpw", both, eye).reshape(2 * ZH * LY, KZ * 2 * LY)
    n = PY * LY
    cy, sy = tables(n, kept(n), np.ones(Q))
    y_fwd = forward(cy, sy).reshape(2, PX, Q // PX, 2, PY, LY).transpose(1, 0, 2, 4, 3, 5)
    y_fwd = y_fwd.reshape(2 * Q, 2 * n)
    y_inv = backward(cy, sy).reshape(2, PY, LY, 2, PX, Q // PX)
    y_inv = y_inv.transpose(1, 0, 2, 4, 3, 5).reshape(2 * n, 2 * Q)
    n = PX * LX
    cx, sx = tables(n, kept(n), np.ones(Q))
    x_fwd = forward(cx, sx)
    extra = np.zeros((2, Q, 2, PX, 1, 2))
    extra[..., 1:, 0, 0] = x_fwd[..., LX - 1 : n - LX : LX]
    extra[..., :-1, 0, 1] = x_fwd[..., LX::LX]
    x_fwd = np.concatenate([x_fwd.reshape(2, Q, 2, PX, XP, 2), extra], axis=4)
    x_fwd = x_fwd.transpose(5, 0, 1, 3, 4, 2).reshape(4 * Q, 2 * PX * XE)
    x_inv = backward(cx, sx).reshape(2, PX, XP, 2, 2, Q)
    x_inv = x_inv.transpose(3, 0, 1, 2, 4, 5).reshape(4 * PX * XP, 2 * Q)
    return [as_bf16(m) for m in (z_fwd, z_inv, y_fwd, y_inv, x_fwd, x_inv)]


def dot(a, b):
    return jnp.dot(a, b, preferred_element_type=F32)


def low_half(rows):
    return lax.broadcasted_iota(jnp.int32, (rows, W), 1) < C


def swap(value):
    return pltpu.roll(value, C, 1)


def odd(axis):
    return lax.rem(lax.axis_index(axis), 2) == 1


def by_order(axis, first, second):
    second, first = second.astype(F32), first.astype(F32)
    up, at = odd(axis), lax.axis_index(axis)
    below, above = jnp.where(up, first, second), jnp.where(up, second, first)
    return jnp.where(at == 0, 0.0, below), jnp.where(at == lax.axis_size(axis) - 1, 0.0, above)


def rows_kernel(tok, send_first, send_second):
    step = MERGED // 4
    row = lax.broadcasted_iota(jnp.int32, (2 * LX, LX * LY), 0)
    cell = lax.broadcasted_iota(jnp.int32, (2 * LX, LX * LY), 1)
    wanted = jnp.where(row < LX, row * LY, (row - LX) * LY + LY - 1)
    pick = jnp.where(cell == wanted, 1.0, 0.0).astype(BF16)
    up = odd("py")
    for j in range(4):
        here = slice(j * step, (j + 1) * step)
        data = tok[:, :, here].astype(F32).reshape(LX * LY, step).astype(BF16)
        out = dot(pick, data)
        send_first[:, here] = jnp.where(up, out[:LX], out[LX:]).astype(BF16)
        send_second[:, here] = jnp.where(up, out[LX:], out[:LX]).astype(BF16)


def conv_kernel(tok, narrow, out, shifted, mixed):
    taps = narrow[...]
    w0, w1, w2 = taps[:9], taps[9:18], taps[18:]
    for p, value in enumerate((w0, (w0 + w1 + w2) * 0.5, (w0 - w1 + w2) * 0.5, w2)):
        value = jnp.concatenate([value, value], axis=1)
        for t in range(9):
            mixed[p * 9 + t] = jnp.broadcast_to(value[t : t + 1], (LY, W))
    pad = jnp.zeros((LY, C), F32)
    for x in range(LX):
        shifted[x] = jnp.concatenate([pad, tok[x].astype(F32), pad], axis=1)
    row_at = lax.broadcasted_iota(jnp.int32, (LY, 128), 0)

    @pl.loop(0, MERGED // 128, unroll=6)
    def _(j):
        at = pl.multiple_of(j * 128, 128)
        after = pl.multiple_of(j * 128 + W, 128)
        here = pl.ds(at, 128)
        phase = pl.multiple_of(lax.rem(j, 3) * 128, 128)
        phase = pl.ds(phase, 128)

        def load(x):
            if not 0 <= x < LX:
                return None
            return shifted[x, :, here], tok[x, :, here].astype(F32), shifted[x, :, pl.ds(after, 128)]

        def combine(one, two, sign):
            if two is None:
                return one
            if one is None:
                return two if sign > 0 else tuple(-v for v in two)
            return tuple(u + v if sign > 0 else u - v for u, v in zip(one, two))

        d0, d1 = None, None
        for i in range(0, LX + 2, 2):
            d2, d3 = load(i), load(i + 1)
            points = combine(d0, d2, -1), combine(d1, d2, 1), combine(d2, d1, -1), combine(d1, d3, -1)
            d0, d1 = d2, d3
            sides = []
            for b in range(3):
                m = []
                for p, (before, mid, behind) in enumerate(points):
                    t = p * 9 + b * 3
                    m.append(
                        before * mixed[t, :, phase] + mid * mixed[t + 1, :, phase] + behind * mixed[t + 2, :, phase]
                    )
                sides.append((m[0] + m[1] + m[2], m[1] - m[2] - m[3]))
            for k in range(2):
                down = pltpu.roll(sides[0][k], 1, 0)
                up = pltpu.roll(sides[2][k], LY - 1, 0)
                down = jnp.where(row_at == 0, 0.0, down)
                up = jnp.where(row_at == LY - 1, 0.0, up)
                out[j, (i + k) * LY : (i + k + 1) * LY, :] = sides[1][k] + down + up


def edge_kernel(
    conv, first, second, narrow, z_fwd, field, freq, to_below, to_above, ylo, yhi, ylo_s, yhi_s, edge, weight
):
    weight[...] = jnp.concatenate([narrow[...], narrow[...]], axis=1)
    for rows, rows_s, value in zip((ylo, yhi), (ylo_s, yhi_s), by_order("py", first[...], second[...])):
        rows[...] = value
        pad = jnp.zeros((LX, C), F32)
        rows_s[...] = jnp.concatenate([pad, value, pad], axis=1)

    @pl.loop(0, MERGED // 128, unroll=6)
    def _(j):
        at = pl.multiple_of(j * 128, 128)
        after = pl.multiple_of(j * 128 + W, 128)
        here = pl.ds(at, 128)
        phase = pl.multiple_of(lax.rem(j, 3) * 128, 128)
        edge[j, : (LX + 2) * LY, :] = jnp.zeros(((LX + 2) * LY, 128), F32)
        for side, rows, rows_s, b in ((0, ylo, ylo_s, 0), (1, yhi, yhi_s, 2)):
            mid = rows[:, here]
            before = rows_s[:, here]
            behind = rows_s[:, pl.ds(after, 128)]
            total = None
            for a in range(3):
                t = a * 9 + b * 3
                taps = [weight[t + e : t + e + 1, pl.ds(phase, 128)] for e in range(3)]
                term = before * taps[0] + mid * taps[1] + behind * taps[2]
                around = [jnp.zeros((n, 128), F32) for n in (2 - a, a) if n]
                term = jnp.concatenate([term] + around if a == 2 else around[:1] + [term] + around[1:], axis=0)
                total = term if total is None else total + term
            cells = pl.ds(side * (LY - 1), LX + 2, stride=LY)
            edge[j, cells, :] = total

    low = low_half(ZH * LY)
    for xp in range(XE):
        parts = []
        for x in (2 * xp, 2 * xp + 1) if xp < XP else (-1, LX):
            rows = slice((x + 1) * LY, (x + 2) * LY)
            part = (conv[:, rows, :] + edge[:, rows, :]).reshape(ZH, W // 128, LY, 128)
            part = jnp.concatenate([part[:, t].reshape(ZH * LY, 128) for t in range(W // 128)], axis=1)
            part = part.astype(BF16)
            if xp < XP:
                field[x] = part
            parts.append(part)
        first, second = parts
        if xp == XP:
            to_below[...] = first
            to_above[...] = second
        crossed = swap(jnp.where(low, second, first))
        even = jnp.where(low, first, crossed)
        odd_z = jnp.where(low, crossed, second)
        out = dot(z_fwd[...], jnp.concatenate([even, odd_z], axis=0))
        freq[:, xp] = out.astype(BF16).reshape(KZ, 2 * LY, W)


def y_forward_kernel(given, y_fwd, out):
    for xp in range(XE):
        data = given[:, xp].reshape(2 * PY * LY, W)
        out[:, xp] = dot(y_fwd[...], data).astype(BF16).reshape(PX, 2 * Q // PX, W)


def gather(rows, out):
    count = 2 * XP * Q // PX
    for d in range(PX):
        block = [rows[t, pl.ds(d * count, count), :] for t in range(W // 128)]
        out[d] = jnp.concatenate(block, axis=1).astype(BF16).reshape(out.shape[1:])


def shrink(v):
    return v - jnp.clip(v, -shrink_level, shrink_level)


def lay_out(weight, width, copies, out):
    for b in range(C // CB):
        columns = []
        for part in range(2):
            block = weight[part, b].astype(F32)
            columns += [jnp.zeros((CB, b * CB), F32)] * (b > 0) + [block]
            columns += [jnp.zeros((CB, width - (b + 1) * CB), F32)] * (width > (b + 1) * CB)
            columns += columns[-2:] * (copies - 1)
        out[b * CB : (b + 1) * CB] = jnp.concatenate(columns, axis=1).astype(BF16)
    out[C:] = jnp.zeros((256 - C, out.shape[1]), BF16)


def spectrum_kernel(given, x_fwd, x_inv, inner_weight, outer_weight, out, rows, arrived, inner, outer):
    lay_out(inner_weight, 256, 1, inner)
    lay_out(outer_weight, 256, 1, outer)
    count = Q // PX
    low = low_half(2 * PX * XP)
    wide = given[...].astype(F32).reshape(2 * count * PX * XE, W)
    for t in range(W // 128):
        arrived[t] = wide[:, t * 128 : (t + 1) * 128]
    data = []
    for q in range(count):
        some = [arrived[t, pl.ds(q, 2 * PX * XE, stride=count), :] for t in range(W // 128)]
        data.append(jnp.concatenate(some, axis=1).astype(BF16))
    both = dot(x_fwd[...], jnp.concatenate(data, axis=1))
    spec = []
    for q in range(count):
        part = both[:, q * W : (q + 1) * W]
        part = part[: 2 * Q] + swap(part[2 * Q :])
        spec.append(part[:, :256].astype(BF16))
    mixed = dot(jnp.concatenate(spec, axis=0), inner[...]).reshape(count, 2, Q, 512)
    hidden_r = jnp.tanh(mixed[:, 0, :, :256] - mixed[:, 1, :, 256:])
    hidden_i = jnp.tanh(mixed[:, 0, :, 256:] + mixed[:, 1, :, :256])
    hidden = jnp.stack([hidden_r, hidden_i], axis=1).astype(BF16).reshape(count * 2 * Q, 256)
    mixed = dot(hidden, outer[...]).reshape(count, 2, Q, 512)
    filt_r = shrink(mixed[:, 0, :, :256] - mixed[:, 1, :, 256:]).astype(BF16)
    filt_i = shrink(mixed[:, 0, :, 256:] + mixed[:, 1, :, :256]).astype(BF16)
    filt = [jnp.concatenate([filt_r[q], filt_i[q]], axis=0) for q in range(count)]
    both = dot(x_inv[...], jnp.concatenate(filt, axis=1))
    for q in range(count):
        part = both[:, q * 256 : (q + 1) * 256]
        part = jnp.concatenate([part, jnp.zeros((4 * PX * XP, W - 256), F32)], axis=1)
        back = jnp.where(low, part[: 2 * PX * XP], swap(part[2 * PX * XP :]))
        for part in range(2):
            for t in range(W // 128):
                rows[t, pl.ds(part * count + q, PX * XP, stride=2 * count), :] = back[
                    part * PX * XP : (part + 1) * PX * XP, t * 128 : (t + 1) * 128
                ]
    gather(rows, out)


def y_inverse_kernel(given, y_inv, out):
    for xp in range(XP):
        data = given[:, xp].reshape(2 * Q, W)
        out[:, xp] = dot(y_inv[...], data).astype(BF16).reshape(PY, 2 * LY, W)


def z_inverse_kernel(given, z_inv, field, below, above, out_hbm, out, sems):
    low = low_half(ZH * LY)
    below, above = by_order("px", below[...], above[...])
    copies = []
    for xp in range(XP):
        here = pl.ds(2 * xp, 2)
        data = given[:, xp].reshape(2 * KZ * LY, W)
        value = dot(z_inv[...], data)
        even, odd = value[: ZH * LY], value[ZH * LY :]
        crossed = swap(jnp.where(low, odd, even))
        first = jnp.where(low, even, crossed) + field[2 * xp].astype(F32)
        second = jnp.where(low, crossed, odd) + field[2 * xp + 1].astype(F32)
        if xp == 0:
            first = first + below
        if xp == XP - 1:
            second = second + above
        for x, value in ((2 * xp, first), (2 * xp + 1, second)):
            for z in range(ZH):
                out[x, :, z * W : (z + 1) * W] = value[z * LY : (z + 1) * LY].astype(BF16)
        copies.append(pltpu.make_async_copy(out.at[here], out_hbm.at[here], sems.at[xp]))
        copies[xp].start()
    for copy in copies:
        copy.wait()


def call(kernel, outs, scratch=(), name=None, **specs):
    return pl.pallas_call(
        kernel,
        out_shape=outs,
        scratch_shapes=list(scratch),
        **specs,
        compiler_params=pltpu.CompilerParams(vmem_limit_bytes=20 * 2**20),
        name=name,
    )


def shape(*dims):
    return jax.ShapeDtypeStruct(dims, BF16)


def swap_pairs(value, axis, start):
    pairs = []
    for x in range(PX):
        for y in range(PY):
            at, count = (x, PX) if axis == "px" else (y, PY)
            to = at + 1 if (at - start) % 2 == 0 else at - 1
            if 0 <= to < count:
                x_to, y_to = (to, y) if axis == "px" else (x, to)
            else:
                x_to, y_to = (x, y ^ 1) if axis == "px" else (x ^ 1, y)
            pairs.append((x * PY + y, x_to * PY + y_to))
    return lax.ppermute(value, ("px", "py"), pairs)


def body(tokens, conv_weight, inner_weight, outer_weight):
    z_fwd, z_inv, y_fwd, y_inv, x_fwd, x_inv = (jnp.asarray(m) for m in matrices())
    wide = MERGED + 2 * C
    first, second = call(rows_kernel, [shape(LX, MERGED)] * 2, name="y_rows")(tokens)
    second = swap_pairs(second, "py", 1)
    first = swap_pairs(first, "py", 0)
    filtered = jax.ShapeDtypeStruct((MERGED // 128, (LX + 2) * LY, 128), F32)
    conv = call(
        conv_kernel,
        filtered,
        [VMEM((LX, LY, wide), F32), VMEM((36, LY, W), F32)],
        name="conv",
    )(tokens, conv_weight)
    rows = [VMEM((LX, MERGED), F32)] * 2 + [VMEM((LX, wide), F32)] * 2
    field, freq, to_below, to_above = call(
        edge_kernel,
        [shape(LX, ZH * LY, W), shape(KZ, XE, 2 * LY, W)] + [shape(ZH * LY, W)] * 2,
        rows + [VMEM((MERGED // 128, 24 * LY, 128), F32), VMEM((27, W), F32)],
        name="edge_z",
    )(conv, first, second, conv_weight, z_fwd)
    rows = VMEM((W // 128, 2 * XP * Q, 128), F32)
    freq = lax.all_to_all(freq, "py", 0, 0, tiled=True)
    freq = call(y_forward_kernel, shape(PX, XE, 2 * Q // PX, W), name="y_fwd")(freq, y_fwd)
    freq = lax.all_to_all(freq, "px", 0, 0, tiled=True)
    mixing = [VMEM((256, 512), BF16), VMEM((256, 512), BF16)]
    freq = call(spectrum_kernel, shape(PX, XP, 2 * Q // PX, W), [rows, VMEM((W // 128, 2 * XE * Q, 128), F32)] + mixing, name="spec")(
        freq, x_fwd, x_inv, inner_weight, outer_weight
    )
    freq, to_below, to_above = lax.optimization_barrier((freq, to_below, to_above))
    up = odd("px")
    first = swap_pairs(jnp.where(up, to_below, to_above), "px", 0)
    second = swap_pairs(jnp.where(up, to_above, to_below), "px", 1)
    freq = lax.all_to_all(freq, "px", 0, 0, tiled=True)
    freq = call(y_inverse_kernel, shape(PY, XP, 2 * LY, W), name="y_inv")(freq, y_inv)
    freq, first, second = lax.optimization_barrier((freq, first, second))
    freq = lax.all_to_all(freq, "py", 0, 0, tiled=True)
    return call(
        z_inverse_kernel,
        shape(LX, LY, MERGED),
        [VMEM((LX, LY, MERGED), BF16), pltpu.SemaphoreType.DMA((XP,))],
        name="z_inv",
        out_specs=pl.BlockSpec(memory_space=pl.ANY),
    )(freq, z_inv, field, first, second)


def solution(mesh):
    in_specs = (P("px", "py", None), P(), P(), P())
    out_specs = P("px", "py", None)
    return jax.shard_map(body, mesh=mesh, in_specs=in_specs, out_specs=out_specs, check_vma=False)
```

```python
import functools
import math

import jax
import jax.numpy as jnp
import ml_dtypes
import numpy as np
from jax import lax
from jax.experimental import pallas as pl
from jax.experimental.pallas import tpu as pltpu
from jax.sharding import PartitionSpec as P

shrink_level = 0.2
F32 = jnp.float32
BF16 = jnp.bfloat16
VMEM = pltpu.VMEM

PX, PY = 8, 16
LX, LY = 16, 8
Z, KZ, C, CB = 32, 16, 192, 96
W = 2 * C
MERGED = Z * C
XP = LX // 2
XE = XP + 1
ZH = Z // 2
Q = 64


def tables(length, modes, weights):
    product = np.asarray(modes)[:, None] * np.arange(length)[None, :] % length
    angle = product.astype(np.float32) * np.float32(2.0 * math.pi / length)
    factor = np.asarray(weights, np.float32)[:, None] / np.float32(math.sqrt(length))
    rounded = [(f(angle) * factor).astype(ml_dtypes.bfloat16) for f in (np.cos, np.sin)]
    return [t.astype(np.float64) for t in rounded]


def kept(length):
    return np.concatenate([np.arange(length // 4), np.arange(length - length // 4, length)])


def forward(cos, sin):
    return np.stack([np.stack([cos, sin], 1), np.stack([-sin, cos], 1)])


def backward(cos, sin):
    cos, sin = cos.T, sin.T
    return np.stack([np.stack([cos, -sin], 1), np.stack([sin, cos], 1)])


def as_bf16(matrix):
    return np.ascontiguousarray(matrix).astype(ml_dtypes.bfloat16)


@functools.cache
def matrices():
    eye = np.eye(LY)
    one = np.ones(KZ)
    cz, sz = tables(Z, np.arange(KZ), one)
    both = np.stack([cz, -sz], 1).reshape(KZ, 2, ZH, 2)
    z_fwd = np.einsum("kpzs,yw->kpyszw", both, eye).reshape(KZ * 2 * LY, 2 * ZH * LY)
    two = np.where(np.arange(KZ) == 0, 1.0, 2.0)
    cz, sz = tables(Z, np.arange(KZ), two)
    both = np.stack([cz, -sz], 1).reshape(KZ, 2, ZH, 2)
    z_inv = np.einsum("kpzs,yw->szykpw", both, eye).reshape(2 * ZH * LY, KZ * 2 * LY)
    n = PY * LY
    cy, sy = tables(n, kept(n), np.ones(Q))
    y_fwd = forward(cy, sy).reshape(2, PX, Q // PX, 2, PY, LY).transpose(1, 0, 2, 4, 3, 5)
    y_fwd = y_fwd.reshape(2 * Q, 2 * n)
    y_inv = backward(cy, sy).reshape(2, PY, LY, 2, PX, Q // PX)
    y_inv = y_inv.transpose(1, 0, 2, 4, 3, 5).reshape(2 * n, 2 * Q)
    n = PX * LX
    cx, sx = tables(n, kept(n), np.ones(Q))
    x_fwd = forward(cx, sx)
    extra = np.zeros((2, Q, 2, PX, 1, 2))
    extra[..., 1:, 0, 0] = x_fwd[..., LX - 1 : n - LX : LX]
    extra[..., :-1, 0, 1] = x_fwd[..., LX::LX]
    x_fwd = np.concatenate([x_fwd.reshape(2, Q, 2, PX, XP, 2), extra], axis=4)
    x_fwd = x_fwd.transpose(0, 1, 5, 3, 4, 2).reshape(2 * Q, 4 * PX * XE)
    x_inv = backward(cx, sx).reshape(2, PX, XP, 2, 2, Q)
    x_inv = x_inv.transpose(3, 0, 1, 2, 4, 5).reshape(4 * PX * XP, 2 * Q)
    return [as_bf16(m) for m in (z_fwd, z_inv, y_fwd, y_inv, x_fwd, x_inv)]


def dot(a, b):
    return jnp.dot(a, b, preferred_element_type=F32)


def low_half(rows):
    return lax.broadcasted_iota(jnp.int32, (rows, W), 1) < C


def swap(value):
    return pltpu.roll(value, C, 1)


def odd(axis):
    return lax.rem(lax.axis_index(axis), 2) == 1


def by_order(axis, first, second):
    second, first = second.astype(F32), first.astype(F32)
    up, at = odd(axis), lax.axis_index(axis)
    below, above = jnp.where(up, first, second), jnp.where(up, second, first)
    return jnp.where(at == 0, 0.0, below), jnp.where(at == lax.axis_size(axis) - 1, 0.0, above)


def rows_kernel(tok, send_first, send_second):
    step = MERGED // 4
    row = lax.broadcasted_iota(jnp.int32, (2 * LX, LX * LY), 0)
    cell = lax.broadcasted_iota(jnp.int32, (2 * LX, LX * LY), 1)
    wanted = jnp.where(row < LX, row * LY, (row - LX) * LY + LY - 1)
    pick = jnp.where(cell == wanted, 1.0, 0.0).astype(BF16)
    up = odd("py")
    for j in range(4):
        here = slice(j * step, (j + 1) * step)
        data = tok[:, :, here].astype(F32).reshape(LX * LY, step).astype(BF16)
        out = dot(pick, data)
        send_first[:, here] = jnp.where(up, out[:LX], out[LX:]).astype(BF16)
        send_second[:, here] = jnp.where(up, out[LX:], out[:LX]).astype(BF16)


def conv_kernel(tok, narrow, out, shifted, mixed):
    taps = narrow[...]
    w0, w1, w2 = taps[:9], taps[9:18], taps[18:]
    for p, value in enumerate((w0, (w0 + w1 + w2) * 0.5, (w0 - w1 + w2) * 0.5, w2)):
        value = jnp.concatenate([value, value], axis=1)
        for t in range(9):
            mixed[p * 9 + t] = jnp.broadcast_to(value[t : t + 1], (LY, W))
    pad = jnp.zeros((LY, C), F32)
    for x in range(LX):
        shifted[x] = jnp.concatenate([pad, tok[x].astype(F32), pad], axis=1)
    row_at = lax.broadcasted_iota(jnp.int32, (LY, 128), 0)

    @pl.loop(0, MERGED // 128, unroll=12)
    def _(j):
        at = pl.multiple_of(j * 128, 128)
        after = pl.multiple_of(j * 128 + W, 128)
        here = pl.ds(at, 128)
        phase = pl.multiple_of(lax.rem(j, 3) * 128, 128)
        phase = pl.ds(phase, 128)

        def load(x):
            if not 0 <= x < LX:
                return None
            return shifted[x, :, here], tok[x, :, here].astype(F32), shifted[x, :, pl.ds(after, 128)]

        def combine(one, two, sign):
            if two is None:
                return one
            if one is None:
                return two if sign > 0 else tuple(-v for v in two)
            return tuple(u + v if sign > 0 else u - v for u, v in zip(one, two))

        d0, d1 = None, None
        for i in range(0, LX + 2, 2):
            d2, d3 = load(i), load(i + 1)
            points = combine(d0, d2, -1), combine(d1, d2, 1), combine(d2, d1, -1), combine(d1, d3, -1)
            d0, d1 = d2, d3
            sides = []
            for b in range(3):
                m = []
                for p, (before, mid, behind) in enumerate(points):
                    t = p * 9 + b * 3
                    m.append(
                        before * mixed[t, :, phase] + mid * mixed[t + 1, :, phase] + behind * mixed[t + 2, :, phase]
                    )
                sides.append((m[0] + m[1] + m[2], m[1] - m[2] - m[3]))
            for k in range(2):
                down = pltpu.roll(sides[0][k], 1, 0)
                up = pltpu.roll(sides[2][k], LY - 1, 0)
                down = jnp.where(row_at == 0, 0.0, down)
                up = jnp.where(row_at == LY - 1, 0.0, up)
                out[j, (i + k) * LY : (i + k + 1) * LY, :] = sides[1][k] + down + up


def edge_kernel(
    conv, first, second, narrow, z_fwd, field, freq, to_below, to_above, ylo, yhi, ylo_s, yhi_s, edge, weight
):
    weight[...] = jnp.concatenate([narrow[...], narrow[...]], axis=1)
    for rows, rows_s, value in zip((ylo, yhi), (ylo_s, yhi_s), by_order("py", first[...], second[...])):
        rows[...] = value
        pad = jnp.zeros((LX, C), F32)
        rows_s[...] = jnp.concatenate([pad, value, pad], axis=1)

    @pl.loop(0, MERGED // 128, unroll=6)
    def _(j):
        at = pl.multiple_of(j * 128, 128)
        after = pl.multiple_of(j * 128 + W, 128)
        here = pl.ds(at, 128)
        phase = pl.multiple_of(lax.rem(j, 3) * 128, 128)
        edge[j, : (LX + 2) * LY, :] = jnp.zeros(((LX + 2) * LY, 128), F32)
        for side, rows, rows_s, b in ((0, ylo, ylo_s, 0), (1, yhi, yhi_s, 2)):
            mid = rows[:, here]
            before = rows_s[:, here]
            behind = rows_s[:, pl.ds(after, 128)]
            total = None
            for a in range(3):
                t = a * 9 + b * 3
                taps = [weight[t + e : t + e + 1, pl.ds(phase, 128)] for e in range(3)]
                term = before * taps[0] + mid * taps[1] + behind * taps[2]
                around = [jnp.zeros((n, 128), F32) for n in (2 - a, a) if n]
                term = jnp.concatenate([term] + around if a == 2 else around[:1] + [term] + around[1:], axis=0)
                total = term if total is None else total + term
            cells = pl.ds(side * (LY - 1), LX + 2, stride=LY)
            edge[j, cells, :] = total

    low = low_half(ZH * LY)
    for xp in range(XE):
        parts = []
        for x in (2 * xp, 2 * xp + 1) if xp < XP else (-1, LX):
            rows = slice((x + 1) * LY, (x + 2) * LY)
            part = (conv[:, rows, :] + edge[:, rows, :]).reshape(ZH, W // 128, LY, 128)
            part = jnp.concatenate([part[:, t].reshape(ZH * LY, 128) for t in range(W // 128)], axis=1)
            part = part.astype(BF16)
            if xp < XP:
                field[x] = part
            parts.append(part)
        first, second = parts
        if xp == XP:
            to_below[...] = first
            to_above[...] = second
        crossed = swap(jnp.where(low, second, first))
        even = jnp.where(low, first, crossed)
        odd_z = jnp.where(low, crossed, second)
        out = dot(z_fwd[...], jnp.concatenate([even, odd_z], axis=0))
        freq[:, xp] = out.astype(BF16).reshape(KZ, 2 * LY, W)


def y_forward_kernel(given, y_fwd, out):
    for xp in range(XE):
        data = given[:, xp].reshape(2 * PY * LY, W)
        out[:, xp] = dot(y_fwd[...], data).astype(BF16).reshape(PX, 2 * Q // PX, W)


def gather(rows, out):
    count = 2 * XP * Q // PX
    for d in range(PX):
        block = [rows[t, pl.ds(d * count, count), :] for t in range(W // 128)]
        out[d] = jnp.concatenate(block, axis=1).astype(BF16).reshape(out.shape[1:])


def shrink(v):
    return v - jnp.clip(v, -shrink_level, shrink_level)


def lay_out(weight, width, copies, out):
    for b in range(C // CB):
        columns = []
        for part in range(2):
            block = weight[part, b].astype(F32)
            columns += [jnp.zeros((CB, b * CB), F32)] * (b > 0) + [block]
            columns += [jnp.zeros((CB, width - (b + 1) * CB), F32)] * (width > (b + 1) * CB)
            columns += columns[-2:] * (copies - 1)
        out[b * CB : (b + 1) * CB] = jnp.concatenate(columns, axis=1).astype(BF16)
    out[C:] = jnp.zeros((256 - C, out.shape[1]), BF16)


def spectrum_kernel(given, x_fwd, x_inv, inner_weight, outer_weight, out, rows, arrived, inner, outer):
    lay_out(inner_weight, 256, 1, inner)
    lay_out(outer_weight, 256, 1, outer)
    count = Q // PX
    low = low_half(2 * PX * XP)
    wide = given[...].astype(F32).reshape(2 * count * PX * XE, W)
    for t in range(W // 128):
        arrived[t] = wide[:, t * 128 : (t + 1) * 128]
    data = []
    for q in range(count):
        some = [arrived[t, pl.ds(q, 2 * PX * XE, stride=count), :] for t in range(W // 128)]
        both = jnp.concatenate(some, axis=1).astype(BF16)
        data.append(jnp.concatenate([both[:, :256], swap(both)[:, :256]], axis=0))
    both = dot(x_fwd[...], jnp.concatenate(data, axis=1))
    spec = [both[:, q * 256 : (q + 1) * 256].astype(BF16) for q in range(count)]
    mixed = dot(jnp.concatenate(spec, axis=0), inner[...]).reshape(count, 2, Q, 512)
    hidden_r = jnp.tanh(mixed[:, 0, :, :256] - mixed[:, 1, :, 256:])
    hidden_i = jnp.tanh(mixed[:, 0, :, 256:] + mixed[:, 1, :, :256])
    hidden = jnp.stack([hidden_r, hidden_i], axis=1).astype(BF16).reshape(count * 2 * Q, 256)
    mixed = dot(hidden, outer[...]).reshape(count, 2, Q, 512)
    filt_r = shrink(mixed[:, 0, :, :256] - mixed[:, 1, :, 256:]).astype(BF16)
    filt_i = shrink(mixed[:, 0, :, 256:] + mixed[:, 1, :, :256]).astype(BF16)
    filt = [jnp.concatenate([filt_r[q], filt_i[q]], axis=0) for q in range(count)]
    both = dot(x_inv[...], jnp.concatenate(filt, axis=1))
    for q in range(count):
        part = both[:, q * 256 : (q + 1) * 256]
        part = jnp.concatenate([part, jnp.zeros((4 * PX * XP, W - 256), F32)], axis=1)
        back = jnp.where(low, part[: 2 * PX * XP], swap(part[2 * PX * XP :]))
        for part in range(2):
            for t in range(W // 128):
                rows[t, pl.ds(part * count + q, PX * XP, stride=2 * count), :] = back[
                    part * PX * XP : (part + 1) * PX * XP, t * 128 : (t + 1) * 128
                ]
    gather(rows, out)


def y_inverse_kernel(given, y_inv, out):
    for xp in range(XP):
        data = given[:, xp].reshape(2 * Q, W)
        out[:, xp] = dot(y_inv[...], data).astype(BF16).reshape(PY, 2 * LY, W)


def z_inverse_kernel(given, z_inv, field, below, above, out_hbm, out, sems):
    low = low_half(ZH * LY)
    below, above = by_order("px", below[...], above[...])
    copies = []
    for xp in range(XP):
        here = pl.ds(2 * xp, 2)
        data = given[:, xp].reshape(2 * KZ * LY, W)
        value = dot(z_inv[...], data)
        even, odd = value[: ZH * LY], value[ZH * LY :]
        crossed = swap(jnp.where(low, odd, even))
        first = jnp.where(low, even, crossed) + field[2 * xp].astype(F32)
        second = jnp.where(low, crossed, odd) + field[2 * xp + 1].astype(F32)
        if xp == 0:
            first = first + below
        if xp == XP - 1:
            second = second + above
        for x, value in ((2 * xp, first), (2 * xp + 1, second)):
            for z in range(ZH):
                out[x, :, z * W : (z + 1) * W] = value[z * LY : (z + 1) * LY].astype(BF16)
        copies.append(pltpu.make_async_copy(out.at[here], out_hbm.at[here], sems.at[xp]))
        copies[xp].start()
    for copy in copies:
        copy.wait()


def call(kernel, outs, scratch=(), name=None, **specs):
    return pl.pallas_call(
        kernel,
        out_shape=outs,
        scratch_shapes=list(scratch),
        **specs,
        compiler_params=pltpu.CompilerParams(vmem_limit_bytes=20 * 2**20),
        name=name,
    )


def shape(*dims):
    return jax.ShapeDtypeStruct(dims, BF16)


def swap_pairs(value, axis, start):
    pairs = []
    for x in range(PX):
        for y in range(PY):
            at, count = (x, PX) if axis == "px" else (y, PY)
            to = at + 1 if (at - start) % 2 == 0 else at - 1
            if 0 <= to < count:
                x_to, y_to = (to, y) if axis == "px" else (x, to)
            else:
                x_to, y_to = (x, y ^ 1) if axis == "px" else (x ^ 1, y)
            pairs.append((x * PY + y, x_to * PY + y_to))
    return lax.ppermute(value, ("px", "py"), pairs)


def body(tokens, conv_weight, inner_weight, outer_weight):
    z_fwd, z_inv, y_fwd, y_inv, x_fwd, x_inv = (jnp.asarray(m) for m in matrices())
    wide = MERGED + 2 * C
    first, second = call(rows_kernel, [shape(LX, MERGED)] * 2, name="y_rows")(tokens)
    second = swap_pairs(second, "py", 1)
    first = swap_pairs(first, "py", 0)
    filtered = jax.ShapeDtypeStruct((MERGED // 128, (LX + 2) * LY, 128), F32)
    conv = call(
        conv_kernel,
        filtered,
        [VMEM((LX, LY, wide), F32), VMEM((36, LY, W), F32)],
        name="conv",
    )(tokens, conv_weight)
    rows = [VMEM((LX, MERGED), F32)] * 2 + [VMEM((LX, wide), F32)] * 2
    field, freq, to_below, to_above = call(
        edge_kernel,
        [shape(LX, ZH * LY, W), shape(KZ, XE, 2 * LY, W)] + [shape(ZH * LY, W)] * 2,
        rows + [VMEM((MERGED // 128, 24 * LY, 128), F32), VMEM((27, W), F32)],
        name="edge_z",
    )(conv, first, second, conv_weight, z_fwd)
    rows = VMEM((W // 128, 2 * XP * Q, 128), F32)
    freq = lax.all_to_all(freq, "py", 0, 0, tiled=True)
    freq = call(y_forward_kernel, shape(PX, XE, 2 * Q // PX, W), name="y_fwd")(freq, y_fwd)
    freq = lax.all_to_all(freq, "px", 0, 0, tiled=True)
    mixing = [VMEM((256, 512), BF16), VMEM((256, 512), BF16)]
    freq = call(spectrum_kernel, shape(PX, XP, 2 * Q // PX, W), [rows, VMEM((W // 128, 2 * XE * Q, 128), F32)] + mixing, name="spec")(
        freq, x_fwd, x_inv, inner_weight, outer_weight
    )
    freq, to_below, to_above = lax.optimization_barrier((freq, to_below, to_above))
    up = odd("px")
    first = swap_pairs(jnp.where(up, to_below, to_above), "px", 0)
    second = swap_pairs(jnp.where(up, to_above, to_below), "px", 1)
    freq = lax.all_to_all(freq, "px", 0, 0, tiled=True)
    freq = call(y_inverse_kernel, shape(PY, XP, 2 * LY, W), name="y_inv")(freq, y_inv)
    freq, first, second = lax.optimization_barrier((freq, first, second))
    freq = lax.all_to_all(freq, "py", 0, 0, tiled=True)
    return call(
        z_inverse_kernel,
        shape(LX, LY, MERGED),
        [VMEM((LX, LY, MERGED), BF16), pltpu.SemaphoreType.DMA((XP,))],
        name="z_inv",
        out_specs=pl.BlockSpec(memory_space=pl.ANY),
    )(freq, z_inv, field, first, second)


def solution(mesh):
    in_specs = (P("px", "py", None), P(), P(), P())
    out_specs = P("px", "py", None)
    return jax.shard_map(body, mesh=mesh, in_specs=in_specs, out_specs=out_specs, check_vma=False)
```

```python
import functools
import math

import jax
import jax.numpy as jnp
import ml_dtypes
import numpy as np
from jax import lax
from jax.experimental import pallas as pl
from jax.experimental.pallas import tpu as pltpu
from jax.sharding import PartitionSpec as P

shrink_level = 0.2
F32 = jnp.float32
BF16 = jnp.bfloat16
VMEM = pltpu.VMEM

PX, PY = 8, 16
LX, LY = 16, 8
Z, KZ, C, CB = 32, 16, 192, 96
W = 2 * C
MERGED = Z * C
XP = LX // 2
XE = XP + 1
ZH = Z // 2
Q = 64


def tables(length, modes, weights):
    product = np.asarray(modes)[:, None] * np.arange(length)[None, :] % length
    angle = product.astype(np.float32) * np.float32(2.0 * math.pi / length)
    factor = np.asarray(weights, np.float32)[:, None] / np.float32(math.sqrt(length))
    rounded = [(f(angle) * factor).astype(ml_dtypes.bfloat16) for f in (np.cos, np.sin)]
    return [t.astype(np.float64) for t in rounded]


def kept(length):
    return np.concatenate([np.arange(length // 4), np.arange(length - length // 4, length)])


def forward(cos, sin):
    return np.stack([np.stack([cos, sin], 1), np.stack([-sin, cos], 1)])


def backward(cos, sin):
    cos, sin = cos.T, sin.T
    return np.stack([np.stack([cos, -sin], 1), np.stack([sin, cos], 1)])


def as_bf16(matrix):
    return np.ascontiguousarray(matrix).astype(ml_dtypes.bfloat16)


@functools.cache
def matrices():
    eye = np.eye(LY)
    one = np.ones(KZ)
    cz, sz = tables(Z, np.arange(KZ), one)
    both = np.stack([cz, -sz], 1).reshape(KZ, 2, ZH, 2)
    z_fwd = np.einsum("kpzs,yw->kpyszw", both, eye).reshape(KZ * 2 * LY, 2 * ZH * LY)
    two = np.where(np.arange(KZ) == 0, 1.0, 2.0)
    cz, sz = tables(Z, np.arange(KZ), two)
    both = np.stack([cz, -sz], 1).reshape(KZ, 2, ZH, 2)
    z_inv = np.einsum("kpzs,yw->szykpw", both, eye).reshape(2 * ZH * LY, KZ * 2 * LY)
    n = PY * LY
    cy, sy = tables(n, kept(n), np.ones(Q))
    y_fwd = forward(cy, sy).reshape(2, PX, Q // PX, 2, PY, LY).transpose(1, 0, 2, 4, 3, 5)
    y_fwd = y_fwd.reshape(2 * Q, 2 * n)
    y_inv = backward(cy, sy).reshape(2, PY, LY, 2, PX, Q // PX)
    y_inv = y_inv.transpose(1, 0, 2, 4, 3, 5).reshape(2 * n, 2 * Q)
    n = PX * LX
    cx, sx = tables(n, kept(n), np.ones(Q))
    x_fwd = forward(cx, sx)
    extra = np.zeros((2, Q, 2, PX, 1, 2))
    extra[..., 1:, 0, 0] = x_fwd[..., LX - 1 : n - LX : LX]
    extra[..., :-1, 0, 1] = x_fwd[..., LX::LX]
    x_fwd = np.concatenate([x_fwd.reshape(2, Q, 2, PX, XP, 2), extra], axis=4)
    x_fwd = x_fwd.transpose(0, 1, 5, 3, 4, 2).reshape(2 * Q, 4 * PX * XE)
    x_inv = backward(cx, sx).reshape(2, PX, XP, 2, 2, Q)
    x_inv = x_inv.transpose(3, 0, 1, 2, 4, 5).reshape(4 * PX * XP, 2 * Q)
    return [as_bf16(m) for m in (z_fwd, z_inv, y_fwd, y_inv, x_fwd, x_inv)]


def dot(a, b):
    return jnp.dot(a, b, preferred_element_type=F32)


def low_half(rows):
    return lax.broadcasted_iota(jnp.int32, (rows, W), 1) < C


def swap(value):
    return pltpu.roll(value, C, 1)


def odd(axis):
    return lax.rem(lax.axis_index(axis), 2) == 1


def by_order(axis, first, second):
    second, first = second.astype(F32), first.astype(F32)
    up, at = odd(axis), lax.axis_index(axis)
    below, above = jnp.where(up, first, second), jnp.where(up, second, first)
    return jnp.where(at == 0, 0.0, below), jnp.where(at == lax.axis_size(axis) - 1, 0.0, above)


def rows_kernel(tok, send_first, send_second):
    step = MERGED // 4
    row = lax.broadcasted_iota(jnp.int32, (2 * LX, LX * LY), 0)
    cell = lax.broadcasted_iota(jnp.int32, (2 * LX, LX * LY), 1)
    wanted = jnp.where(row < LX, row * LY, (row - LX) * LY + LY - 1)
    pick = jnp.where(cell == wanted, 1.0, 0.0).astype(BF16)
    up = odd("py")
    for j in range(4):
        here = slice(j * step, (j + 1) * step)
        data = tok[:, :, here].astype(F32).reshape(LX * LY, step).astype(BF16)
        out = dot(pick, data)
        send_first[:, here] = jnp.where(up, out[:LX], out[LX:]).astype(BF16)
        send_second[:, here] = jnp.where(up, out[LX:], out[:LX]).astype(BF16)


def conv_kernel(tok, narrow, out, shifted, mixed):
    taps = narrow[...]
    w0, w1, w2 = taps[:9], taps[9:18], taps[18:]
    for p, value in enumerate((w0, (w0 + w1 + w2) * 0.5, (w0 - w1 + w2) * 0.5, w2)):
        value = jnp.concatenate([value, value], axis=1)
        for t in range(9):
            mixed[p * 9 + t] = jnp.broadcast_to(value[t : t + 1], (LY, W))
    pad = jnp.zeros((LY, C), F32)
    for x in range(LX):
        shifted[x] = jnp.concatenate([pad, tok[x].astype(F32), pad], axis=1)
    row_at = lax.broadcasted_iota(jnp.int32, (LY, 128), 0)

    @pl.loop(0, MERGED // 128, unroll=12)
    def _(j):
        at = pl.multiple_of(j * 128, 128)
        after = pl.multiple_of(j * 128 + W, 128)
        here = pl.ds(at, 128)
        phase = pl.multiple_of(lax.rem(j, 3) * 128, 128)
        phase = pl.ds(phase, 128)

        def load(x):
            if not 0 <= x < LX:
                return None
            return shifted[x, :, here], tok[x, :, here].astype(F32), shifted[x, :, pl.ds(after, 128)]

        def combine(one, two, sign):
            if two is None:
                return one
            if one is None:
                return two if sign > 0 else tuple(-v for v in two)
            return tuple(u + v if sign > 0 else u - v for u, v in zip(one, two))

        d0, d1 = None, None
        for i in range(0, LX + 2, 2):
            d2, d3 = load(i), load(i + 1)
            points = combine(d0, d2, -1), combine(d1, d2, 1), combine(d2, d1, -1), combine(d1, d3, -1)
            d0, d1 = d2, d3
            sides = []
            for b in range(3):
                m = []
                for p, (before, mid, behind) in enumerate(points):
                    t = p * 9 + b * 3
                    m.append(
                        before * mixed[t, :, phase] + mid * mixed[t + 1, :, phase] + behind * mixed[t + 2, :, phase]
                    )
                sides.append((m[0] + m[1] + m[2], m[1] - m[2] - m[3]))
            for k in range(2):
                down = pltpu.roll(sides[0][k], 1, 0)
                up = pltpu.roll(sides[2][k], LY - 1, 0)
                down = jnp.where(row_at == 0, 0.0, down)
                up = jnp.where(row_at == LY - 1, 0.0, up)
                out[j, (i + k) * LY : (i + k + 1) * LY, :] = sides[1][k] + down + up


def edge_kernel(
    conv, first, second, narrow, z_fwd, field, freq, to_below, to_above, ylo, yhi, ylo_s, yhi_s, edge, weight
):
    weight[...] = jnp.concatenate([narrow[...], narrow[...]], axis=1)
    for rows, rows_s, value in zip((ylo, yhi), (ylo_s, yhi_s), by_order("py", first[...], second[...])):
        rows[...] = value
        pad = jnp.zeros((LX, C), F32)
        rows_s[...] = jnp.concatenate([pad, value, pad], axis=1)

    @pl.loop(0, MERGED // 128, unroll=6)
    def _(j):
        at = pl.multiple_of(j * 128, 128)
        after = pl.multiple_of(j * 128 + W, 128)
        here = pl.ds(at, 128)
        phase = pl.multiple_of(lax.rem(j, 3) * 128, 128)
        edge[j, : (LX + 2) * LY, :] = jnp.zeros(((LX + 2) * LY, 128), F32)
        for side, rows, rows_s, b in ((0, ylo, ylo_s, 0), (1, yhi, yhi_s, 2)):
            mid = rows[:, here]
            before = rows_s[:, here]
            behind = rows_s[:, pl.ds(after, 128)]
            total = None
            for a in range(3):
                t = a * 9 + b * 3
                taps = [weight[t + e : t + e + 1, pl.ds(phase, 128)] for e in range(3)]
                term = before * taps[0] + mid * taps[1] + behind * taps[2]
                around = [jnp.zeros((n, 128), F32) for n in (2 - a, a) if n]
                term = jnp.concatenate([term] + around if a == 2 else around[:1] + [term] + around[1:], axis=0)
                total = term if total is None else total + term
            cells = pl.ds(side * (LY - 1), LX + 2, stride=LY)
            edge[j, cells, :] = total

    low = low_half(ZH * LY)
    for xp in range(XE):
        parts = []
        for x in (2 * xp, 2 * xp + 1) if xp < XP else (-1, LX):
            rows = slice((x + 1) * LY, (x + 2) * LY)
            part = (conv[:, rows, :] + edge[:, rows, :]).reshape(ZH, W // 128, LY, 128)
            part = jnp.concatenate([part[:, t].reshape(ZH * LY, 128) for t in range(W // 128)], axis=1)
            part = part.astype(BF16)
            if xp < XP:
                field[x] = part
            parts.append(part)
        first, second = parts
        if xp == XP:
            to_below[...] = first
            to_above[...] = second
        crossed = swap(jnp.where(low, second, first))
        even = jnp.where(low, first, crossed)
        odd_z = jnp.where(low, crossed, second)
        out = dot(z_fwd[...], jnp.concatenate([even, odd_z], axis=0))
        freq[:, xp] = out.astype(BF16).reshape(KZ, 2 * LY, W)


def y_forward_kernel(given, y_fwd, out):
    data = [given[:, xp].reshape(2 * PY * LY, W) for xp in range(XE)]
    value = dot(y_fwd[...], jnp.concatenate(data, axis=1)).astype(BF16)
    for xp in range(XE):
        out[:, xp] = value[:, xp * W : (xp + 1) * W].reshape(PX, 2 * Q // PX, W)


def gather(rows, out):
    count = 2 * XP * Q // PX
    for d in range(PX):
        block = [rows[t, pl.ds(d * count, count), :] for t in range(W // 128)]
        out[d] = jnp.concatenate(block, axis=1).astype(BF16).reshape(out.shape[1:])


def shrink(v):
    return v - jnp.clip(v, -shrink_level, shrink_level)


def lay_out(weight, width, copies, out):
    for b in range(C // CB):
        columns = []
        for part in range(2):
            block = weight[part, b].astype(F32)
            columns += [jnp.zeros((CB, b * CB), F32)] * (b > 0) + [block]
            columns += [jnp.zeros((CB, width - (b + 1) * CB), F32)] * (width > (b + 1) * CB)
            columns += columns[-2:] * (copies - 1)
        out[b * CB : (b + 1) * CB] = jnp.concatenate(columns, axis=1).astype(BF16)
    out[C:] = jnp.zeros((256 - C, out.shape[1]), BF16)


def spectrum_kernel(given, x_fwd, x_inv, inner_weight, outer_weight, out, rows, arrived, inner, outer):
    lay_out(inner_weight, 256, 1, inner)
    lay_out(outer_weight, 256, 1, outer)
    count = Q // PX
    low = low_half(2 * PX * XP)
    wide = given[...].astype(F32).reshape(2 * count * PX * XE, W)
    for t in range(W // 128):
        arrived[t] = wide[:, t * 128 : (t + 1) * 128]
    data = []
    for q in range(count):
        some = [arrived[t, pl.ds(q, 2 * PX * XE, stride=count), :] for t in range(W // 128)]
        both = jnp.concatenate(some, axis=1).astype(BF16)
        data.append(jnp.concatenate([both[:, :256], swap(both)[:, :256]], axis=0))
    both = dot(x_fwd[...], jnp.concatenate(data, axis=1))
    spec = [both[:, q * 256 : (q + 1) * 256].astype(BF16) for q in range(count)]
    mixed = dot(jnp.concatenate(spec, axis=0), inner[...]).reshape(count, 2, Q, 512)
    hidden_r = jnp.tanh(mixed[:, 0, :, :256] - mixed[:, 1, :, 256:])
    hidden_i = jnp.tanh(mixed[:, 0, :, 256:] + mixed[:, 1, :, :256])
    hidden = jnp.stack([hidden_r, hidden_i], axis=1).astype(BF16).reshape(count * 2 * Q, 256)
    mixed = dot(hidden, outer[...]).reshape(count, 2, Q, 512)
    filt_r = shrink(mixed[:, 0, :, :256] - mixed[:, 1, :, 256:]).astype(BF16)
    filt_i = shrink(mixed[:, 0, :, 256:] + mixed[:, 1, :, :256]).astype(BF16)
    filt = [jnp.concatenate([filt_r[q], filt_i[q]], axis=0) for q in range(count)]
    both = dot(x_inv[...], jnp.concatenate(filt, axis=1))
    for q in range(count):
        part = both[:, q * 256 : (q + 1) * 256]
        part = jnp.concatenate([part, jnp.zeros((4 * PX * XP, W - 256), F32)], axis=1)
        back = jnp.where(low, part[: 2 * PX * XP], swap(part[2 * PX * XP :]))
        for part in range(2):
            for t in range(W // 128):
                rows[t, pl.ds(part * count + q, PX * XP, stride=2 * count), :] = back[
                    part * PX * XP : (part + 1) * PX * XP, t * 128 : (t + 1) * 128
                ]
    gather(rows, out)


def y_inverse_kernel(given, y_inv, out):
    data = [given[:, xp].reshape(2 * Q, W) for xp in range(XP)]
    value = dot(y_inv[...], jnp.concatenate(data, axis=1)).astype(BF16)
    for xp in range(XP):
        out[:, xp] = value[:, xp * W : (xp + 1) * W].reshape(PY, 2 * LY, W)


def z_inverse_kernel(given, z_inv, field, below, above, out_hbm, out, sems):
    low = low_half(ZH * LY)
    below, above = by_order("px", below[...], above[...])
    copies = []
    for xp in range(XP):
        here = pl.ds(2 * xp, 2)
        data = given[:, xp].reshape(2 * KZ * LY, W)
        value = dot(z_inv[...], data)
        even, odd = value[: ZH * LY], value[ZH * LY :]
        crossed = swap(jnp.where(low, odd, even))
        first = jnp.where(low, even, crossed) + field[2 * xp].astype(F32)
        second = jnp.where(low, crossed, odd) + field[2 * xp + 1].astype(F32)
        if xp == 0:
            first = first + below
        if xp == XP - 1:
            second = second + above
        for x, value in ((2 * xp, first), (2 * xp + 1, second)):
            for z in range(ZH):
                out[x, :, z * W : (z + 1) * W] = value[z * LY : (z + 1) * LY].astype(BF16)
        copies.append(pltpu.make_async_copy(out.at[here], out_hbm.at[here], sems.at[xp]))
        copies[xp].start()
    for copy in copies:
        copy.wait()


def call(kernel, outs, scratch=(), name=None, **specs):
    return pl.pallas_call(
        kernel,
        out_shape=outs,
        scratch_shapes=list(scratch),
        **specs,
        compiler_params=pltpu.CompilerParams(vmem_limit_bytes=20 * 2**20),
        name=name,
    )


def shape(*dims):
    return jax.ShapeDtypeStruct(dims, BF16)


def swap_pairs(value, axis, start):
    pairs = []
    for x in range(PX):
        for y in range(PY):
            at, count = (x, PX) if axis == "px" else (y, PY)
            to = at + 1 if (at - start) % 2 == 0 else at - 1
            if 0 <= to < count:
                x_to, y_to = (to, y) if axis == "px" else (x, to)
            else:
                x_to, y_to = (x, y ^ 1) if axis == "px" else (x ^ 1, y)
            pairs.append((x * PY + y, x_to * PY + y_to))
    return lax.ppermute(value, ("px", "py"), pairs)


def body(tokens, conv_weight, inner_weight, outer_weight):
    z_fwd, z_inv, y_fwd, y_inv, x_fwd, x_inv = (jnp.asarray(m) for m in matrices())
    wide = MERGED + 2 * C
    first, second = call(rows_kernel, [shape(LX, MERGED)] * 2, name="y_rows")(tokens)
    second = swap_pairs(second, "py", 1)
    first = swap_pairs(first, "py", 0)
    filtered = jax.ShapeDtypeStruct((MERGED // 128, (LX + 2) * LY, 128), F32)
    conv = call(
        conv_kernel,
        filtered,
        [VMEM((LX, LY, wide), F32), VMEM((36, LY, W), F32)],
        name="conv",
    )(tokens, conv_weight)
    rows = [VMEM((LX, MERGED), F32)] * 2 + [VMEM((LX, wide), F32)] * 2
    field, freq, to_below, to_above = call(
        edge_kernel,
        [shape(LX, ZH * LY, W), shape(KZ, XE, 2 * LY, W)] + [shape(ZH * LY, W)] * 2,
        rows + [VMEM((MERGED // 128, 24 * LY, 128), F32), VMEM((27, W), F32)],
        name="edge_z",
    )(conv, first, second, conv_weight, z_fwd)
    rows = VMEM((W // 128, 2 * XP * Q, 128), F32)
    freq = lax.all_to_all(freq, "py", 0, 0, tiled=True)
    freq = call(y_forward_kernel, shape(PX, XE, 2 * Q // PX, W), name="y_fwd")(freq, y_fwd)
    freq = lax.all_to_all(freq, "px", 0, 0, tiled=True)
    mixing = [VMEM((256, 512), BF16), VMEM((256, 512), BF16)]
    freq = call(spectrum_kernel, shape(PX, XP, 2 * Q // PX, W), [rows, VMEM((W // 128, 2 * XE * Q, 128), F32)] + mixing, name="spec")(
        freq, x_fwd, x_inv, inner_weight, outer_weight
    )
    freq, to_below, to_above = lax.optimization_barrier((freq, to_below, to_above))
    up = odd("px")
    first = swap_pairs(jnp.where(up, to_below, to_above), "px", 0)
    second = swap_pairs(jnp.where(up, to_above, to_below), "px", 1)
    freq = lax.all_to_all(freq, "px", 0, 0, tiled=True)
    freq = call(y_inverse_kernel, shape(PY, XP, 2 * LY, W), name="y_inv")(freq, y_inv)
    freq, first, second = lax.optimization_barrier((freq, first, second))
    freq = lax.all_to_all(freq, "py", 0, 0, tiled=True)
    return call(
        z_inverse_kernel,
        shape(LX, LY, MERGED),
        [VMEM((LX, LY, MERGED), BF16), pltpu.SemaphoreType.DMA((XP,))],
        name="z_inv",
        out_specs=pl.BlockSpec(memory_space=pl.ANY),
    )(freq, z_inv, field, first, second)


def solution(mesh):
    in_specs = (P("px", "py", None), P(), P(), P())
    out_specs = P("px", "py", None)
    return jax.shard_map(body, mesh=mesh, in_specs=in_specs, out_specs=out_specs, check_vma=False)
```

```python
import functools
import math

import jax
import jax.numpy as jnp
import ml_dtypes
import numpy as np
from jax import lax
from jax.experimental import pallas as pl
from jax.experimental.pallas import tpu as pltpu
from jax.sharding import PartitionSpec as P

shrink_level = 0.2
F32 = jnp.float32
BF16 = jnp.bfloat16
VMEM = pltpu.VMEM

PX, PY = 8, 16
LX, LY = 16, 8
Z, KZ, C, CB = 32, 16, 192, 96
W = 2 * C
MERGED = Z * C
XP = LX // 2
XE = XP + 1
ZH = Z // 2
Q = 64


def tables(length, modes, weights):
    product = np.asarray(modes)[:, None] * np.arange(length)[None, :] % length
    angle = product.astype(np.float32) * np.float32(2.0 * math.pi / length)
    factor = np.asarray(weights, np.float32)[:, None] / np.float32(math.sqrt(length))
    rounded = [(f(angle) * factor).astype(ml_dtypes.bfloat16) for f in (np.cos, np.sin)]
    return [t.astype(np.float64) for t in rounded]


def kept(length):
    return np.concatenate([np.arange(length // 4), np.arange(length - length // 4, length)])


def forward(cos, sin):
    return np.stack([np.stack([cos, sin], 1), np.stack([-sin, cos], 1)])


def backward(cos, sin):
    cos, sin = cos.T, sin.T
    return np.stack([np.stack([cos, -sin], 1), np.stack([sin, cos], 1)])


def as_bf16(matrix):
    return np.ascontiguousarray(matrix).astype(ml_dtypes.bfloat16)


@functools.cache
def matrices():
    eye = np.eye(LY)
    one = np.ones(KZ)
    cz, sz = tables(Z, np.arange(KZ), one)
    both = np.stack([cz, -sz], 1).reshape(KZ, 2, ZH, 2)
    z_fwd = np.einsum("kpzs,yw->kpyszw", both, eye).reshape(KZ * 2 * LY, 2 * ZH * LY)
    two = np.where(np.arange(KZ) == 0, 1.0, 2.0)
    cz, sz = tables(Z, np.arange(KZ), two)
    both = np.stack([cz, -sz], 1).reshape(KZ, 2, ZH, 2)
    z_inv = np.einsum("kpzs,yw->szykpw", both, eye).reshape(2 * ZH * LY, KZ * 2 * LY)
    n = PY * LY
    cy, sy = tables(n, kept(n), np.ones(Q))
    y_fwd = forward(cy, sy).reshape(2, PX, Q // PX, 2, PY, LY).transpose(1, 0, 2, 4, 3, 5)
    y_fwd = y_fwd.reshape(2 * Q, 2 * n)
    y_inv = backward(cy, sy).reshape(2, PY, LY, 2, PX, Q // PX)
    y_inv = y_inv.transpose(1, 0, 2, 4, 3, 5).reshape(2 * n, 2 * Q)
    n = PX * LX
    cx, sx = tables(n, kept(n), np.ones(Q))
    x_fwd = forward(cx, sx)
    extra = np.zeros((2, Q, 2, PX, 1, 2))
    extra[..., 1:, 0, 0] = x_fwd[..., LX - 1 : n - LX : LX]
    extra[..., :-1, 0, 1] = x_fwd[..., LX::LX]
    x_fwd = np.concatenate([x_fwd.reshape(2, Q, 2, PX, XP, 2), extra], axis=4)
    x_fwd = x_fwd.transpose(0, 1, 5, 3, 4, 2).reshape(2 * Q, 4 * PX * XE)
    x_inv = backward(cx, sx).reshape(2, PX, XP, 2, 2, Q)
    x_inv = x_inv.transpose(3, 0, 1, 2, 4, 5).reshape(4 * PX * XP, 2 * Q)
    return [as_bf16(m) for m in (z_fwd, z_inv, y_fwd, y_inv, x_fwd, x_inv)]


def dot(a, b):
    return jnp.dot(a, b, preferred_element_type=F32)


def low_half(rows):
    return lax.broadcasted_iota(jnp.int32, (rows, W), 1) < C


def swap(value):
    return pltpu.roll(value, C, 1)


def odd(axis):
    return lax.rem(lax.axis_index(axis), 2) == 1


def by_order(axis, first, second):
    second, first = second.astype(F32), first.astype(F32)
    up, at = odd(axis), lax.axis_index(axis)
    below, above = jnp.where(up, first, second), jnp.where(up, second, first)
    return jnp.where(at == 0, 0.0, below), jnp.where(at == lax.axis_size(axis) - 1, 0.0, above)


def rows_kernel(tok, send_first, send_second):
    step = MERGED // 4
    row = lax.broadcasted_iota(jnp.int32, (2 * LX, LX * LY), 0)
    cell = lax.broadcasted_iota(jnp.int32, (2 * LX, LX * LY), 1)
    wanted = jnp.where(row < LX, row * LY, (row - LX) * LY + LY - 1)
    pick = jnp.where(cell == wanted, 1.0, 0.0).astype(BF16)
    up = odd("py")
    for j in range(4):
        here = slice(j * step, (j + 1) * step)
        data = tok[:, :, here].astype(F32).reshape(LX * LY, step).astype(BF16)
        out = dot(pick, data)
        send_first[:, here] = jnp.where(up, out[:LX], out[LX:]).astype(BF16)
        send_second[:, here] = jnp.where(up, out[LX:], out[:LX]).astype(BF16)


def conv_kernel(tok, narrow, out, shifted, mixed):
    taps = narrow[...]
    w0, w1, w2 = taps[:9], taps[9:18], taps[18:]
    for p, value in enumerate((w0, (w0 + w1 + w2) * 0.5, (w0 - w1 + w2) * 0.5, w2)):
        value = jnp.concatenate([value, value], axis=1)
        for t in range(9):
            mixed[p * 9 + t] = jnp.broadcast_to(value[t : t + 1], (LY, W))
    pad = jnp.zeros((LY, C), F32)
    for x in range(LX):
        shifted[x] = jnp.concatenate([pad, tok[x].astype(F32), pad], axis=1)
    row_at = lax.broadcasted_iota(jnp.int32, (LY, 128), 0)

    @pl.loop(0, MERGED // 128, unroll=12)
    def _(j):
        at = pl.multiple_of(j * 128, 128)
        after = pl.multiple_of(j * 128 + W, 128)
        here = pl.ds(at, 128)
        phase = pl.multiple_of(lax.rem(j, 3) * 128, 128)
        phase = pl.ds(phase, 128)

        def load(x):
            if not 0 <= x < LX:
                return None
            return shifted[x, :, here], tok[x, :, here].astype(F32), shifted[x, :, pl.ds(after, 128)]

        def combine(one, two, sign):
            if two is None:
                return one
            if one is None:
                return two if sign > 0 else tuple(-v for v in two)
            return tuple(u + v if sign > 0 else u - v for u, v in zip(one, two))

        d0, d1 = None, None
        for i in range(0, LX + 2, 2):
            d2, d3 = load(i), load(i + 1)
            points = combine(d0, d2, -1), combine(d1, d2, 1), combine(d2, d1, -1), combine(d1, d3, -1)
            d0, d1 = d2, d3
            sides = []
            for b in range(3):
                m = []
                for p, (before, mid, behind) in enumerate(points):
                    t = p * 9 + b * 3
                    m.append(
                        before * mixed[t, :, phase] + mid * mixed[t + 1, :, phase] + behind * mixed[t + 2, :, phase]
                    )
                sides.append((m[0] + m[1] + m[2], m[1] - m[2] - m[3]))
            for k in range(2):
                down = pltpu.roll(sides[0][k], 1, 0)
                up = pltpu.roll(sides[2][k], LY - 1, 0)
                down = jnp.where(row_at == 0, 0.0, down)
                up = jnp.where(row_at == LY - 1, 0.0, up)
                out[j, (i + k) * LY : (i + k + 1) * LY, :] = sides[1][k] + down + up


def edge_kernel(
    conv, first, second, narrow, z_fwd, field, freq, to_below, to_above, ylo, yhi, ylo_s, yhi_s, edge, weight
):
    weight[...] = jnp.concatenate([narrow[...], narrow[...]], axis=1)
    for rows, rows_s, value in zip((ylo, yhi), (ylo_s, yhi_s), by_order("py", first[...], second[...])):
        rows[...] = value
        pad = jnp.zeros((LX, C), F32)
        rows_s[...] = jnp.concatenate([pad, value, pad], axis=1)

    @pl.loop(0, MERGED // 128, unroll=6)
    def _(j):
        at = pl.multiple_of(j * 128, 128)
        after = pl.multiple_of(j * 128 + W, 128)
        here = pl.ds(at, 128)
        phase = pl.multiple_of(lax.rem(j, 3) * 128, 128)
        edge[j, : (LX + 2) * LY, :] = jnp.zeros(((LX + 2) * LY, 128), F32)
        for side, rows, rows_s, b in ((0, ylo, ylo_s, 0), (1, yhi, yhi_s, 2)):
            mid = rows[:, here]
            before = rows_s[:, here]
            behind = rows_s[:, pl.ds(after, 128)]
            total = None
            for a in range(3):
                t = a * 9 + b * 3
                taps = [weight[t + e : t + e + 1, pl.ds(phase, 128)] for e in range(3)]
                term = before * taps[0] + mid * taps[1] + behind * taps[2]
                around = [jnp.zeros((n, 128), F32) for n in (2 - a, a) if n]
                term = jnp.concatenate([term] + around if a == 2 else around[:1] + [term] + around[1:], axis=0)
                total = term if total is None else total + term
            cells = pl.ds(side * (LY - 1), LX + 2, stride=LY)
            edge[j, cells, :] = total

    low = low_half(ZH * LY)
    for xp in range(XE):
        parts = []
        for x in (2 * xp, 2 * xp + 1) if xp < XP else (-1, LX):
            rows = slice((x + 1) * LY, (x + 2) * LY)
            part = (conv[:, rows, :] + edge[:, rows, :]).reshape(ZH, W // 128, LY, 128)
            part = jnp.concatenate([part[:, t].reshape(ZH * LY, 128) for t in range(W // 128)], axis=1)
            part = part.astype(BF16)
            if xp < XP:
                field[x] = part
            parts.append(part)
        first, second = parts
        if xp == XP:
            to_below[...] = first
            to_above[...] = second
        crossed = swap(jnp.where(low, second, first))
        even = jnp.where(low, first, crossed)
        odd_z = jnp.where(low, crossed, second)
        out = dot(z_fwd[...], jnp.concatenate([even, odd_z], axis=0))
        freq[:, xp] = out.astype(BF16).reshape(KZ, 2 * LY, W)


def y_forward_kernel(given, y_fwd, out):
    for xp in range(XE):
        data = given[:, xp].reshape(2 * PY * LY, W)
        out[:, xp] = dot(y_fwd[...], data).astype(BF16).reshape(PX, 2 * Q // PX, W)


def gather(rows, out):
    count = 2 * XP * Q // PX
    for d in range(PX):
        block = [rows[t, pl.ds(d * count, count), :] for t in range(W // 128)]
        out[d] = jnp.concatenate(block, axis=1).astype(BF16).reshape(out.shape[1:])


def shrink(v):
    return v - jnp.clip(v, -shrink_level, shrink_level)


def lay_out(weight, width, copies, out):
    for b in range(C // CB):
        columns = []
        for part in range(2):
            block = weight[part, b].astype(F32)
            columns += [jnp.zeros((CB, b * CB), F32)] * (b > 0) + [block]
            columns += [jnp.zeros((CB, width - (b + 1) * CB), F32)] * (width > (b + 1) * CB)
            columns += columns[-2:] * (copies - 1)
        out[b * CB : (b + 1) * CB] = jnp.concatenate(columns, axis=1).astype(BF16)
    out[C:] = jnp.zeros((256 - C, out.shape[1]), BF16)


def spectrum_kernel(given, x_fwd, x_inv, inner_weight, outer_weight, out, rows, arrived, inner, outer):
    lay_out(inner_weight, 256, 1, inner)
    lay_out(outer_weight, 256, 1, outer)
    count = Q // PX
    low = low_half(2 * PX * XP)
    wide = given[...].astype(F32).reshape(2 * count * PX * XE, W)
    for t in range(W // 128):
        arrived[t] = wide[:, t * 128 : (t + 1) * 128]
    data = []
    for q in range(count):
        some = [arrived[t, pl.ds(q, 2 * PX * XE, stride=count), :] for t in range(W // 128)]
        both = jnp.concatenate(some, axis=1).astype(BF16)
        data.append(jnp.concatenate([both[:, :256], swap(both)[:, :256]], axis=0))
    both = dot(x_fwd[...], jnp.concatenate(data, axis=1))
    spec = [both[:, q * 256 : (q + 1) * 256].astype(BF16) for q in range(count)]
    mixed = dot(jnp.concatenate(spec, axis=0), inner[...]).reshape(count, 2, Q, 512)
    hidden_r = jnp.tanh(mixed[:, 0, :, :256] - mixed[:, 1, :, 256:])
    hidden_i = jnp.tanh(mixed[:, 0, :, 256:] + mixed[:, 1, :, :256])
    hidden = jnp.stack([hidden_r, hidden_i], axis=1).astype(BF16).reshape(count * 2 * Q, 256)
    mixed = dot(hidden, outer[...]).reshape(count, 2, Q, 512)
    filt_r = shrink(mixed[:, 0, :, :256] - mixed[:, 1, :, 256:]).astype(BF16)
    filt_i = shrink(mixed[:, 0, :, 256:] + mixed[:, 1, :, :256]).astype(BF16)
    filt = [jnp.concatenate([filt_r[q], filt_i[q]], axis=0) for q in range(count)]
    both = dot(x_inv[...], jnp.concatenate(filt, axis=1))
    for q in range(count):
        part = both[:, q * 256 : (q + 1) * 256]
        part = jnp.concatenate([part, jnp.zeros((4 * PX * XP, W - 256), F32)], axis=1)
        back = jnp.where(low, part[: 2 * PX * XP], swap(part[2 * PX * XP :]))
        for part in range(2):
            for t in range(W // 128):
                rows[t, pl.ds(part * count + q, PX * XP, stride=2 * count), :] = back[
                    part * PX * XP : (part + 1) * PX * XP, t * 128 : (t + 1) * 128
                ]
    gather(rows, out)


def y_inverse_kernel(given, y_inv, out):
    for xp in range(XP):
        data = given[:, xp].reshape(2 * Q, W)
        out[:, xp] = dot(y_inv[...], data).astype(BF16).reshape(PY, 2 * LY, W)


def z_inverse_kernel(given, z_inv, field, below, above, out_hbm, out, sems):
    low = low_half(ZH * LY)
    below, above = by_order("px", below[...], above[...])
    copies = []
    for xp in range(XP):
        here = pl.ds(2 * xp, 2)
        if xp % 2 == 0:
            data = [given[:, i].reshape(2 * KZ * LY, W) for i in (xp, xp + 1)]
            both = dot(z_inv[...], jnp.concatenate(data, axis=1))
        value = both[:, xp % 2 * W : (xp % 2 + 1) * W]
        even, odd = value[: ZH * LY], value[ZH * LY :]
        crossed = swap(jnp.where(low, odd, even))
        first = jnp.where(low, even, crossed) + field[2 * xp].astype(F32)
        second = jnp.where(low, crossed, odd) + field[2 * xp + 1].astype(F32)
        if xp == 0:
            first = first + below
        if xp == XP - 1:
            second = second + above
        for x, value in ((2 * xp, first), (2 * xp + 1, second)):
            for z in range(ZH):
                out[x, :, z * W : (z + 1) * W] = value[z * LY : (z + 1) * LY].astype(BF16)
        copies.append(pltpu.make_async_copy(out.at[here], out_hbm.at[here], sems.at[xp]))
        copies[xp].start()
    for copy in copies:
        copy.wait()


def call(kernel, outs, scratch=(), name=None, **specs):
    return pl.pallas_call(
        kernel,
        out_shape=outs,
        scratch_shapes=list(scratch),
        **specs,
        compiler_params=pltpu.CompilerParams(vmem_limit_bytes=20 * 2**20),
        name=name,
    )


def shape(*dims):
    return jax.ShapeDtypeStruct(dims, BF16)


def swap_pairs(value, axis, start):
    pairs = []
    for x in range(PX):
        for y in range(PY):
            at, count = (x, PX) if axis == "px" else (y, PY)
            to = at + 1 if (at - start) % 2 == 0 else at - 1
            if 0 <= to < count:
                x_to, y_to = (to, y) if axis == "px" else (x, to)
            else:
                x_to, y_to = (x, y ^ 1) if axis == "px" else (x ^ 1, y)
            pairs.append((x * PY + y, x_to * PY + y_to))
    return lax.ppermute(value, ("px", "py"), pairs)


def body(tokens, conv_weight, inner_weight, outer_weight):
    z_fwd, z_inv, y_fwd, y_inv, x_fwd, x_inv = (jnp.asarray(m) for m in matrices())
    wide = MERGED + 2 * C
    first, second = call(rows_kernel, [shape(LX, MERGED)] * 2, name="y_rows")(tokens)
    second = swap_pairs(second, "py", 1)
    first = swap_pairs(first, "py", 0)
    filtered = jax.ShapeDtypeStruct((MERGED // 128, (LX + 2) * LY, 128), F32)
    conv = call(
        conv_kernel,
        filtered,
        [VMEM((LX, LY, wide), F32), VMEM((36, LY, W), F32)],
        name="conv",
    )(tokens, conv_weight)
    rows = [VMEM((LX, MERGED), F32)] * 2 + [VMEM((LX, wide), F32)] * 2
    field, freq, to_below, to_above = call(
        edge_kernel,
        [shape(LX, ZH * LY, W), shape(KZ, XE, 2 * LY, W)] + [shape(ZH * LY, W)] * 2,
        rows + [VMEM((MERGED // 128, 24 * LY, 128), F32), VMEM((27, W), F32)],
        name="edge_z",
    )(conv, first, second, conv_weight, z_fwd)
    rows = VMEM((W // 128, 2 * XP * Q, 128), F32)
    freq = lax.all_to_all(freq, "py", 0, 0, tiled=True)
    freq = call(y_forward_kernel, shape(PX, XE, 2 * Q // PX, W), name="y_fwd")(freq, y_fwd)
    freq = lax.all_to_all(freq, "px", 0, 0, tiled=True)
    mixing = [VMEM((256, 512), BF16), VMEM((256, 512), BF16)]
    freq = call(spectrum_kernel, shape(PX, XP, 2 * Q // PX, W), [rows, VMEM((W // 128, 2 * XE * Q, 128), F32)] + mixing, name="spec")(
        freq, x_fwd, x_inv, inner_weight, outer_weight
    )
    freq, to_below, to_above = lax.optimization_barrier((freq, to_below, to_above))
    up = odd("px")
    first = swap_pairs(jnp.where(up, to_below, to_above), "px", 0)
    second = swap_pairs(jnp.where(up, to_above, to_below), "px", 1)
    freq = lax.all_to_all(freq, "px", 0, 0, tiled=True)
    freq = call(y_inverse_kernel, shape(PY, XP, 2 * LY, W), name="y_inv")(freq, y_inv)
    freq, first, second = lax.optimization_barrier((freq, first, second))
    freq = lax.all_to_all(freq, "py", 0, 0, tiled=True)
    return call(
        z_inverse_kernel,
        shape(LX, LY, MERGED),
        [VMEM((LX, LY, MERGED), BF16), pltpu.SemaphoreType.DMA((XP,))],
        name="z_inv",
        out_specs=pl.BlockSpec(memory_space=pl.ANY),
    )(freq, z_inv, field, first, second)


def solution(mesh):
    in_specs = (P("px", "py", None), P(), P(), P())
    out_specs = P("px", "py", None)
    return jax.shard_map(body, mesh=mesh, in_specs=in_specs, out_specs=out_specs, check_vma=False)
```
